32 devices in a mesh: ctx: 8 (over y, x, core), head: 4 (over z).
Axes of the slice: x: 2, y: 2, z: 4, core: 2. Of those that a mesh axis runs over, the one named last changes fastest.
Arguments:
- q_lin: float32 [2048, 4096], P('ctx', 'head'), may hold values from -6 to 6
- k_lin: float32 [2048, 4096], P('ctx', 'head'), may hold values from -0.9722718 to 0.9722718
- v_lin: float32 [2048, 4096], P('ctx', 'head'), may hold values from -201 to 201
- log_decay: float32 [32, 2048], P('head', 'ctx'), may hold values from -1 to 0
- lin_gain: float32 [4096], P('head'), may hold values from 0.1 to 1.9
- q_soft: float32 [2048, 6144], P('ctx', 'head'), may hold values from -36 to 36
- k_soft: float32 [2048, 1024], P('ctx', 'head'), may hold values from -4 to 4
- v_soft: float32 [2048, 1024], P('ctx', 'head'), may hold values from -6 to 6
Outputs:
- lin_out: float32 [2048, 4096], P('ctx', 'head')
- soft_out: float32 [2048, 6144], P('ctx', 'head')
The draws below stay inside these ranges and needn't reach their ends.
All inputs are finite; a program needn't handle non-finite values.
Results may differ from the reference program's by a relative error of at most 0.0003.
Values sent between devices are 32-bit elements; how exact they have to be, the bound alone decides.
No kernel may reach another device: no remote copies, remote signals or barrier semaphores. Data moves between devices by JAX's collectives and lax.ppermute only.
A program may use at most 128 MiB of HBM per device.

```python
import math
import jax
import jax.numpy as jnp
from jax import lax

HD = 128
LH = 32
QH = 48
KVH = 8
TOK_DEV = 256
WINDOW_TOKENS = 2048


def decay_rates(key, slow_share):
    key = jax.random.fold_in(key, 21)
    class_key, rapid_key, gentle_key = jax.random.split(key, 3)
    slow_heads = jax.random.uniform(class_key, (LH, 1), jnp.float32) < slow_share
    fast_rate = jax.random.uniform(rapid_key, (LH, 1), jnp.float32, 1.0 / 50.0, 1.0 / 30.0)
    slow_rate = jax.random.uniform(gentle_key, (LH, 1), jnp.float32, 0.1, 0.8) / WINDOW_TOKENS
    return jnp.where(slow_heads, slow_rate, fast_rate)


def draw_k_soft(key, part):
    key = jax.random.fold_in(key, 11)
    base_keys = jax.random.truncated_normal(key, -4.0, 4.0, (WINDOW_TOKENS, KVH, HD), jnp.float32)
    result = base_keys
    return result.reshape(WINDOW_TOKENS, KVH * HD)


def draw_q_soft(key, part):
    key = jax.random.fold_in(key, 12)
    shape = (WINDOW_TOKENS, KVH, QH // KVH, HD)
    result = 2.0 * jax.random.truncated_normal(key, -4.0, 4.0, shape, jnp.float32)
    return result.reshape(WINDOW_TOKENS, QH * HD)


def draw_log_decay(key, part):
    slow_share = 0.6
    head_decay_rate = decay_rates(key, slow_share)
    key = jax.random.fold_in(key, 13)
    block_seed_key, cell_seed_key, spike_key, dropped_key = jax.random.split(key, 4)
    block_multiplier = jnp.exp(jax.random.uniform(block_seed_key, (LH, WINDOW_TOKENS // TOK_DEV, 1), jnp.float32, -0.5, 0.5))
    block_multiplier = jnp.broadcast_to(block_multiplier, (LH, WINDOW_TOKENS // TOK_DEV, TOK_DEV)).reshape(LH, WINDOW_TOKENS)
    cell_multiplier = jax.random.uniform(cell_seed_key, (LH, WINDOW_TOKENS), jnp.float32, 0.5, 1.5)
    spike_positions = jax.random.randint(spike_key, (3,), 0, WINDOW_TOKENS)
    spike_values = jnp.any(jnp.arange(WINDOW_TOKENS)[None, :] == spike_positions[:, None], axis=0)[None, :]
    dropped_entries = jax.random.uniform(dropped_key, (1, WINDOW_TOKENS), jnp.float32, 0.22, 0.69)
    return -head_decay_rate * block_multiplier * cell_multiplier - jnp.where(spike_values, dropped_entries, 0.0)


def draw_v_lin(key, part):
    slow_share = 0.6
    head_decay_rate = decay_rates(key, slow_share)
    key = jax.random.fold_in(key, 14)
    value_key, column_key, row_key = jax.random.split(key, 3)
    memory_scale = jnp.repeat(jnp.sqrt(jnp.minimum(1.0, 48.0 * head_decay_rate[:, 0])), HD)[None, :]
    column_scale = jnp.exp(jax.random.uniform(column_key, (1, LH * HD), jnp.float32, math.log(0.3), math.log(3.0)))
    row_scale = jnp.exp(jax.random.uniform(row_key, (WINDOW_TOKENS, 1), jnp.float32, math.log(0.5), math.log(5.0)))
    head_share = (jnp.arange(LH * HD) // HD).astype(jnp.float32)[None, :] / (LH - 1)
    head_scale = jnp.power(3.0, head_share)
    base_rows = jax.random.truncated_normal(value_key, -4.0, 4.0, (WINDOW_TOKENS, LH * HD), jnp.float32)
    return base_rows * head_scale * column_scale * row_scale * memory_scale


def draw_q_lin(key, part):
    key = jax.random.fold_in(key, 15)
    value_key, picked_key, depth_key = jax.random.split(key, 3)
    shape = (WINDOW_TOKENS, LH * HD)
    base_rows = jax.random.truncated_normal(value_key, -6.0, 6.0, shape, jnp.float32)
    picked = jax.random.uniform(picked_key, (WINDOW_TOKENS, 1), jnp.float32) < 1.0 / 16.0
    depth_scale = jnp.power(10.0, jax.random.uniform(depth_key, (WINDOW_TOKENS, 1), jnp.float32, -5.0, -1.0))
    return base_rows * jnp.where(picked, depth_scale, 1.0)


def draw_k_lin(key, part):
    key = jax.random.fold_in(key, 16)
    value_key, loudness_key = jax.random.split(key, 2)
    shape = (WINDOW_TOKENS, LH * HD)
    group_count = WINDOW_TOKENS // 8 + 1
    loudness = jnp.exp(jax.random.uniform(loudness_key, (group_count, LH), jnp.float32, -2.0, 1.0))
    loudness_rows = jnp.repeat(loudness[jnp.arange(WINDOW_TOKENS) // 8], HD, axis=1)
    base_rows = jax.random.truncated_normal(value_key, -4.0, 4.0, shape, jnp.float32)
    return base_rows * loudness_rows / math.sqrt(HD)


def level_of(stream_key, shape, pieces, smallest, top_value):
    level, own = 1.0, jax.random.fold_in(stream_key, 6)
    for axis_at, blocks in pieces:
        steps = jnp.exp(jax.random.uniform(jax.random.fold_in(own, axis_at), (blocks,), jnp.float32, smallest / len(pieces), top_value / len(pieces)))
        level = level * jnp.repeat(steps, shape[axis_at] // blocks).reshape([-1 if axis == axis_at else 1 for axis in range(len(shape))])
    return level


def normal_values(rng, extent, spread, limit, pieces=(), kind=jnp.bfloat16):
    values = spread * jax.random.normal(rng, extent, jnp.float32)
    if pieces:
        values = values * level_of(rng, extent, pieces, -0.22, 0.18)
    return jnp.clip(values, -limit, limit).astype(kind)


def setup_inputs(seed: int = 0) -> dict:
    key_of = jax.random.split(jax.random.key(seed), 9)
    return {
        "q_lin": draw_q_lin(jax.random.fold_in(key_of[8], 71), 0),
        "k_lin": draw_k_lin(jax.random.fold_in(key_of[8], 71), 0),
        "v_lin": draw_v_lin(jax.random.fold_in(key_of[8], 71), 0),
        "log_decay": draw_log_decay(jax.random.fold_in(key_of[8], 71), 0),
        "lin_gain": jnp.clip(1.0 + 0.18 * jax.random.normal(key_of[4], (LH * HD,), jnp.float32), 0.1, 1.9),
        "q_soft": draw_q_soft(jax.random.fold_in(key_of[8], 71), 0),
        "k_soft": draw_k_soft(jax.random.fold_in(key_of[8], 71), 0),
        "v_soft": normal_values(key_of[7], (WINDOW_TOKENS, KVH * HD), 1.0, 6.0, ((0, 8), (1, 4)), jnp.float32),
    }


HIGHEST = lax.Precision.HIGHEST
EPSILON = 1e-05

def block_terms(queries, key_rows, value_rows, log_rates):
    length = queries.shape[0]
    cumulative = jnp.cumsum(log_rates, axis=1)
    positions = jnp.arange(length)
    causal = (positions[:, None] >= positions[None, :])[None]
    decay_gaps = cumulative[:, :, None] - cumulative[:, None, :]
    weights = jnp.where(causal, jnp.exp(jnp.where(causal, decay_gaps, 0.0)), 0.0)
    scores = jnp.einsum('thd,shd->hts', queries, key_rows, precision=HIGHEST)
    inside = jnp.einsum('hts,shd->thd', scores * weights, value_rows, precision=HIGHEST)
    block_total = cumulative[:, -1]
    trailing = jnp.exp(block_total[:, None] - cumulative)
    scaled_keys = key_rows * jnp.transpose(trailing)[:, :, None]
    local_state = jnp.einsum('shd,she->hde', scaled_keys, value_rows, precision=HIGHEST)
    leading = jnp.transpose(jnp.exp(cumulative))[:, :, None]
    return (inside, leading, block_total, local_state)

def lightning(q_lin, k_lin, v_lin, log_decay):
    head_count = log_decay.shape[0]
    block_count = WINDOW_TOKENS // TOK_DEV

    def by_block(array):
        return array.reshape(block_count, TOK_DEV, head_count, HD)
    rates = jnp.transpose(log_decay.reshape(head_count, block_count, TOK_DEV), (1, 0, 2))

    def advance(carried, operands):
        queries, key_rows, value_rows, log_rates = operands
        inside, leading, block_total, local_state = block_terms(queries, key_rows, value_rows, log_rates)
        result = inside + leading * jnp.einsum('thd,hde->the', queries, carried, precision=HIGHEST)
        carried = jnp.exp(block_total)[:, None, None] * carried + local_state
        return (carried, result)
    initial = jnp.zeros((head_count, HD, HD), jnp.float32)
    _, outputs = lax.scan(advance, initial, (by_block(q_lin), by_block(k_lin), by_block(v_lin), rates))
    return outputs.reshape(WINDOW_TOKENS, head_count * HD)

def softmax_layer(q_soft, k_soft, v_soft):
    group_size = QH // KVH
    block_count = WINDOW_TOKENS // TOK_DEV
    score_scale = 1.0 / math.sqrt(HD)
    query_blocks = jnp.transpose(q_soft.reshape(block_count, TOK_DEV, KVH, group_size, HD), (2, 0, 3, 1, 4))
    key_heads = jnp.transpose(k_soft.reshape(WINDOW_TOKENS, KVH, HD), (1, 0, 2))
    value_heads = jnp.transpose(v_soft.reshape(WINDOW_TOKENS, KVH, HD), (1, 0, 2))
    positions = jnp.arange(WINDOW_TOKENS)
    starts = jnp.arange(block_count) * TOK_DEV

    def per_head(operands):
        head_queries, head_keys, head_values = operands

        def per_block(block_operands):
            block_queries, first_row = block_operands
            scores = jnp.einsum('gtd,sd->gts', block_queries, head_keys, precision=HIGHEST) * score_scale
            query_pos = first_row + jnp.arange(TOK_DEV)
            visible = (positions[None, :] <= query_pos[:, None])[None]
            scores = jnp.where(visible, scores, -jnp.inf)
            row_peak = lax.optimization_barrier(jnp.max(scores, axis=2, keepdims=True))
            weights = jnp.exp(scores - row_peak)
            summed = jnp.einsum('gts,sd->gtd', weights, head_values, precision=HIGHEST)
            return summed / lax.optimization_barrier(jnp.sum(weights, axis=2, keepdims=True))
        return lax.map(per_block, (head_queries, starts))
    merged = lax.map(per_head, (query_blocks, key_heads, value_heads))
    return jnp.transpose(merged, (1, 3, 0, 2, 4)).reshape(WINDOW_TOKENS, QH * HD)

def reference(q_lin, k_lin, v_lin, log_decay, lin_gain, q_soft, k_soft, v_soft):
    linear = lightning(q_lin, k_lin, v_lin, log_decay)
    energy = lax.optimization_barrier(jnp.sum(linear * linear, axis=1, keepdims=True))
    lin_out = linear * lax.rsqrt(energy / (LH * HD) + EPSILON) * lin_gain
    soft_out = softmax_layer(q_soft, k_soft, v_soft)
    return (lin_out, soft_out)
```

```python
import functools
import math

import jax
import jax.numpy as jnp
from jax import lax
from jax.experimental import pallas as pl
from jax.experimental.pallas import tpu as pltpu
from jax.sharding import PartitionSpec as P

HD = 128
NEGATIVE = -1e30
EPSILON = 1e-05
F32 = jnp.float32
BF16 = jnp.bfloat16
NT = (((1,), (1,)), ((), ()))
VMEM_LIMIT = 32 * 1024 * 1024


def split(x):
    high = x.astype(BF16)
    low = (x - high.astype(F32)).astype(BF16)
    return high, low


def dot(a, b):
    return jnp.dot(a, b, preferred_element_type=F32)


def three_term(a, b):
    a_high, a_low = split(a)
    b_high, b_low = split(b)
    wide = dot(a_high, jnp.concatenate([b_high, b_low], axis=1))
    n = b.shape[1]
    return wide[:, :n] + wide[:, n:] + dot(a_low, b_high)


def three_term_nt(a, b):
    a_high, a_low = split(a)
    b_high, b_low = split(b)
    left = jnp.concatenate([a_high, a_low, a_high], axis=1)
    right = jnp.concatenate([b_high, b_high, b_low], axis=1)
    return lax.dot_general(left, right, NT, preferred_element_type=F32)


def column(array, lane):
    lanes = lax.broadcasted_iota(jnp.int32, array.shape, 1)
    return jnp.sum(jnp.where(lanes == lane, array, 0.0), axis=1, keepdims=True)


def cost(flops, size, exps=0):
    return pl.CostEstimate(flops=int(flops), bytes_accessed=int(size), transcendentals=int(exps))


def smem():
    return pl.BlockSpec(memory_space=pltpu.SMEM)


def call(kernel, grid, in_specs, out_specs, out_shape, estimate, scratch=()):
    return pl.pallas_call(
        kernel,
        grid=grid,
        in_specs=in_specs,
        out_specs=out_specs,
        out_shape=out_shape,
        scratch_shapes=list(scratch),
        cost_estimate=estimate,
        compiler_params=pltpu.CompilerParams(
            dimension_semantics=("arbitrary",) * len(grid), vmem_limit_bytes=VMEM_LIMIT
        ),
    )


def state_kernel(half, rate_ref, k_ref, v_ref, state_ref, col_ref, row_ref):
    step = pl.program_id(0)
    rows = k_ref.shape[0]

    @pl.when(step == 0)
    def _():
        upto = lax.broadcasted_iota(jnp.int32, (rows, rows), 0)
        upto = (upto >= lax.broadcasted_iota(jnp.int32, (rows, rows), 1)).astype(F32)
        rates = rate_ref[...]
        heads = rates.shape[0]
        row_ref[...] = lax.dot_general(
            rates, upto, NT, precision=lax.Precision.HIGHEST, preferred_element_type=F32
        )
        padded = jnp.concatenate([rates, jnp.zeros((HD - heads, rows), F32)], axis=0)
        col_ref[...] = lax.dot_general(
            upto, padded, NT, precision=lax.Precision.HIGHEST, preferred_element_type=F32
        )

    state_ref[0, half * HD :, :] = jnp.zeros((8, HD), F32)
    for i in range(half):
        cumulative = column(col_ref[...], step * half + i)
        total = cumulative[rows - 1 : rows, :]
        scaled = k_ref[:, i * HD : (i + 1) * HD] * jnp.exp(total - cumulative)
        state_ref[0, i * HD : (i + 1) * HD, :] = three_term(
            scaled.T, v_ref[:, i * HD : (i + 1) * HD]
        )
        state_ref[0, half * HD + i : half * HD + i + 1, :] = jnp.broadcast_to(total, (1, HD))


def local_states(k_lin, v_lin, rates):
    rows, width = k_lin.shape
    heads = rates.shape[0]
    half = heads // 2
    block = pl.BlockSpec((rows, half * HD), lambda j: (0, j))
    packed = half * HD + 8
    return call(
        functools.partial(state_kernel, half),
        (2,),
        [pl.BlockSpec((heads, rows), lambda j: (0, 0)), block, block],
        [
            pl.BlockSpec((1, packed, HD), lambda j: (j, 0, 0)),
            pl.BlockSpec((rows, HD), lambda j: (0, 0)),
            pl.BlockSpec((heads, rows), lambda j: (0, 0)),
        ],
        [
            jax.ShapeDtypeStruct((2, packed, HD), F32),
            jax.ShapeDtypeStruct((rows, HD), F32),
            jax.ShapeDtypeStruct((heads, rows), F32),
        ],
        cost(6 * rows * width * HD, 10 * rows * width, rows * heads),
    )(rates, k_lin, v_lin)


def inside_kernel(half, q_ref, k_ref, v_ref, col_ref, row_ref, out_ref):
    step = pl.program_id(0)
    rows = q_ref.shape[0]
    causal = lax.broadcasted_iota(jnp.int32, (rows, rows), 0) >= lax.broadcasted_iota(
        jnp.int32, (rows, rows), 1
    )
    for i in range(half):
        at = slice(i * HD, (i + 1) * HD)
        scores = three_term_nt(q_ref[:, at], k_ref[:, at])
        gaps = column(col_ref[...], step * half + i) - row_ref[pl.ds(step * half + i, 1), :]
        weights = jnp.where(causal, jnp.exp(jnp.where(causal, gaps, 0.0)), 0.0)
        out_ref[:, at] = three_term(scores * weights, v_ref[:, at])


def inside_blocks(q_lin, k_lin, v_lin, col, row):
    rows, width = q_lin.shape
    heads = row.shape[0]
    half = heads // 2
    block = pl.BlockSpec((rows, half * HD), lambda j: (0, j))
    return call(
        functools.partial(inside_kernel, half),
        (2,),
        [
            block,
            block,
            block,
            pl.BlockSpec((rows, HD), lambda j: (0, 0)),
            pl.BlockSpec((heads, rows), lambda j: (0, 0)),
        ],
        block,
        jax.ShapeDtypeStruct((rows, width), F32),
        cost(12 * rows * rows * width, 16 * rows * width, rows * rows * heads),
    )(q_lin, k_lin, v_lin, col, row)


def joined(half, first, second):
    decay = jnp.exp(second[half * HD :, :])
    parts = [
        first[i * HD : (i + 1) * HD] * decay[i : i + 1] + second[i * HD : (i + 1) * HD]
        for i in range(half)
    ]
    parts.append(first[half * HD :] + second[half * HD :])
    return jnp.concatenate(parts, axis=0)


def chip_kernel(half, core_ref, mine_ref, theirs_ref, out_ref):
    mine, theirs = mine_ref[0], theirs_ref[0]
    late = core_ref[0] == 1
    out_ref[...] = joined(half, jnp.where(late, theirs, mine), jnp.where(late, mine, theirs))


def chip_total(core, states, other):
    _, packed, _ = states.shape
    half = (packed - 8) // HD
    spec = pl.BlockSpec((1, packed, HD), lambda j, core: (core[0], 0, 0))
    return pl.pallas_call(
        functools.partial(chip_kernel, half),
        grid_spec=pltpu.PrefetchScalarGridSpec(
            num_scalar_prefetch=1,
            grid=(1,),
            in_specs=[spec, spec],
            out_specs=pl.BlockSpec((packed, HD), lambda j, core: (0, 0)),
        ),
        out_shape=jax.ShapeDtypeStruct((packed, HD), F32),
        cost_estimate=cost(packed * HD * 2, packed * HD * 12),
        compiler_params=pltpu.CompilerParams(vmem_limit_bytes=VMEM_LIMIT),
    )(core, states, other)


def turn_kernel(half, first, last, late_ref, total_ref, theirs_ref, *refs):
    late = late_ref[0] == 1
    refs = list(refs)
    before_ref = None if first else refs.pop(0)
    prefix_ref = refs.pop(0)
    total, theirs = total_ref[...], theirs_ref[...]
    if first:
        prefix_ref[...] = jnp.where(late, theirs, 0.0)
    else:
        before = before_ref[...]
        prefix_ref[...] = jnp.where(late, joined(half, theirs, before), before)
    if not last:
        refs.pop(0)[...] = joined(
            half, jnp.where(late, theirs, total), jnp.where(late, total, theirs)
        )


def turn(late, total, theirs, before, last):
    packed = total.shape[0]
    half = (packed - 8) // HD
    whole = pl.BlockSpec((packed, HD), lambda j: (0, 0))
    operands = [total, theirs] + ([] if before is None else [before])
    count = 1 if last else 2
    out = call(
        functools.partial(turn_kernel, half, before is None, last),
        (1,),
        [smem()] + [whole] * len(operands),
        [whole] * count,
        [jax.ShapeDtypeStruct((packed, HD), F32)] * count,
        cost(packed * HD * 4, packed * HD * 16),
    )(late, *operands)
    return out[0], (None if last else out[1])


def linear_kernel(
    half, core_ref, q_ref, inside_ref, col_ref, mine_ref, theirs_ref, earlier_ref,
    out_ref, energy_ref, squares,
):
    step = pl.program_id(0)
    rows = q_ref.shape[0]
    core = core_ref[0]
    own = core == step
    summed = jnp.zeros((rows, HD), F32)
    decay = jnp.exp(earlier_ref[0, half * HD :, :])
    for i in range(half):
        at = slice(i * HD, (i + 1) * HD)
        prior = jnp.where(own, mine_ref[at, :], theirs_ref[at, :])
        prior = jnp.where(core == 1, prior * decay[i : i + 1] + earlier_ref[0, at, :], prior)
        leading = jnp.exp(column(col_ref[...], step * half + i))
        linear = inside_ref[:, at] + leading * three_term(q_ref[:, at], prior)
        out_ref[:, at] = linear
        summed = summed + linear * linear

    @pl.when(step == 0)
    def _():
        squares[...] = summed

    @pl.when(step == 1)
    def _():
        energy_ref[...] = lax.dot_general(
            jnp.ones((8, HD), F32),
            squares[...] + summed,
            NT,
            precision=lax.Precision.HIGHEST,
            preferred_element_type=F32,
        )


def linear_blocks(core, q_lin, inside, col, mine, theirs, earlier):
    rows, width = q_lin.shape
    packed = mine.shape[0]
    half = (packed - 8) // HD
    block = pl.BlockSpec((rows, half * HD), lambda j: (0, j))
    whole = pl.BlockSpec((packed, HD), lambda j: (0, 0))
    return call(
        functools.partial(linear_kernel, half),
        (2,),
        [
            smem(),
            block,
            block,
            pl.BlockSpec((rows, HD), lambda j: (0, 0)),
            whole,
            whole,
            pl.BlockSpec((1, packed, HD), lambda j: (j, 0, 0)),
        ],
        [block, pl.BlockSpec((8, rows), lambda j: (0, 0))],
        [jax.ShapeDtypeStruct((rows, width), F32), jax.ShapeDtypeStruct((8, rows), F32)],
        cost(6 * rows * width * HD, 14 * rows * width),
        [pltpu.VMEM((rows, HD), F32)],
    )(core, q_lin, inside, col, mine, theirs, earlier)


def norm_kernel(columns, *refs):
    linear_ref, gain_ref, out_ref = refs[-3:]
    energy = refs[0][...]
    for ref in refs[1:-3]:
        energy = energy + ref[...]
    factor = lax.rsqrt(energy / columns + EPSILON).T[:, 0:1]
    out_ref[...] = linear_ref[...] * factor * gain_ref[...]


def normalized(energies, linear, gain, columns):
    rows, width = linear.shape
    block = pl.BlockSpec((rows, width // 2), lambda j: (0, j))
    return call(
        functools.partial(norm_kernel, columns),
        (2,),
        [pl.BlockSpec((8, rows), lambda j: (0, 0))] * len(energies)
        + [block, pl.BlockSpec((1, width // 2), lambda j: (0, j))],
        block,
        jax.ShapeDtypeStruct((rows, width), F32),
        cost(rows * width * 2, rows * width * 8),
    )(*energies, linear, gain)


def soft_kernel(group, own, last, factor, flag_ref, q_ref, k0_ref, v0_ref, k1_ref, v1_ref, *refs):
    refs = list(refs)
    acc_ref, stat_ref = (None, None) if own else (refs.pop(0), refs.pop(0))
    out_ref = refs.pop(0)
    new_ref = None if last else refs.pop(0)
    rows = q_ref.shape[0]

    def visit(key_refs, value_refs):
        keys = jnp.concatenate([ref[...] for ref in key_refs], axis=0)
        values = jnp.concatenate([ref[...] for ref in value_refs], axis=0)
        k_high, k_low = split(keys)
        k_terms = jnp.concatenate([k_high, k_high, k_low], axis=1)
        v_high, v_low = split(values)
        v_terms = jnp.concatenate([v_high, v_low], axis=1)
        count = keys.shape[0]
        lanes = lax.broadcasted_iota(jnp.int32, (rows, HD), 1)
        stats = jnp.zeros((rows, HD), F32)
        if own:
            key_at = lax.broadcasted_iota(jnp.int32, (rows, count), 1)
            visible = key_at <= lax.broadcasted_iota(jnp.int32, (rows, count), 0) + (count - rows)
        else:
            old_stats = stat_ref[0]
        for g in range(group):
            at = slice(g * HD, (g + 1) * HD)
            q_high, q_low = split(q_ref[:, at] * factor)
            q_terms = jnp.concatenate([q_high, q_low, q_high], axis=1)
            scores = lax.dot_general(q_terms, k_terms, NT, preferred_element_type=F32)
            if own:
                scores = jnp.where(visible, scores, NEGATIVE)
            peak = jnp.max(scores, axis=1, keepdims=True)
            if not own:
                old_peak = old_stats[:, g : g + 1]
                peak = jnp.maximum(peak, old_peak)
            weights = jnp.exp2(scores - peak)
            total = jnp.sum(weights, axis=1, keepdims=True)
            w_high, w_low = split(weights)
            wide = dot(w_high, v_terms)
            summed = wide[:, :HD] + wide[:, HD:] + dot(w_low, v_high)
            if not own:
                shrink = jnp.exp2(old_peak - peak)
                total = total + old_stats[:, 64 + g : 65 + g] * shrink
                summed = summed + acc_ref[:, at] * shrink
            if last:
                summed = summed / total
            else:
                stats = jnp.where(lanes == g, peak, stats)
                stats = jnp.where(lanes == 64 + g, total, stats)
            out_ref[:, at] = summed
        if not last:
            new_ref[0] = stats

    if own:

        @pl.when(flag_ref[0] == 0)
        def _():
            visit([k0_ref], [v0_ref])

    else:

        @pl.when(flag_ref[0] == 0)
        def _():
            if last:
                for g in range(group):
                    at = slice(g * HD, (g + 1) * HD)
                    out_ref[:, at] = acc_ref[:, at] / stat_ref[0, :, 64 + g : 65 + g]
            else:
                out_ref[...] = acc_ref[...]
                new_ref[...] = stat_ref[...]

    @pl.when(flag_ref[0] == 1)
    def _():
        visit([k1_ref, k0_ref], [v1_ref, v0_ref])


def soft_stage(flag, q_soft, first, second, carried, last):
    rows, width = q_soft.shape
    kv_heads = first[0].shape[1] // HD
    group = width // (kv_heads * HD)
    own = carried is None
    factor = math.log2(math.e) / math.sqrt(HD)
    wide = pl.BlockSpec((rows, group * HD), lambda j: (0, j))
    narrow = pl.BlockSpec((first[0].shape[0], HD), lambda j: (0, j))
    stat = pl.BlockSpec((1, rows, HD), lambda j: (j, 0, 0))
    out_specs, out_shape = [wide], [jax.ShapeDtypeStruct((rows, width), F32)]
    if not last:
        out_specs.append(stat)
        out_shape.append(jax.ShapeDtypeStruct((kv_heads, rows, HD), F32))
    out = call(
        functools.partial(soft_kernel, group, own, last, factor),
        (kv_heads,),
        [smem(), wide] + [narrow] * 4 + ([] if own else [wide, stat]),
        out_specs,
        out_shape,
        cost(24 * rows * width * 2 * rows, rows * width * 12, 2 * rows * rows * width // HD),
    )(flag, q_soft, *first, *second, *(() if own else carried))
    return out[0] if last else out


def body(q_lin, k_lin, v_lin, log_decay, lin_gain, q_soft, k_soft, v_soft):
    devices = lax.axis_size("ctx")
    chips = devices // 2
    heads = lax.axis_size("head")
    me = lax.axis_index("ctx")
    core, chip = me % 2, me // 2
    as_flag = lambda value: jnp.reshape(value, (1,)).astype(jnp.int32)
    core_flag = as_flag(core)

    def send(array, pairs):
        return lax.ppermute(array, "ctx", pairs)

    swap = [(2 * c + e, 2 * c + 1 - e) for c in range(chips) for e in range(2)]

    def near(distance):
        return [
            (2 * (c ^ distance) + e, 2 * c + e)
            for c in range(chips)
            if c ^ distance < c
            for e in range(2)
        ]

    def far(distance):
        return [
            (2 * c + e, 2 * c + 1 - e)
            for c in range(chips)
            if c ^ distance < c
            for e in range(2)
        ]

    arrived = {}
    for distance in range(1, chips):
        here = [send(array, near(distance)) for array in (k_soft, v_soft)]
        arrived[distance] = (here, [send(array, far(distance)) for array in here])
    beside = [send(array, [(2 * c, 2 * c + 1) for c in range(chips)]) for array in (k_soft, v_soft)]

    states, col, row = local_states(k_lin, v_lin, log_decay)
    other = send(states, swap)
    total = chip_total(core_flag, states, other)
    prefix = None
    distance = 1
    while distance < chips:
        last = 2 * distance >= chips
        pairs = [
            (2 * (c ^ distance) + e, 2 * c + e)
            for c in range(chips)
            if not last or c ^ distance < c
            for e in range(2)
        ]
        theirs = send(total, pairs)
        late = as_flag((chip // distance) % 2)
        prefix, total = turn(late, total, theirs, prefix, last)
        distance *= 2
    prefix_other = send(prefix, swap)

    carried = soft_stage(core_flag, q_soft, (k_soft, v_soft), beside, None, False)
    inside = inside_blocks(q_lin, k_lin, v_lin, col, row)

    def energies_of(energy):
        count = heads
        parts = [energy]
        for shift in range(1, count):
            parts.append(
                lax.ppermute(energy, "head", [(i, (i + shift) % count) for i in range(count)])
            )
        return parts

    soft_out = None
    for distance in range(1, chips):
        last = distance == chips - 1
        if last:
            linear, energy = linear_blocks(
                core_flag, q_lin, inside, col, prefix, prefix_other, other
            )
            energies = energies_of(energy)
        flag = as_flag((chip ^ distance) < chip)
        out = soft_stage(flag, q_soft, *arrived[distance], carried, last)
        if last:
            soft_out = out
        else:
            carried = out
    columns = q_lin.shape[1] * heads
    lin_out = normalized(energies, linear, lin_gain.reshape(1, -1), columns)
    return (lin_out, soft_out)


def solution(mesh):
    return jax.shard_map(
        body,
        mesh=mesh,
        in_specs=(
            P("ctx", "head"),
            P("ctx", "head"),
            P("ctx", "head"),
            P("head", "ctx"),
            P("head"),
            P("ctx", "head"),
            P("ctx", "head"),
            P("ctx", "head"),
        ),
        out_specs=(P("ctx", "head"), P("ctx", "head")),
        check_vma=False,
    )
```

```python
import functools
import math

import jax
import jax.numpy as jnp
from jax import lax
from jax.experimental import pallas as pl
from jax.experimental.pallas import tpu as pltpu
from jax.sharding import PartitionSpec as P

HD = 128
NEGATIVE = -1e30
EPSILON = 1e-05
F32 = jnp.float32
BF16 = jnp.bfloat16
NT = (((1,), (1,)), ((), ()))
VMEM_LIMIT = 32 * 1024 * 1024
VMEM = pl.BlockSpec(memory_space=pltpu.VMEM)
SMEM = pl.BlockSpec(memory_space=pltpu.SMEM)


def split(x):
    high = x.astype(BF16)
    low = (x - high.astype(F32)).astype(BF16)
    return high, low


def dot(a, b):
    return jnp.dot(a, b, preferred_element_type=F32)


def three_term(a, b):
    a_high, a_low = split(a)
    b_high, b_low = split(b)
    wide = dot(a_high, jnp.concatenate([b_high, b_low], axis=1))
    n = b.shape[1]
    return wide[:, :n] + wide[:, n:] + dot(a_low, b_high)


def three_term_nt(a, b):
    a_high, a_low = split(a)
    b_high, b_low = split(b)
    left = jnp.concatenate([a_high, a_low, a_high], axis=1)
    right = jnp.concatenate([b_high, b_high, b_low], axis=1)
    return lax.dot_general(left, right, NT, preferred_element_type=F32)


def call(kernel, in_specs, out_specs, out_shape, flops, size, exps=0, scratch=(), grid=(), alias=None):
    return pl.pallas_call(
        kernel,
        grid=grid,
        in_specs=in_specs,
        out_specs=out_specs,
        out_shape=out_shape,
        scratch_shapes=list(scratch),
        input_output_aliases=alias or {},
        cost_estimate=pl.CostEstimate(
            flops=int(flops), bytes_accessed=int(size), transcendentals=int(exps)
        ),
        compiler_params=pltpu.CompilerParams(vmem_limit_bytes=VMEM_LIMIT),
    )


def state_kernel(rate_ref, k_ref, v_ref, packed_ref, sums_ref):
    tokens = k_ref.shape[0]
    heads = rate_ref.shape[0]
    part = packed_ref.shape[1] - 8
    upto = lax.broadcasted_iota(jnp.int32, (tokens, tokens), 0)
    upto = (upto <= lax.broadcasted_iota(jnp.int32, (tokens, tokens), 1)).astype(F32)
    sums = jnp.dot(
        rate_ref[...], upto, precision=lax.Precision.HIGHEST, preferred_element_type=F32
    )
    sums_ref[...] = sums
    totals = sums[:, tokens - 1 : tokens]
    trailing = jnp.exp(totals - sums)
    for h in range(heads):
        at = slice(h * HD, (h + 1) * HD)
        state = three_term(k_ref[:, at].T * trailing[h : h + 1], v_ref[:, at])
        total = jnp.broadcast_to(totals[h : h + 1], (8, HD))
        for j in range(HD // part):
            packed_ref[h * (HD // part) + j, :part] = state[j * part : (j + 1) * part]
            packed_ref[h * (HD // part) + j, part:] = total


def local_states(rates, k_lin, v_lin, count):
    tokens, width = k_lin.shape
    heads = rates.shape[0]
    part = width // count
    assert part <= HD and part % 8 == 0
    return call(
        state_kernel,
        [VMEM] * 3,
        [VMEM] * 2,
        [
            jax.ShapeDtypeStruct((count, part + 8, HD), F32),
            jax.ShapeDtypeStruct((heads, tokens), F32),
        ],
        6 * tokens * width * HD,
        10 * tokens * width,
        tokens * heads,
    )(rates, k_lin, v_lin)


def chain_kernel(states_ref, prior_ref):
    count, part, _ = prior_ref.shape
    prior = jnp.zeros((part, HD), F32)
    for c in range(count):
        prior_ref[c] = prior
        if c < count - 1:
            prior = prior * jnp.exp(states_ref[c, part : part + 1, :]) + states_ref[c, :part, :]


def chained(states):
    count, packed, _ = states.shape
    return call(
        chain_kernel,
        [VMEM],
        VMEM,
        jax.ShapeDtypeStruct((count, packed - 8, HD), F32),
        states.size * 2,
        states.size * 8,
    )(states)


def inside_kernel(q_ref, k_ref, v_ref, sums_ref, out_ref):
    tokens = q_ref.shape[0]
    heads = sums_ref.shape[0]
    causal = lax.broadcasted_iota(jnp.int32, (tokens, tokens), 0) >= lax.broadcasted_iota(
        jnp.int32, (tokens, tokens), 1
    )
    columns = sums_ref[...].T
    for h in range(heads):
        at = slice(h * HD, (h + 1) * HD)
        scores = three_term_nt(q_ref[:, at], k_ref[:, at])
        gaps = columns[:, h : h + 1] - sums_ref[h : h + 1, :]
        weights = jnp.where(causal, jnp.exp(jnp.where(causal, gaps, 0.0)), 0.0)
        out_ref[:, at] = three_term(scores * weights, v_ref[:, at])


def inside_blocks(q_lin, k_lin, v_lin, sums):
    tokens, width = q_lin.shape
    return call(
        inside_kernel,
        [VMEM] * 4,
        VMEM,
        jax.ShapeDtypeStruct((tokens, width), F32),
        12 * tokens * tokens * width,
        16 * tokens * width,
        tokens * tokens * sums.shape[0],
    )(q_lin, k_lin, v_lin, sums)


def linear_kernel(q_ref, inside_ref, sums_ref, prior_ref, out_ref, energy_ref):
    tokens = q_ref.shape[0]
    heads = sums_ref.shape[0]
    leading = jnp.exp(sums_ref[...]).T
    squares = jnp.zeros((tokens, HD), F32)
    for h in range(heads):
        at = slice(h * HD, (h + 1) * HD)
        carried = three_term(q_ref[:, at], prior_ref[at, :])
        linear = inside_ref[:, at] + leading[:, h : h + 1] * carried
        out_ref[:, at] = linear
        squares = squares + linear * linear
    energy = lax.dot_general(
        jnp.ones((8, HD), F32),
        squares,
        NT,
        precision=lax.Precision.HIGHEST,
        preferred_element_type=F32,
    )
    for i in range(energy_ref.shape[0]):
        energy_ref[i] = energy


def linear_blocks(q_lin, inside, sums, prior, copies):
    tokens, width = q_lin.shape
    return call(
        linear_kernel,
        [VMEM] * 4,
        [VMEM] * 2,
        [
            jax.ShapeDtypeStruct((tokens, width), F32),
            jax.ShapeDtypeStruct((copies, 8, tokens), F32),
        ],
        6 * tokens * width * HD,
        14 * tokens * width,
    )(q_lin, inside, sums, prior)


def pair_kernel(core_ref, k_ref, v_ref, k_other_ref, v_other_ref, out_ref):
    core = core_ref[0]
    tokens = k_ref.shape[0]
    at = pl.ds(pl.multiple_of(core * HD, HD), HD)
    first = core == 0
    for side, (mine_ref, other_ref) in enumerate([(k_ref, k_other_ref), (v_ref, v_other_ref)]):
        mine, other = mine_ref[:, at], other_ref[:, at]
        to = slice(side * HD, (side + 1) * HD)
        out_ref[:tokens, to] = jnp.where(first, mine, other)
        out_ref[tokens:, to] = jnp.where(first, other, mine)


def pair_block(core, k_soft, v_soft, k_other, v_other):
    tokens = k_soft.shape[0]
    return call(
        pair_kernel,
        [SMEM] + [VMEM] * 4,
        VMEM,
        jax.ShapeDtypeStruct((2 * tokens, 2 * HD), F32),
        tokens * HD * 4,
        tokens * HD * 48,
    )(core, k_soft, v_soft, k_other, v_other)


def run_tiles(count, load, soften, gather):
    load(0, 0)
    load(1, 1)
    soften(0, 0)

    def turn(j, carry):
        for i, slot in ((2 * j + 1, 1), (2 * j + 2, 0)):
            load(i + 1, 1 - slot)
            gather(i - 1, 1 - slot)
            soften(i, slot)
        return carry

    lax.fori_loop(0, count // 2 - 1, turn, 0)
    gather(count - 2, 0)
    soften(count - 1, 1)
    gather(count - 1, 1)


def key_terms(kv_ref):
    k_high, k_low = split(kv_ref[:, :HD])
    v_high, v_low = split(kv_ref[:, HD:].T)
    return (
        jnp.concatenate([k_high, k_high, k_low], axis=1),
        jnp.concatenate([v_high, v_low], axis=0),
    )


def own_kernel(factor, core_ref, q_ref, q_other_ref, kv_ref, q_out, acc_out, stat_out, *scratch):
    keys_ref, values_ref = scratch[:2]
    scores, highs, lows, peaks = scratch[2:4], scratch[4:6], scratch[6:8], scratch[8:10]
    core = core_ref[0]
    tokens = q_ref.shape[0]
    group = q_out.shape[0] // 2
    keys_ref[...], values_ref[...] = key_terms(kv_ref)
    first = core == 0
    for g in range(group):
        at = pl.ds(pl.multiple_of(core * (group * HD) + g * HD, HD), HD)
        mine, other = q_ref[:, at], q_other_ref[:, at]
        for t, rows in enumerate(
            (jnp.where(first, mine, other), jnp.where(first, other, mine))
        ):
            high, low = split(rows.T * factor)
            q_out[2 * g + t, :HD] = high
            q_out[2 * g + t, HD:] = low

    def load(i, slot):
        count = tokens * (slot + 1)
        high_low = q_out[i]
        terms = jnp.concatenate([high_low, high_low[:HD]], axis=0)
        s = dot(keys_ref[:count], terms)
        key_at = lax.broadcasted_iota(jnp.int32, (tokens, tokens), 0)
        seen = key_at <= lax.broadcasted_iota(jnp.int32, (tokens, tokens), 1)
        edge = jnp.where(seen, s[count - tokens :], NEGATIVE)
        peak = jnp.max(edge, axis=0, keepdims=True)
        scores[slot][count - tokens : count] = edge
        if slot:
            scores[slot][:tokens] = s[:tokens]
            peak = jnp.maximum(peak, jnp.max(s[:tokens], axis=0, keepdims=True))
        peaks[slot][...] = jnp.broadcast_to(peak, (8, tokens))

    def soften(i, slot):
        peak = peaks[slot][0:1]
        total = jnp.zeros((1, tokens), F32)
        for c in range(slot + 1):
            at = slice(c * tokens, (c + 1) * tokens)
            w = jnp.exp2(scores[slot][at] - peak)
            total = total + jnp.sum(w, axis=0, keepdims=True)
            highs[slot][at], lows[slot][at] = split(w)
        stat_out[i, 0:1] = peak
        stat_out[i, 1:2] = total

    def gather(i, slot):
        count = tokens * (slot + 1)
        wide = dot(values_ref[:, :count], highs[slot][:count])
        acc_out[i] = wide[:HD] + wide[HD:] + dot(values_ref[:HD, :count], lows[slot][:count])

    run_tiles(2 * group, load, soften, gather)


def stage_scratch(tokens):
    return [
        pltpu.VMEM((2 * tokens, 3 * HD), BF16),
        pltpu.VMEM((2 * HD, 2 * tokens), BF16),
        *[pltpu.VMEM((2 * tokens, tokens), F32)] * 2,
        *[pltpu.VMEM((2 * tokens, tokens), BF16)] * 4,
        *[pltpu.VMEM((8, tokens), F32)] * 2,
    ]


def own_stage(core, q_soft, q_other, kv):
    tokens, width = q_soft.shape
    tiles = width // HD
    return call(
        functools.partial(own_kernel, math.log2(math.e) / math.sqrt(HD)),
        [SMEM] + [VMEM] * 3,
        [VMEM] * 3,
        [
            jax.ShapeDtypeStruct((tiles, 2 * HD, tokens), BF16),
            jax.ShapeDtypeStruct((tiles, HD, tokens), F32),
            jax.ShapeDtypeStruct((tiles, 8, tokens), F32),
        ],
        16 * tokens * width * 2 * tokens,
        tokens * width * 12,
        2 * tokens * tokens * tiles,
        stage_scratch(tokens),
    )(core, q_soft, q_other, kv)


def later_kernel(last, flag_ref, kv_ref, q_ref, acc_ref, stat_ref, *refs):
    if last:
        out_ref, *scratch = refs
    else:
        acc_out, stat_out, *scratch = refs
    keys_ref, values_ref = scratch[:2]
    scores, highs, lows, peaks = scratch[2:4], scratch[4:6], scratch[6:8], scratch[8:10]
    tiles, _, tokens = q_ref.shape
    group = tiles // 2

    def place(i):
        return 2 * i + flag_ref[1] if last else i

    def finish(i, acc, total):
        out_ref[:, pl.ds(pl.multiple_of(i * HD, HD), HD)] = (acc / total).T

    def load(i, slot):
        high_low = q_ref[place(i)]
        terms = jnp.concatenate([high_low, high_low[:HD]], axis=0)
        s = dot(keys_ref[...], terms)
        scores[slot][...] = s
        peaks[slot][0:1] = jnp.max(s, axis=0, keepdims=True)

    def soften(i, slot):
        old_peak = stat_ref[place(i), 0:1]
        peak = jnp.maximum(peaks[slot][0:1], old_peak)
        shrink = jnp.exp2(old_peak - peak)
        total = stat_ref[place(i), 1:2] * shrink
        for c in range(2):
            at = slice(c * tokens, (c + 1) * tokens)
            w = jnp.exp2(scores[slot][at] - peak)
            total = total + jnp.sum(w, axis=0, keepdims=True)
            highs[slot][at], lows[slot][at] = split(w)
        peaks[slot][1:2] = shrink
        peaks[slot][2:3] = total
        if not last:
            stat_out[place(i), 0:1] = peak
            stat_out[place(i), 1:2] = total

    def gather(i, slot):
        wide = dot(values_ref[...], highs[slot][...])
        new = wide[:HD] + wide[HD:] + dot(values_ref[:HD], lows[slot][...])
        acc = acc_ref[place(i)] * peaks[slot][1:2] + new
        if last:
            finish(i, acc, peaks[slot][2:3])
        else:
            acc_out[place(i)] = acc

    @pl.when(flag_ref[0] == 1)
    def _():
        keys_ref[...], values_ref[...] = key_terms(kv_ref)
        run_tiles(group if last else tiles, load, soften, gather)

    if last:

        @pl.when(flag_ref[0] == 0)
        def _():
            def only(i, carry):
                finish(i, acc_ref[place(i)], stat_ref[place(i), 1:2])
                return carry

            lax.fori_loop(0, group, only, 0)


def later_stage(flags, kv, q_terms, acc, stats, last):
    tiles, _, tokens = q_terms.shape
    if last:
        width = tiles // 2 * HD
        out_shape, out_specs, alias = jax.ShapeDtypeStruct((tokens, width), F32), VMEM, None
    else:
        out_shape = [jax.ShapeDtypeStruct(a.shape, F32) for a in (acc, stats)]
        out_specs, alias = [VMEM] * 2, {3: 0, 4: 1}
    share = 1 if last else 2
    return call(
        functools.partial(later_kernel, last),
        [SMEM] + [VMEM] * 4,
        out_specs,
        out_shape,
        share * 6 * tiles * HD * tokens * 2 * tokens,
        share * acc.size * 5,
        share * tokens * tokens * tiles,
        stage_scratch(tokens),
        alias=alias,
    )(flags, kv, q_terms, acc, stats)


def final_kernel(columns, core_ref, energy_ref, gain_ref, linear_ref, mine_ref, other_ref, lin_ref, soft_ref):
    energy = energy_ref[0]
    for i in range(1, energy_ref.shape[0]):
        energy = energy + energy_ref[i]
    factor = lax.rsqrt(energy / columns + EPSILON).T[:, 0:1]
    lin_ref[...] = linear_ref[...] * factor * gain_ref[...]
    soft_ref[...] = jnp.where(core_ref[0] == pl.program_id(0), mine_ref[...], other_ref[...])


def final(core, energies, gain, linear, mine, other, columns):
    tokens, width = linear.shape
    soft_half = mine.shape[1]
    half = pl.BlockSpec((tokens, width // 2), lambda j: (0, j))
    whole = pl.BlockSpec((tokens, soft_half), lambda j: (0, 0))
    return call(
        functools.partial(final_kernel, columns),
        [
            SMEM,
            pl.BlockSpec(energies.shape, lambda j: (0, 0, 0)),
            pl.BlockSpec((1, width // 2), lambda j: (0, j)),
            half,
            whole,
            whole,
        ],
        [half, pl.BlockSpec((tokens, soft_half), lambda j: (0, j))],
        [
            jax.ShapeDtypeStruct((tokens, width), F32),
            jax.ShapeDtypeStruct((tokens, 2 * soft_half), F32),
        ],
        tokens * width * 2,
        tokens * (width + 2 * soft_half) * 8,
        grid=(2,),
    )(core, energies, gain, linear, mine, other)


def body(q_lin, k_lin, v_lin, log_decay, lin_gain, q_soft, k_soft, v_soft):
    devices = lax.axis_size("ctx")
    chips = devices // 2
    heads = lax.axis_size("head")
    me = lax.axis_index("ctx")
    core, chip = me % 2, me // 2
    assert k_soft.shape[1] == 2 * HD

    def as_flags(*values):
        return jnp.stack([jnp.asarray(value).astype(jnp.int32) for value in values])

    core_flag = as_flags(core)
    swap_pairs = [(2 * c + e, 2 * c + 1 - e) for c in range(chips) for e in range(2)]

    def swap(array):
        return lax.ppermute(array, "ctx", swap_pairs)

    k_other, v_other, q_other = swap(k_soft), swap(v_soft), swap(q_soft)
    kv = pair_block(core_flag, k_soft, v_soft, k_other, v_other)
    arrived = [
        lax.ppermute(
            kv,
            "ctx",
            [
                (2 * (c ^ distance) + e, 2 * c + e)
                for c in range(chips)
                if c ^ distance < c
                for e in range(2)
            ],
        )
        for distance in range(1, chips)
    ]

    states, sums = local_states(log_decay, k_lin, v_lin, devices)
    states = lax.all_to_all(states, "ctx", 0, 0, tiled=True)
    prior = lax.all_to_all(chained(states), "ctx", 0, 0, tiled=True)
    prior = prior.reshape(-1, HD)
    inside = inside_blocks(q_lin, k_lin, v_lin, sums)

    q_terms, acc, stats = own_stage(core_flag, q_soft, q_other, kv)
    for distance in range(1, chips - 1):
        flags = as_flags((chip ^ distance) < chip, 0)
        acc, stats = later_stage(flags, arrived[distance - 1], q_terms, acc, stats, False)

    linear, energy = linear_blocks(q_lin, inside, sums, prior, heads)
    energies = lax.all_to_all(energy, "head", 0, 0, tiled=True)

    visible = (chip ^ (chips - 1)) < chip
    theirs = later_stage(as_flags(visible, 1 - core), arrived[-1], q_terms, acc, stats, True)
    other = swap(theirs)
    mine = later_stage(as_flags(visible, core), arrived[-1], q_terms, acc, stats, True)
    columns = q_lin.shape[1] * heads
    return final(core_flag, energies, lin_gain.reshape(1, -1), linear, mine, other, columns)


def solution(mesh):
    return jax.shard_map(
        body,
        mesh=mesh,
        in_specs=(
            P("ctx", "head"),
            P("ctx", "head"),
            P("ctx", "head"),
            P("head", "ctx"),
            P("head"),
            P("ctx", "head"),
            P("ctx", "head"),
            P("ctx", "head"),
        ),
        out_specs=(P("ctx", "head"), P("ctx", "head")),
        check_vma=False,
    )
```

```python
import functools
import math

import jax
import jax.numpy as jnp
from jax import lax
from jax.experimental import pallas as pl
from jax.experimental.pallas import tpu as pltpu
from jax.sharding import PartitionSpec as P

HD = 128
NEGATIVE = -1e30
EPSILON = 1e-05
F32 = jnp.float32
BF16 = jnp.bfloat16
NT = (((1,), (1,)), ((), ()))
VMEM_LIMIT = 32 * 1024 * 1024
VMEM = pl.BlockSpec(memory_space=pltpu.VMEM)
SMEM = pl.BlockSpec(memory_space=pltpu.SMEM)
ANY = pl.BlockSpec(memory_space=pl.ANY)
HBM = pl.BlockSpec(memory_space=pltpu.HBM)


def split(x):
    high = x.astype(BF16)
    low = (x - high.astype(F32)).astype(BF16)
    return high, low


def dot(a, b):
    return jnp.dot(a, b, preferred_element_type=F32)


def three_term(a, b):
    a_high, a_low = split(a)
    b_high, b_low = split(b)
    wide = dot(a_high, jnp.concatenate([b_high, b_low], axis=1))
    n = b.shape[1]
    return wide[:, :n] + wide[:, n:] + dot(a_low, b_high)


def call(kernel, in_specs, out_specs, out_shape, flops, size, exps=0, scratch=(), alias=None, after=()):
    count = len(in_specs)

    def ordered(*refs):
        kernel(*refs[:count], *refs[count + len(after) :])

    made = pl.pallas_call(
        ordered,
        in_specs=in_specs + [ANY] * len(after),
        out_specs=out_specs,
        out_shape=out_shape,
        scratch_shapes=list(scratch),
        input_output_aliases=alias or {},
        cost_estimate=pl.CostEstimate(flops=1, bytes_accessed=1, transcendentals=0),
        compiler_params=pltpu.CompilerParams(vmem_limit_bytes=VMEM_LIMIT),
    )
    return lambda *operands: made(*operands, *after)


def column_copy(source, at, target, sem):
    copy = pltpu.make_async_copy(source.at[:, at], target, sem)
    copy.start()
    return copy


def head_copies(source, target, sems):
    return [
        column_copy(source, pl.ds(h * HD, HD), target.at[h], sems.at[h])
        for h in range(target.shape[0])
    ]


def state_kernel(rate_hbm, k_hbm, v_hbm, packed_ref, sums_ref, rate_ref, k_ref, v_ref, sem, k_sem, v_sem):
    tokens = k_hbm.shape[0]
    heads = rate_hbm.shape[0]
    half = heads // 2
    rate_copy = pltpu.make_async_copy(rate_hbm, rate_ref, sem)
    rate_copy.start()
    copies = list(zip(head_copies(k_hbm, k_ref, k_sem), head_copies(v_hbm, v_ref, v_sem)))
    upto = lax.broadcasted_iota(jnp.int32, (tokens, tokens), 0)
    upto = (upto <= lax.broadcasted_iota(jnp.int32, (tokens, tokens), 1)).astype(F32)
    rate_copy.wait()
    sums = jnp.dot(
        rate_ref[...], upto, precision=lax.Precision.HIGHEST, preferred_element_type=F32
    )
    sums_ref[...] = sums
    totals = sums[:, tokens - 1 : tokens]
    trailing = jnp.exp(totals - sums)
    for side in range(2):
        packed_ref[side, half * HD :] = jnp.zeros((8, HD), F32)
    for h in range(heads):
        side, i = h // half, h % half
        for copy in copies[h]:
            copy.wait()
        packed_ref[side, i * HD : (i + 1) * HD] = three_term(
            k_ref[h].T * trailing[h : h + 1], v_ref[h]
        )
        packed_ref[side, half * HD + i : half * HD + i + 1] = jnp.broadcast_to(
            totals[h : h + 1], (1, HD)
        )


def local_states(rates, k_lin, v_lin, after):
    tokens, width = k_lin.shape
    heads = rates.shape[0]
    return call(
        state_kernel,
        [HBM] * 3,
        [VMEM] * 2,
        [
            jax.ShapeDtypeStruct((2, heads // 2 * HD + 8, HD), F32),
            jax.ShapeDtypeStruct((heads, tokens), F32),
        ],
        6 * tokens * width * HD,
        10 * tokens * width,
        tokens * heads,
        [
            pltpu.VMEM((heads, tokens), F32),
            pltpu.VMEM((heads, tokens, HD), F32),
            pltpu.VMEM((heads, tokens, HD), F32),
            pltpu.SemaphoreType.DMA,
            pltpu.SemaphoreType.DMA((heads,)),
            pltpu.SemaphoreType.DMA((heads,)),
        ],
        after=after,
    )(rates, k_lin, v_lin)


def join(half, first, second, out_ref):
    decay = jnp.exp(second[half * HD :, :])
    for i in range(half):
        at = slice(i * HD, (i + 1) * HD)
        out_ref[at] = first[at] * decay[i : i + 1] + second[at]
    out_ref[half * HD :] = first[half * HD :] + second[half * HD :]


def chip_kernel(half, flags_ref, states_ref, others_ref, out_ref):
    core = flags_ref[0]

    @pl.when(core == 0)
    def _():
        join(half, states_ref[0], others_ref[0], out_ref)

    @pl.when(core == 1)
    def _():
        join(half, others_ref[1], states_ref[1], out_ref)


def chip_total(flags, states, others, after):
    _, packed, _ = states.shape
    return call(
        functools.partial(chip_kernel, (packed - 8) // HD),
        [SMEM, VMEM, VMEM],
        VMEM,
        jax.ShapeDtypeStruct((packed, HD), F32),
        packed * HD * 2,
        packed * HD * 12,
        after=after,
    )(flags, states, others)


def turn_kernel(half, bit, first, last, flags_ref, total_ref, theirs_ref, *refs):
    refs = list(refs)
    before_ref = None if first else refs.pop(0)
    prefix_ref = refs.pop(0)
    total_out = None if last else refs.pop(0)
    late = lax.rem(lax.div(flags_ref[1], 1 << bit), 2)

    @pl.when(late == 0)
    def _():
        prefix_ref[...] = jnp.zeros_like(prefix_ref) if first else before_ref[...]
        if not last:
            join(half, total_ref[...], theirs_ref[...], total_out)

    @pl.when(late == 1)
    def _():
        if first:
            prefix_ref[...] = theirs_ref[...]
        else:
            join(half, theirs_ref[...], before_ref[...], prefix_ref)
        if not last:
            join(half, theirs_ref[...], total_ref[...], total_out)


def turn(flags, bit, total, theirs, before, last, after):
    packed = total.shape[0]
    operands = [total, theirs] + ([] if before is None else [before])
    count = 1 if last else 2
    out = call(
        functools.partial(turn_kernel, (packed - 8) // HD, bit, before is None, last),
        [SMEM] + [VMEM] * len(operands),
        [VMEM] * count,
        [jax.ShapeDtypeStruct((packed, HD), F32)] * count,
        packed * HD * 4,
        packed * HD * 16,
        after=after,
    )(flags, *operands)
    return out[0], (None if last else out[1])


def inside_kernel(q_hbm, k_hbm, v_hbm, sums_ref, out_ref, terms_ref, q_ref, k_ref, v_ref, q_sem, k_sem, v_sem):
    tokens = q_hbm.shape[0]
    heads = sums_ref.shape[0]
    copies = list(
        zip(
            head_copies(q_hbm, q_ref, q_sem),
            head_copies(k_hbm, k_ref, k_sem),
            head_copies(v_hbm, v_ref, v_sem),
        )
    )
    causal = lax.broadcasted_iota(jnp.int32, (tokens, tokens), 0) >= lax.broadcasted_iota(
        jnp.int32, (tokens, tokens), 1
    )
    columns = sums_ref[...].T
    for h in range(heads):
        for copy in copies[h]:
            copy.wait()
        q_high, q_low = split(q_ref[h])
        k_high, k_low = split(k_ref[h])
        terms_ref[h, :, :HD] = q_high
        terms_ref[h, :, HD:] = q_low
        scores = lax.dot_general(
            jnp.concatenate([q_high, q_low, q_high], axis=1),
            jnp.concatenate([k_high, k_high, k_low], axis=1),
            NT,
            preferred_element_type=F32,
        )
        gaps = columns[:, h : h + 1] - sums_ref[h : h + 1, :]
        weights = jnp.where(causal, jnp.exp(jnp.where(causal, gaps, 0.0)), 0.0)
        out_ref[h] = three_term(scores * weights, v_ref[h])


def inside_blocks(q_lin, k_lin, v_lin, sums):
    tokens, width = q_lin.shape
    heads = sums.shape[0]
    return call(
        inside_kernel,
        [HBM] * 3 + [VMEM],
        [VMEM] * 2,
        [
            jax.ShapeDtypeStruct((heads, tokens, HD), F32),
            jax.ShapeDtypeStruct((heads, tokens, 2 * HD), BF16),
        ],
        12 * tokens * tokens * width,
        16 * tokens * width,
        tokens * tokens * heads,
        [pltpu.VMEM((heads, tokens, HD), F32)] * 3 + [pltpu.SemaphoreType.DMA((heads,))] * 3,
    )(q_lin, k_lin, v_lin, sums)


def linear_kernel(flags_ref, terms_ref, inside_ref, sums_ref, mine_ref, theirs_ref, other_ref, out_ref, energy_ref):
    heads, tokens, _ = out_ref.shape
    half = heads // 2
    core = flags_ref[0]
    leading = jnp.exp(sums_ref[...]).T
    squares = jnp.zeros((tokens, HD), F32)
    for side in range(2):
        decay = jnp.exp(other_ref[side, half * HD :])
        for i in range(half):
            h = side * half + i
            at = slice(i * HD, (i + 1) * HD)
            prior = jnp.where(core == side, mine_ref[at], theirs_ref[at])
            prior = jnp.where(core == 1, prior * decay[i : i + 1] + other_ref[side, at], prior)
            high, low = split(prior)
            wide = dot(terms_ref[h, :, :HD], jnp.concatenate([high, low], axis=1))
            carried = wide[:, :HD] + wide[:, HD:] + dot(terms_ref[h, :, HD:], high)
            linear = inside_ref[h] + leading[:, h : h + 1] * carried
            out_ref[h] = linear
            squares = squares + linear * linear
    energy_ref[...] = lax.dot_general(
        jnp.ones((8, HD), F32),
        squares,
        NT,
        precision=lax.Precision.HIGHEST,
        preferred_element_type=F32,
    )


def linear_blocks(flags, terms, inside, sums, mine, theirs, other, after):
    heads, tokens, _ = inside.shape
    width = heads * HD
    return call(
        linear_kernel,
        [SMEM] + [VMEM] * 6,
        [VMEM] * 2,
        [
            jax.ShapeDtypeStruct(inside.shape, F32),
            jax.ShapeDtypeStruct((8, tokens), F32),
        ],
        6 * tokens * width * HD,
        14 * tokens * width,
        after=after,
    )(flags, terms, inside, sums, mine, theirs, other)


def norm_kernel(columns, energy_ref, other_ref, gain_ref, linear_ref, out_hbm, out_ref, sems):
    heads = linear_ref.shape[0]
    factor = lax.rsqrt((energy_ref[...] + other_ref[...]) / columns + EPSILON).T[:, 0:1]
    copies = []
    for h in range(heads):
        at = slice(h * HD, (h + 1) * HD)
        out_ref[h] = linear_ref[h] * factor * gain_ref[:, at]
        copy = pltpu.make_async_copy(out_ref.at[h], out_hbm.at[:, pl.ds(h * HD, HD)], sems.at[h])
        copy.start()
        copies.append(copy)
    for copy in copies:
        copy.wait()


def normalized(energy, other, gain, linear, columns, after):
    heads, tokens, _ = linear.shape
    return call(
        functools.partial(norm_kernel, columns),
        [VMEM] * 4,
        ANY,
        jax.ShapeDtypeStruct((tokens, heads * HD), F32),
        linear.size * 2,
        linear.size * 8,
        0,
        [pltpu.VMEM(linear.shape, F32), pltpu.SemaphoreType.DMA((heads,))],
        after=after,
    )(energy, other, gain, linear)


def pair_kernel(flags_ref, k_ref, v_ref, k_other_ref, v_other_ref, out_ref):
    core = flags_ref[0]
    tokens = k_ref.shape[0]
    at = pl.ds(pl.multiple_of(core * HD, HD), HD)
    for side, (mine_ref, other_ref) in enumerate([(k_ref, k_other_ref), (v_ref, v_other_ref)]):
        to = slice(side * HD, (side + 1) * HD)
        out_ref[pl.ds(core * tokens, tokens), to] = mine_ref[:, at]
        out_ref[pl.ds((1 - core) * tokens, tokens), to] = other_ref[:, at]


def pair_block(flags, k_soft, v_soft, k_other, v_other):
    tokens = k_soft.shape[0]
    return call(
        pair_kernel,
        [SMEM] + [VMEM] * 4,
        VMEM,
        jax.ShapeDtypeStruct((2 * tokens, 2 * HD), F32),
        tokens * HD * 4,
        tokens * HD * 48,
    )(flags, k_soft, v_soft, k_other, v_other)


def run_heads(count, load, soften, gather):
    load(0, 0)
    load(1, 1)
    soften(0, 0)

    def turn(j, carry):
        for i, slot in ((2 * j + 1, 1), (2 * j + 2, 0)):
            load(i + 1, 1 - slot)
            gather(i - 1, 1 - slot)
            soften(i, slot)
        return carry

    lax.fori_loop(0, count // 2 - 1, turn, 0)
    gather(count - 2, 0)
    soften(count - 1, 1)
    gather(count - 1, 1)


def fill_terms(kv_ref, keys_ref, values_ref):
    k_high, k_low = split(kv_ref[:, :HD].T)
    keys_ref[:HD] = k_high
    keys_ref[HD : 2 * HD] = k_high
    keys_ref[2 * HD :] = k_low
    v_high, v_low = split(kv_ref[:, HD:])
    values_ref[:, :HD] = v_high
    values_ref[:, HD:] = v_low


def lane_max(array):
    peak = array[:, :HD]
    for c in range(1, array.shape[1] // HD):
        peak = jnp.maximum(peak, array[:, c * HD : (c + 1) * HD])
    return peak


def score_terms(pair):
    return jnp.concatenate([pair, pair[:, :HD]], axis=1)


def weigh(scores_ref, rows, count, peak, total, high_ref, low_ref):
    for c in range(count // HD):
        at = slice(c * HD, (c + 1) * HD)
        w = jnp.exp2(scores_ref[rows, at] - peak)
        total = total + w
        high_ref[rows, at], low_ref[rows, at] = split(w)
    return total


def summed(high, low, values):
    wide = dot(high, values)
    return wide[:, :HD] + wide[:, HD:] + dot(low, values[:, :HD])


def own_kernel(factor, flags_ref, q_hbm, q_other_hbm, kv_ref, q_out, acc_out, peak_out, total_out, *scratch):
    keys_ref, values_ref = scratch[:2]
    scores, highs, lows, peaks = scratch[2:4], scratch[4:6], scratch[6:8], scratch[8:10]
    q_ref, sems = scratch[12:]
    core = flags_ref[0]
    tokens = q_hbm.shape[0]
    group = q_out.shape[0]
    copies = []
    for g in range(group):
        at = pl.ds(pl.multiple_of((core * group + g) * HD, HD), HD)
        mine = q_ref.at[g, pl.ds(pl.multiple_of(core * tokens, tokens), tokens)]
        other = q_ref.at[g, pl.ds(pl.multiple_of((1 - core) * tokens, tokens), tokens)]
        copies.append(
            (
                column_copy(q_hbm, at, mine, sems.at[g, 0]),
                column_copy(q_other_hbm, at, other, sems.at[g, 1]),
            )
        )
    fill_terms(kv_ref, keys_ref, values_ref)
    for g in range(group):
        for copy in copies[g]:
            copy.wait()
        high, low = split(q_ref[g] * factor)
        q_out[g, :, :HD] = high
        q_out[g, :, HD:] = low

    seen = lax.broadcasted_iota(jnp.int32, (tokens, tokens), 1)
    seen = seen <= lax.broadcasted_iota(jnp.int32, (tokens, tokens), 0)
    early, late = slice(0, tokens), slice(tokens, 2 * tokens)

    def load(g, slot):
        terms = score_terms(q_out[g])
        left = dot(terms, keys_ref[:, early])
        right = dot(terms[late], keys_ref[:, late])
        edge = jnp.where(seen, left[early], NEGATIVE)
        far = jnp.where(seen, right, NEGATIVE)
        scores[slot][early, early] = edge
        scores[slot][late, early] = left[late]
        scores[slot][late, late] = far
        peaks[slot][early] = lane_max(edge)
        peaks[slot][late] = jnp.maximum(lane_max(left[late]), lane_max(far))

    def soften(g, slot):
        peak = jnp.max(peaks[slot][...], axis=1, keepdims=True)
        peak = jnp.broadcast_to(peak, (2 * tokens, HD))
        peak_out[g] = peak
        zero = jnp.zeros((tokens, HD), F32)
        total_out[g, early] = weigh(
            scores[slot], early, tokens, peak[early], zero, highs[slot], lows[slot]
        )
        total_out[g, late] = weigh(
            scores[slot], late, 2 * tokens, peak[late], zero, highs[slot], lows[slot]
        )

    def gather(g, slot):
        acc_out[g, early] = summed(
            highs[slot][early, early], lows[slot][early, early], values_ref[early]
        )
        acc_out[g, late] = summed(highs[slot][late], lows[slot][late], values_ref[...])

    run_heads(group, load, soften, gather)


def stage_scratch(rows, keys):
    return [
        *[pltpu.VMEM((rows, keys), F32)] * 2,
        *[pltpu.VMEM((rows, keys), BF16)] * 4,
        *[pltpu.VMEM((rows, HD), F32)] * 4,
    ]


def own_stage(flags, q_soft, q_other, kv, after):
    tokens, width = q_soft.shape
    group = width // (2 * HD)
    stat = jax.ShapeDtypeStruct((group, 2 * tokens, HD), F32)
    return call(
        functools.partial(own_kernel, math.log2(math.e) / math.sqrt(HD)),
        [SMEM, HBM, ANY, VMEM],
        [VMEM] * 4,
        [jax.ShapeDtypeStruct((group, 2 * tokens, 2 * HD), BF16), stat, stat, stat],
        16 * tokens * width * 2 * tokens,
        tokens * width * 12,
        4 * tokens * tokens * group,
        [
            pltpu.VMEM((3 * HD, 2 * tokens), BF16),
            pltpu.VMEM((2 * tokens, 2 * HD), BF16),
            *stage_scratch(2 * tokens, 2 * tokens),
            pltpu.VMEM((group, 2 * tokens, HD), F32),
            pltpu.SemaphoreType.DMA((group, 2)),
        ],
        after=after,
    )(flags, q_soft, q_other, kv)


def later_kernel(distance, flags_ref, kv_ref, q_ref, acc_ref, peak_ref, total_ref, acc_out, peak_out, total_out, *scratch):
    keys_ref, values_ref = scratch[:2]
    scores, highs, lows, peaks = scratch[2:4], scratch[4:6], scratch[6:8], scratch[8:10]
    shrinks = scratch[10:12]
    group, rows, _ = q_ref.shape
    everything = slice(0, rows)
    chip = flags_ref[1]

    def load(g, slot):
        s = dot(score_terms(q_ref[g]), keys_ref[...])
        scores[slot][...] = s
        peaks[slot][...] = lane_max(s)

    def soften(g, slot):
        old = peak_ref[g]
        peak = jnp.maximum(jnp.max(peaks[slot][...], axis=1, keepdims=True), old)
        shrink = jnp.exp2(old - peak)
        peak_out[g] = peak
        total_out[g] = weigh(
            scores[slot], everything, keys_ref.shape[1], peak, total_ref[g] * shrink,
            highs[slot], lows[slot],
        )
        shrinks[slot][...] = shrink

    def gather(g, slot):
        acc_out[g] = acc_ref[g] * shrinks[slot][...] + summed(
            highs[slot][...], lows[slot][...], values_ref[...]
        )

    @pl.when(lax.bitwise_xor(chip, distance) < chip)
    def _():
        fill_terms(kv_ref, keys_ref, values_ref)
        run_heads(group, load, soften, gather)


def later_stage(flags, distance, kv, q_terms, acc, peak, total, after):
    group, rows, _ = q_terms.shape
    keys = kv.shape[0]
    return call(
        functools.partial(later_kernel, distance),
        [SMEM] + [VMEM] * 5,
        [VMEM] * 3,
        [jax.ShapeDtypeStruct(acc.shape, F32)] * 3,
        12 * group * HD * rows * keys,
        acc.size * 8,
        rows * keys * group,
        [
            pltpu.VMEM((3 * HD, keys), BF16),
            pltpu.VMEM((keys, 2 * HD), BF16),
            *stage_scratch(rows, keys),
        ],
        alias={3: 0, 4: 1, 5: 2},
        after=after,
    )(flags, kv, q_terms, acc, peak, total)


def last_kernel(distance, whose, flags_ref, kv_ref, q_ref, acc_ref, peak_ref, total_ref, out, *scratch):
    keys_ref, values_ref = scratch[:2]
    scores, highs, lows, peaks = scratch[2:4], scratch[4:6], scratch[6:8], scratch[8:10]
    shrinks, totals, scratch = scratch[10:12], scratch[12:14], scratch[14:]
    group, rows, _ = q_ref.shape
    tokens = rows // 2
    everything = slice(0, tokens)
    core, chip = flags_ref[0], flags_ref[1]
    side = core if whose == "own" else 1 - core
    at = pl.ds(pl.multiple_of(side * tokens, tokens), tokens)

    def copy_out(g):
        out_ref, sems = scratch
        to = pl.ds(pl.multiple_of((core * group + g) * HD, HD), HD)
        return pltpu.make_async_copy(out_ref.at[g], out.at[:, to], sems.at[g])

    def finish(g, acc, total):
        result = acc / jnp.sum(total, axis=1, keepdims=True)
        if whose == "own":
            scratch[0][g] = result
            copy_out(g).start()
        else:
            out[g] = result

    def load(g, slot):
        s = dot(score_terms(q_ref[g, at]), keys_ref[...])
        scores[slot][...] = s
        peaks[slot][...] = lane_max(s)

    def soften(g, slot):
        old = peak_ref[g, at]
        peak = jnp.maximum(jnp.max(peaks[slot][...], axis=1, keepdims=True), old)
        shrink = jnp.exp2(old - peak)
        totals[slot][...] = weigh(
            scores[slot], everything, keys_ref.shape[1], peak, total_ref[g, at] * shrink,
            highs[slot], lows[slot],
        )
        shrinks[slot][...] = shrink

    def gather(g, slot):
        acc = acc_ref[g, at] * shrinks[slot][...] + summed(
            highs[slot][...], lows[slot][...], values_ref[...]
        )
        finish(g, acc, totals[slot][...])

    visible = lax.bitwise_xor(chip, distance) < chip

    @pl.when(visible)
    def _():
        fill_terms(kv_ref, keys_ref, values_ref)
        run_heads(group, load, soften, gather)

    @pl.when(jnp.logical_not(visible))
    def _():
        for g in range(group):
            finish(g, acc_ref[g, at], total_ref[g, at])

    if whose == "own":
        for g in range(group):
            copy_out(g).wait()


def last_stage(flags, distance, whose, kv, q_terms, acc, peak, total, after):
    group, rows, _ = q_terms.shape
    keys, tokens = kv.shape[0], rows // 2
    scratch = [
        pltpu.VMEM((3 * HD, keys), BF16),
        pltpu.VMEM((keys, 2 * HD), BF16),
        *stage_scratch(tokens, keys),
        *[pltpu.VMEM((tokens, HD), F32)] * 2,
    ]
    if whose == "own":
        out_shape, out_spec = jax.ShapeDtypeStruct((tokens, 2 * group * HD), F32), ANY
        scratch += [pltpu.VMEM((group, tokens, HD), F32), pltpu.SemaphoreType.DMA((group,))]
    else:
        out_shape, out_spec = jax.ShapeDtypeStruct((group, tokens, HD), F32), VMEM
    return call(
        functools.partial(last_kernel, distance, whose),
        [SMEM] + [VMEM] * 5,
        out_spec,
        out_shape,
        6 * group * HD * rows * keys,
        acc.size * 4,
        rows * keys * group // 2,
        scratch,
        after=after,
    )(flags, kv, q_terms, acc, peak, total)


def place_kernel(flags_ref, other_ref, soft_hbm, out_hbm, sems):
    group = other_ref.shape[0]
    copies = []
    for g in range(group):
        to = pl.ds(pl.multiple_of(((1 - flags_ref[0]) * group + g) * HD, HD), HD)
        copy = pltpu.make_async_copy(other_ref.at[g], out_hbm.at[:, to], sems.at[g])
        copy.start()
        copies.append(copy)
    for copy in copies:
        copy.wait()


def placed(flags, other, soft):
    return call(
        place_kernel,
        [SMEM, VMEM, ANY],
        ANY,
        jax.ShapeDtypeStruct(soft.shape, F32),
        0,
        other.size * 8,
        0,
        [pltpu.SemaphoreType.DMA((other.shape[0],))],
        alias={2: 0},
    )(flags, other, soft)


def plus_kernel(a_ref, b_ref, out_ref):
    out_ref[...] = a_ref[...] + b_ref[...]


def plus(a, b, after):
    return call(
        plus_kernel, [VMEM] * 2, VMEM, jax.ShapeDtypeStruct(a.shape, F32), a.size, a.size * 12, after=after
    )(a, b)


def relay_kernel(flags_ref, beside_ref, across_ref, out_ref):
    @pl.when(flags_ref[0] == 0)
    def _():
        out_ref[...] = beside_ref[...]

    @pl.when(flags_ref[0] == 1)
    def _():
        out_ref[...] = across_ref[...]


def relayed(flags, beside, across, after):
    return call(
        relay_kernel,
        [SMEM, VMEM, VMEM],
        VMEM,
        jax.ShapeDtypeStruct(beside.shape, F32),
        beside.size,
        beside.size * 8,
        after=after,
    )(flags, beside, across)


def body(q_lin, k_lin, v_lin, log_decay, lin_gain, q_soft, k_soft, v_soft):
    chips = lax.axis_size("ctx") // 2
    heads = lax.axis_size("head")
    me = lax.axis_index("ctx")
    flags = jnp.stack([me & 1, me >> 1]).astype(jnp.int32)
    assert k_soft.shape[1] == 2 * HD
    swap_pairs = [(2 * c + e, 2 * c + 1 - e) for c in range(chips) for e in range(2)]

    def swap(array):
        return lax.ppermute(array, "ctx", swap_pairs)

    def across(array, distance, wanted=lambda c, e: True):
        pairs = [
            (2 * (c ^ distance) + e, 2 * c + e)
            for c in range(chips)
            for e in range(2)
            if wanted(c, e)
        ]
        return lax.ppermute(array, "ctx", pairs)

    square = chips == 4
    k_other, v_other, q_other = swap(k_soft), swap(v_soft), swap(q_soft)
    kv = pair_block(flags, k_soft, v_soft, k_other, v_other)
    arrived = {}
    for distance in range(1, chips - 1 if square else chips):
        arrived[distance] = across(
            kv,
            distance,
            lambda c, e, d=distance: c ^ d < c or (square and d == 1 and c == 0 and e == 0),
        )

    states, sums = local_states(log_decay, k_lin, v_lin, [kv])
    others = swap(states)
    inside, terms = inside_blocks(q_lin, k_lin, v_lin, sums)
    total, prefix = chip_total(flags, states, others, [inside]), None

    q_terms, *carried = own_stage(flags, q_soft, q_other, kv, [total])
    if square:
        relay = relayed(flags, arrived[1], arrived[2], [carried[0]])
        pairs = [(2, 6), (0, 4), (5, 7), (7, 5)]
        arrived[3] = lax.ppermute(relay, "ctx", pairs)
        token = relay
    else:
        token = carried[0]

    bits = chips.bit_length() - 1
    for bit in range(bits):
        last = bit == bits - 1
        theirs = across(total, 1 << bit, lambda c, e: not last or c ^ (1 << bit) < c)
        prefix, total = turn(flags, bit, total, theirs, prefix, last, [token])
        distance = bit + 1
        carried = later_stage(flags, distance, arrived[distance], q_terms, *carried, [prefix])
        token = carried[0]
    prefix_other = swap(prefix)
    for distance in range(bits + 1, chips - 1):
        carried = later_stage(flags, distance, arrived[distance], q_terms, *carried, [])

    linear, energy = linear_blocks(
        flags, terms, inside, sums, prefix, prefix_other, others, [carried[0]]
    )

    def exchanged(array, step):
        return lax.ppermute(array, "head", [(i, i ^ step) for i in range(heads)])

    operands = (arrived[chips - 1], q_terms, *carried)
    theirs = last_stage(flags, chips - 1, "other", *operands, [energy])
    step, other = 1, exchanged(energy, 1)
    while 2 * step < heads:
        step *= 2
        energy = plus(energy, other, [theirs])
        other = exchanged(energy, step)
    soft_out = last_stage(flags, chips - 1, "own", *operands, [energy])
    columns = q_lin.shape[1] * heads
    lin_out = normalized(energy, other, lin_gain.reshape(1, -1), linear, columns, [])
    soft_out = placed(flags, swap(theirs), soft_out)
    return (lin_out, soft_out)


def solution(mesh):
    return jax.shard_map(
        body,
        mesh=mesh,
        in_specs=(
            P("ctx", "head"),
            P("ctx", "head"),
            P("ctx", "head"),
            P("head", "ctx"),
            P("head"),
            P("ctx", "head"),
            P("ctx", "head"),
            P("ctx", "head"),
        ),
        out_specs=(P("ctx", "head"), P("ctx", "head")),
        check_vma=False,
    )
```

```python
import functools
import math

import jax
import jax.numpy as jnp
from jax import lax
from jax.experimental import pallas as pl
from jax.experimental.pallas import tpu as pltpu
from jax.sharding import PartitionSpec as P

HD = 128
NEGATIVE = -1e30
EPSILON = 1e-05
F32 = jnp.float32
BF16 = jnp.bfloat16
NT = (((1,), (1,)), ((), ()))
VMEM_LIMIT = 32 * 1024 * 1024
VMEM = pl.BlockSpec(memory_space=pltpu.VMEM)
SMEM = pl.BlockSpec(memory_space=pltpu.SMEM)
ANY = pl.BlockSpec(memory_space=pl.ANY)
HBM = pl.BlockSpec(memory_space=pltpu.HBM)


def split(x):
    high = x.astype(BF16)
    low = (x - high.astype(F32)).astype(BF16)
    return high, low


def dot(a, b):
    return jnp.dot(a, b, preferred_element_type=F32)


def three_term(a, b):
    a_high, a_low = split(a)
    b_high, b_low = split(b)
    wide = dot(a_high, jnp.concatenate([b_high, b_low], axis=1))
    n = b.shape[1]
    return wide[:, :n] + wide[:, n:] + dot(a_low, b_high)


def call(kernel, in_specs, out_specs, out_shape, scratch=(), alias=None, after=()):
    count = len(in_specs)

    def ordered(*refs):
        kernel(*refs[:count], *refs[count + len(after) :])

    made = pl.pallas_call(
        ordered,
        in_specs=in_specs + [ANY] * len(after),
        out_specs=out_specs,
        out_shape=out_shape,
        scratch_shapes=list(scratch),
        input_output_aliases=alias or {},
        cost_estimate=pl.CostEstimate(flops=1, bytes_accessed=1, transcendentals=0),
        compiler_params=pltpu.CompilerParams(vmem_limit_bytes=VMEM_LIMIT),
    )
    return lambda *operands: made(*operands, *after)


def state_kernel(rate_ref, k_ref, v_ref, packed_ref, sums_ref):
    tokens = k_ref.shape[0]
    heads = rate_ref.shape[0]
    half = heads // 2
    upto = lax.broadcasted_iota(jnp.int32, (tokens, tokens), 0)
    upto = (upto <= lax.broadcasted_iota(jnp.int32, (tokens, tokens), 1)).astype(F32)
    sums = jnp.dot(
        rate_ref[...], upto, precision=lax.Precision.HIGHEST, preferred_element_type=F32
    )
    sums_ref[...] = sums
    totals = sums[:, tokens - 1 : tokens]
    trailing = jnp.exp(totals - sums)
    for side in range(2):
        packed_ref[side, half * HD :] = jnp.zeros((8, HD), F32)
    for h in range(heads):
        side, i = h // half, h % half
        at = slice(h * HD, (h + 1) * HD)
        packed_ref[side, i * HD : (i + 1) * HD] = three_term(
            k_ref[:, at].T * trailing[h : h + 1], v_ref[:, at]
        )
        packed_ref[side, half * HD + i : half * HD + i + 1] = jnp.broadcast_to(
            totals[h : h + 1], (1, HD)
        )


def local_states(rates, k_lin, v_lin, after):
    tokens = k_lin.shape[0]
    heads = rates.shape[0]
    return call(
        state_kernel,
        [VMEM] * 3,
        [VMEM] * 2,
        [
            jax.ShapeDtypeStruct((2, heads // 2 * HD + 8, HD), F32),
            jax.ShapeDtypeStruct((heads, tokens), F32),
        ],
        after=after,
    )(rates, k_lin, v_lin)


def join(half, first, second, out_ref):
    decay = jnp.exp(second[half * HD :, :])
    for i in range(half):
        at = slice(i * HD, (i + 1) * HD)
        out_ref[at] = first[at] * decay[i : i + 1] + second[at]
    out_ref[half * HD :] = first[half * HD :] + second[half * HD :]


def chip_kernel(half, me_ref, states_ref, others_ref, out_ref):
    core = me_ref[0] & 1

    @pl.when(core == 0)
    def _():
        join(half, states_ref[0], others_ref[0], out_ref)

    @pl.when(core == 1)
    def _():
        join(half, others_ref[1], states_ref[1], out_ref)


def chip_total(me, states, others, after):
    _, packed, _ = states.shape
    return call(
        functools.partial(chip_kernel, (packed - 8) // HD),
        [SMEM, VMEM, VMEM],
        VMEM,
        jax.ShapeDtypeStruct((packed, HD), F32),
        after=after,
    )(me, states, others)


def turn_kernel(half, bit, first, last, me_ref, total_ref, theirs_ref, *refs):
    refs = list(refs)
    before_ref = None if first else refs.pop(0)
    prefix_ref = refs.pop(0)
    total_out = None if last else refs.pop(0)
    late = (me_ref[0] >> (bit + 1)) & 1

    @pl.when(late == 0)
    def _():
        prefix_ref[...] = jnp.zeros_like(prefix_ref) if first else before_ref[...]
        if not last:
            join(half, total_ref[...], theirs_ref[...], total_out)

    @pl.when(late == 1)
    def _():
        if first:
            prefix_ref[...] = theirs_ref[...]
        else:
            join(half, theirs_ref[...], before_ref[...], prefix_ref)
        if not last:
            join(half, theirs_ref[...], total_ref[...], total_out)


def turn(me, bit, total, theirs, before, last, after):
    packed = total.shape[0]
    operands = [total, theirs] + ([] if before is None else [before])
    count = 1 if last else 2
    out = call(
        functools.partial(turn_kernel, (packed - 8) // HD, bit, before is None, last),
        [SMEM] + [VMEM] * len(operands),
        [VMEM] * count,
        [jax.ShapeDtypeStruct((packed, HD), F32)] * count,
        after=after,
    )(me, *operands)
    return out[0], (None if last else out[1])


def inside_kernel(q_ref, k_ref, v_ref, sums_ref, out_ref, terms_ref):
    tokens = q_ref.shape[0]
    heads = sums_ref.shape[0]
    causal = lax.broadcasted_iota(jnp.int32, (tokens, tokens), 0) >= lax.broadcasted_iota(
        jnp.int32, (tokens, tokens), 1
    )
    columns = sums_ref[...].T
    for h in range(heads):
        at = slice(h * HD, (h + 1) * HD)
        q_high, q_low = split(q_ref[:, at])
        k_high, k_low = split(k_ref[:, at])
        terms_ref[h, :, :HD] = q_high
        terms_ref[h, :, HD:] = q_low
        scores = lax.dot_general(
            jnp.concatenate([q_high, q_low, q_high], axis=1),
            jnp.concatenate([k_high, k_high, k_low], axis=1),
            NT,
            preferred_element_type=F32,
        )
        gaps = columns[:, h : h + 1] - sums_ref[h : h + 1, :]
        weights = jnp.where(causal, jnp.exp(jnp.where(causal, gaps, 0.0)), 0.0)
        out_ref[h] = three_term(scores * weights, v_ref[:, at])


def inside_blocks(q_lin, k_lin, v_lin, sums, after):
    tokens = q_lin.shape[0]
    heads = sums.shape[0]
    return call(
        inside_kernel,
        [VMEM] * 4,
        [VMEM] * 2,
        [
            jax.ShapeDtypeStruct((heads, tokens, HD), F32),
            jax.ShapeDtypeStruct((heads, tokens, 2 * HD), BF16),
        ],
        after=after,
    )(q_lin, k_lin, v_lin, sums)


def linear_kernel(me_ref, terms_ref, inside_ref, sums_ref, mine_ref, theirs_ref, other_ref, out_ref, energy_ref):
    heads, tokens, _ = out_ref.shape
    half = heads // 2
    core = me_ref[0] & 1
    leading = jnp.exp(sums_ref[...]).T
    squares = jnp.zeros((tokens, HD), F32)
    for side in range(2):
        decay = jnp.exp(other_ref[side, half * HD :])
        for i in range(half):
            h = side * half + i
            at = slice(i * HD, (i + 1) * HD)
            prior = jnp.where(core == side, mine_ref[at], theirs_ref[at])
            prior = jnp.where(core == 1, prior * decay[i : i + 1] + other_ref[side, at], prior)
            high, low = split(prior)
            wide = dot(terms_ref[h, :, :HD], jnp.concatenate([high, low], axis=1))
            carried = wide[:, :HD] + wide[:, HD:] + dot(terms_ref[h, :, HD:], high)
            linear = inside_ref[h] + leading[:, h : h + 1] * carried
            out_ref[h] = linear
            squares = squares + linear * linear
    energy_ref[...] = lax.dot_general(
        jnp.ones((8, HD), F32),
        squares,
        NT,
        precision=lax.Precision.HIGHEST,
        preferred_element_type=F32,
    )


def linear_blocks(me, terms, inside, sums, mine, theirs, other, after):
    _, tokens, _ = inside.shape
    return call(
        linear_kernel,
        [SMEM] + [VMEM] * 6,
        [VMEM] * 2,
        [
            jax.ShapeDtypeStruct(inside.shape, F32),
            jax.ShapeDtypeStruct((8, tokens), F32),
        ],
        after=after,
    )(me, terms, inside, sums, mine, theirs, other)


def halves(core, *arrays):
    early = [array[:, :HD] for array in arrays]
    late = [array[:, HD:] for array in arrays]
    mine = jnp.stack([jnp.where(core == 0, a, b) for a, b in zip(early, late)])
    theirs = jnp.stack([jnp.where(core == 0, b, a) for a, b in zip(early, late)])
    return mine, theirs


def pair_kernel(me_ref, mine_ref, other_ref, q_ref, out_ref, send_ref):
    tokens = mine_ref.shape[1]
    group = send_ref.shape[0]
    core = me_ref[0] & 1
    first = core == 0
    for side in range(2):
        mine, other = mine_ref[side], other_ref[side]
        out_ref[side, :tokens] = jnp.where(first, mine, other)
        out_ref[side, tokens:] = jnp.where(first, other, mine)
    for g in range(group):
        at = pl.ds(pl.multiple_of(((1 - core) * group + g) * HD, HD), HD)
        send_ref[g] = q_ref[:, at]


def pair_block(me, mine, other, q_soft, after):
    _, tokens, _ = mine.shape
    group = q_soft.shape[1] // (2 * HD)
    return call(
        pair_kernel,
        [SMEM] + [VMEM] * 3,
        [VMEM] * 2,
        [
            jax.ShapeDtypeStruct((2, 2 * tokens, HD), F32),
            jax.ShapeDtypeStruct((group, tokens, HD), F32),
        ],
        after=after,
    )(me, mine, other, q_soft)


def run_heads(count, load, soften, gather):
    load(0, 0)
    load(1, 1)
    soften(0, 0)

    def turn(j, carry):
        for i, slot in ((2 * j + 1, 1), (2 * j + 2, 0)):
            load(i + 1, 1 - slot)
            gather(i - 1, 1 - slot)
            soften(i, slot)
        return carry

    lax.fori_loop(0, count // 2 - 1, turn, 0)
    gather(count - 2, 0)
    soften(count - 1, 1)
    gather(count - 1, 1)


def fill_terms(kv_ref, keys_ref, values_ref):
    k_high, k_low = split(kv_ref[0].T)
    keys_ref[:HD] = k_high
    keys_ref[HD : 2 * HD] = k_high
    keys_ref[2 * HD :] = k_low
    v_high, v_low = split(kv_ref[1])
    values_ref[:, :HD] = v_high
    values_ref[:, HD:] = v_low


def lane_max(array):
    peak = array[:, :HD]
    for c in range(1, array.shape[1] // HD):
        peak = jnp.maximum(peak, array[:, c * HD : (c + 1) * HD])
    return peak


def score_terms(pair):
    return jnp.concatenate([pair, pair[:, :HD]], axis=1)


def weigh(scores_ref, rows, count, peak, total, high_ref, low_ref):
    for c in range(count // HD):
        at = slice(c * HD, (c + 1) * HD)
        w = jnp.exp2(scores_ref[rows, at] - peak)
        total = total + w
        high_ref[rows, at], low_ref[rows, at] = split(w)
    return total


def summed(high, low, values):
    wide = dot(high, values)
    return wide[:, :HD] + wide[:, HD:] + dot(low, values[:, :HD])


def own_kernel(factor, me_ref, q_ref, q_other_ref, kv_ref, q_out, acc_out, peak_out, total_out, *scratch):
    keys_ref, values_ref = scratch[:2]
    scores, highs, lows, peaks = scratch[2:4], scratch[4:6], scratch[6:8], scratch[8:10]
    group, tokens = q_out.shape[0], q_ref.shape[0]
    core = me_ref[0] & 1
    first = core == 0
    fill_terms(kv_ref, keys_ref, values_ref)
    for g in range(group):
        at = pl.ds(pl.multiple_of((core * group + g) * HD, HD), HD)
        mine, other = q_ref[:, at], q_other_ref[g]
        for t, rows in enumerate(
            (jnp.where(first, mine, other), jnp.where(first, other, mine))
        ):
            high, low = split(rows * factor)
            at = slice(t * tokens, (t + 1) * tokens)
            q_out[g, at, :HD] = high
            q_out[g, at, HD:] = low

    seen = lax.broadcasted_iota(jnp.int32, (tokens, tokens), 1)
    seen = seen <= lax.broadcasted_iota(jnp.int32, (tokens, tokens), 0)
    early, late = slice(0, tokens), slice(tokens, 2 * tokens)

    def load(g, slot):
        terms = score_terms(q_out[g])
        left = dot(terms, keys_ref[:, early])
        right = dot(terms[late], keys_ref[:, late])
        edge = jnp.where(seen, left[early], NEGATIVE)
        far = jnp.where(seen, right, NEGATIVE)
        scores[slot][early, early] = edge
        scores[slot][late, early] = left[late]
        scores[slot][late, late] = far
        peaks[slot][early] = lane_max(edge)
        peaks[slot][late] = jnp.maximum(lane_max(left[late]), lane_max(far))

    def soften(g, slot):
        peak = jnp.max(peaks[slot][...], axis=1, keepdims=True)
        peak = jnp.broadcast_to(peak, (2 * tokens, HD))
        peak_out[g] = peak
        zero = jnp.zeros((tokens, HD), F32)
        total_out[g, early] = weigh(
            scores[slot], early, tokens, peak[early], zero, highs[slot], lows[slot]
        )
        total_out[g, late] = weigh(
            scores[slot], late, 2 * tokens, peak[late], zero, highs[slot], lows[slot]
        )

    def gather(g, slot):
        acc_out[g, early] = summed(
            highs[slot][early, early], lows[slot][early, early], values_ref[early]
        )
        acc_out[g, late] = summed(highs[slot][late], lows[slot][late], values_ref[...])

    run_heads(group, load, soften, gather)


def stage_scratch(rows, keys):
    return [
        *[pltpu.VMEM((rows, keys), F32)] * 2,
        *[pltpu.VMEM((rows, keys), BF16)] * 4,
        *[pltpu.VMEM((rows, HD), F32)] * 4,
    ]


def own_stage(me, q_soft, q_other, kv, after):
    tokens, width = q_soft.shape
    group = width // (2 * HD)
    stat = jax.ShapeDtypeStruct((group, 2 * tokens, HD), F32)
    return call(
        functools.partial(own_kernel, math.log2(math.e) / math.sqrt(HD)),
        [SMEM] + [VMEM] * 3,
        [VMEM] * 4,
        [jax.ShapeDtypeStruct((group, 2 * tokens, 2 * HD), BF16), stat, stat, stat],
        [
            pltpu.VMEM((3 * HD, 2 * tokens), BF16),
            pltpu.VMEM((2 * tokens, 2 * HD), BF16),
            *stage_scratch(2 * tokens, 2 * tokens),
        ],
        after=after,
    )(me, q_soft, q_other, kv)


def later_kernel(distance, form, me_ref, kv_ref, q_ref, acc_ref, peak_ref, total_ref, acc_out, peak_out, total_out, *scratch):
    keys_ref, values_ref = scratch[:2]
    scores, highs, lows, peaks = scratch[2:4], scratch[4:6], scratch[6:8], scratch[8:10]
    shrinks = scratch[10:12]
    group, rows, _ = q_ref.shape
    everything = slice(0, rows)
    chip = me_ref[0] >> 1

    def load(g, slot):
        s = dot(score_terms(q_ref[g]), keys_ref[...])
        scores[slot][...] = s
        peaks[slot][...] = lane_max(s)

    def soften(g, slot):
        old = peak_ref[g]
        peak = jnp.maximum(jnp.max(peaks[slot][...], axis=1, keepdims=True), old)
        shrink = jnp.exp2(old - peak)
        peak_out[g] = peak
        total_out[g] = weigh(
            scores[slot], everything, keys_ref.shape[1], peak, total_ref[g] * shrink,
            highs[slot], lows[slot],
        )
        shrinks[slot][...] = shrink

    def gather(g, slot):
        acc_out[g] = acc_ref[g] * shrinks[slot][...] + summed(
            highs[slot][...], lows[slot][...], values_ref[...]
        )

    tokens = rows // 2

    def score(i):
        at = slice(i % 2 * tokens, (i % 2 + 1) * tokens)
        return dot(score_terms(q_ref[i // 2, at]), keys_ref[...])

    def soft(i, s):
        at = slice(i % 2 * tokens, (i % 2 + 1) * tokens)
        old = peak_ref[i // 2, at]
        peak = jnp.maximum(jnp.max(lane_max(s), axis=1, keepdims=True), old)
        shrink = jnp.exp2(old - peak)
        total = total_ref[i // 2, at] * shrink
        high, low = [], []
        for c in range(s.shape[1] // HD):
            w = jnp.exp2(s[:, c * HD : (c + 1) * HD] - peak)
            total = total + w
            pair = split(w)
            high.append(pair[0])
            low.append(pair[1])
        peak_out[i // 2, at] = peak
        total_out[i // 2, at] = total
        return jnp.concatenate(high, axis=1), jnp.concatenate(low, axis=1), shrink

    def weighted(i, terms):
        at = slice(i % 2 * tokens, (i % 2 + 1) * tokens)
        high, low, shrink = terms
        acc_out[i // 2, at] = acc_ref[i // 2, at] * shrink + summed(high, low, values_ref[...])

    def chunked(i, slot, before, after):
        for c in range(2):
            at = slice(c * tokens, (c + 1) * tokens)
            if after:
                s = dot(score_terms(q_ref[i + 1, at]), keys_ref[...])
                scores[1 - slot][at] = s
                peaks[1 - slot][at] = lane_max(s)
            if before:
                acc_out[i - 1, at] = acc_ref[i - 1, at] * shrinks[1 - slot][at] + summed(
                    highs[1 - slot][at], lows[1 - slot][at], values_ref[...]
                )
            old = peak_ref[i, at]
            peak = jnp.maximum(jnp.max(peaks[slot][at], axis=1, keepdims=True), old)
            shrink = jnp.exp2(old - peak)
            peak_out[i, at] = peak
            total_out[i, at] = weigh(
                scores[slot], at, keys_ref.shape[1], peak, total_ref[i, at] * shrink,
                highs[slot], lows[slot],
            )
            shrinks[slot][at] = shrink

    @pl.when(lax.bitwise_xor(chip, distance) < chip)
    def _():
        fill_terms(kv_ref, keys_ref, values_ref)
        if form == "scratch":
            run_heads(group, load, soften, gather)
        elif form == "values":
            count = 2 * group
            s, before = score(0), None
            for i in range(count):
                following = score(i + 1) if i + 1 < count else None
                if before is not None:
                    weighted(i - 1, before)
                before = soft(i, s)
                s = following
            weighted(count - 1, before)
        else:
            load(0, 0)
            for i in range(group):
                chunked(i, i % 2, i > 0, i + 1 < group)
            gather(group - 1, (group - 1) % 2)


def later_stage(me, distance, kv, q_terms, acc, peak, total, after, form="scratch"):
    group, rows, _ = q_terms.shape
    keys = kv.shape[1]
    return call(
        functools.partial(later_kernel, distance, form),
        [SMEM] + [VMEM] * 5,
        [VMEM] * 3,
        [jax.ShapeDtypeStruct(acc.shape, F32)] * 3,
        [
            pltpu.VMEM((3 * HD, keys), BF16),
            pltpu.VMEM((keys, 2 * HD), BF16),
            *stage_scratch(rows, keys),
        ],
        alias={3: 0, 4: 1, 5: 2},
        after=after,
    )(me, kv, q_terms, acc, peak, total)


def last_kernel(distance, columns, me_ref, kv_ref, q_ref, acc_ref, peak_ref, total_ref, *refs):
    if columns is None:
        out_ref, *scratch = refs
    else:
        theirs_ref, energy_ref, energy_other_ref, gain_ref, linear_ref = refs[:5]
        lin_hbm, soft_hbm, lin_ref, out_ref, sems, *scratch = refs[5:]
    keys_ref, values_ref = scratch[:2]
    scores, highs, lows, peaks = scratch[2:4], scratch[4:6], scratch[6:8], scratch[8:10]
    shrinks, totals = scratch[10:12], scratch[12:14]
    group, rows, _ = q_ref.shape
    tokens = rows // 2
    everything = slice(0, tokens)
    core, chip = me_ref[0] & 1, me_ref[0] >> 1
    side = 1 - core if columns is None else core
    at = pl.ds(pl.multiple_of(side * tokens, tokens), tokens)

    def to_soft(source, whose, g, n):
        to = pl.ds(pl.multiple_of((whose * group + g) * HD, HD), HD)
        return pltpu.make_async_copy(source.at[g], soft_hbm.at[:, to], sems.at[n])

    def to_lin(h):
        return pltpu.make_async_copy(
            lin_ref.at[h], lin_hbm.at[:, pl.ds(h * HD, HD)], sems.at[2 * group + h]
        )

    if columns is not None:
        for g in range(group):
            to_soft(theirs_ref, 1 - core, g, g).start()
        factor = lax.rsqrt((energy_ref[...] + energy_other_ref[...]) / columns + EPSILON)
        factor = factor.T[:, 0:1]
        for h in range(linear_ref.shape[0]):
            lin_ref[h] = linear_ref[h] * factor * gain_ref[:, h * HD : (h + 1) * HD]
            to_lin(h).start()

    def finish(g, acc, total):
        out_ref[g] = acc / jnp.sum(total, axis=1, keepdims=True)
        if columns is not None:
            to_soft(out_ref, core, g, group + g).start()

    def load(g, slot):
        s = dot(score_terms(q_ref[g, at]), keys_ref[...])
        scores[slot][...] = s
        peaks[slot][...] = lane_max(s)

    def soften(g, slot):
        old = peak_ref[g, at]
        peak = jnp.maximum(jnp.max(peaks[slot][...], axis=1, keepdims=True), old)
        shrink = jnp.exp2(old - peak)
        totals[slot][...] = weigh(
            scores[slot], everything, keys_ref.shape[1], peak, total_ref[g, at] * shrink,
            highs[slot], lows[slot],
        )
        shrinks[slot][...] = shrink

    def gather(g, slot):
        acc = acc_ref[g, at] * shrinks[slot][...] + summed(
            highs[slot][...], lows[slot][...], values_ref[...]
        )
        finish(g, acc, totals[slot][...])

    visible = lax.bitwise_xor(chip, distance) < chip

    @pl.when(visible)
    def _():
        fill_terms(kv_ref, keys_ref, values_ref)
        run_heads(group, load, soften, gather)

    @pl.when(jnp.logical_not(visible))
    def _():
        for g in range(group):
            finish(g, acc_ref[g, at], total_ref[g, at])

    if columns is not None:
        for g in range(group):
            to_soft(theirs_ref, 1 - core, g, g).wait()
            to_soft(out_ref, core, g, group + g).wait()
        for h in range(linear_ref.shape[0]):
            to_lin(h).wait()


def last_stage(me, distance, kv, q_terms, acc, peak, total, after, extra=None):
    group, rows, _ = q_terms.shape
    keys, tokens = kv.shape[1], rows // 2
    part = jax.ShapeDtypeStruct((group, tokens, HD), F32)
    scratch = [
        pltpu.VMEM((3 * HD, keys), BF16),
        pltpu.VMEM((keys, 2 * HD), BF16),
        *stage_scratch(tokens, keys),
        *[pltpu.VMEM((tokens, HD), F32)] * 2,
    ]
    operands, columns = [kv, q_terms, acc, peak, total], None
    out_shape, out_spec = part, VMEM
    if extra is not None:
        columns, more = extra
        operands += more
        heads = more[-1].shape[0]
        out_shape = [
            jax.ShapeDtypeStruct((tokens, heads * HD), F32),
            jax.ShapeDtypeStruct((tokens, 2 * group * HD), F32),
        ]
        out_spec = [HBM] * 2
        scratch = [
            pltpu.VMEM((heads, tokens, HD), F32),
            pltpu.VMEM(part.shape, F32),
            pltpu.SemaphoreType.DMA((2 * group + heads,)),
        ] + scratch
    return call(
        functools.partial(last_kernel, distance, columns),
        [SMEM] + [VMEM] * len(operands),
        out_spec,
        out_shape,
        scratch,
        after=after,
    )(me, *operands)


def plus_kernel(a_ref, b_ref, out_ref):
    out_ref[...] = a_ref[...] + b_ref[...]


def plus(a, b, after):
    return call(
        plus_kernel, [VMEM] * 2, VMEM, jax.ShapeDtypeStruct(a.shape, F32), after=after
    )(a, b)


def relay_kernel(me_ref, beside_ref, across_ref, out_ref):
    @pl.when((me_ref[0] & 1) == 0)
    def _():
        out_ref[...] = beside_ref[...]

    @pl.when((me_ref[0] & 1) == 1)
    def _():
        out_ref[...] = across_ref[...]


def relayed(me, beside, across, after):
    return call(
        relay_kernel,
        [SMEM, VMEM, VMEM],
        VMEM,
        jax.ShapeDtypeStruct(beside.shape, F32),
        after=after,
    )(me, beside, across)


def body(q_lin, k_lin, v_lin, log_decay, lin_gain, q_soft, k_soft, v_soft):
    chips = lax.axis_size("ctx") // 2
    heads = lax.axis_size("head")
    me = lax.axis_index("ctx")
    me_flag = me.reshape(1).astype(jnp.int32)
    assert k_soft.shape[1] == 2 * HD
    swap_pairs = [(2 * c + e, 2 * c + 1 - e) for c in range(chips) for e in range(2)]

    def swap(array):
        return lax.ppermute(array, "ctx", swap_pairs)

    def across(array, distance, wanted=lambda c, e: True):
        pairs = [
            (2 * (c ^ distance) + e, 2 * c + e)
            for c in range(chips)
            for e in range(2)
            if wanted(c, e)
        ]
        return lax.ppermute(array, "ctx", pairs)

    square = chips == 4
    kv_mine, kv_send = halves(me & 1, k_soft, v_soft)
    kv_other = swap(kv_send)
    states, sums = local_states(log_decay, k_lin, v_lin, [kv_mine])
    others = swap(states)
    kv, q_send = pair_block(me_flag, kv_mine, kv_other, q_soft, [sums])
    arrived = {}
    for distance in range(1, chips - 1 if square else chips):
        arrived[distance] = across(
            kv,
            distance,
            lambda c, e, d=distance: c ^ d < c or (square and d == 1 and c == 0 and e == 0),
        )
    q_other = swap(q_send)

    total, prefix = chip_total(me_flag, states, others, [q_send]), None
    inside, terms = inside_blocks(q_lin, k_lin, v_lin, sums, [total])
    q_terms, *carried = own_stage(me_flag, q_soft, q_other, kv, [inside])

    def exchanged(array, step):
        return lax.ppermute(array, "head", [(i, i ^ step) for i in range(heads)])

    def stage(distance, carried, after, form):
        return later_stage(
            me_flag, distance, arrived[distance], q_terms, *carried, after, form
        )

    bits = chips.bit_length() - 1
    token = carried[0]
    if square:
        carried = stage(2, carried, [], "values")
        token = carried[0]
    for bit in range(bits):
        last = bit == bits - 1
        theirs = across(total, 1 << bit, lambda c, e: not last or c ^ (1 << bit) < c)
        prefix, total = turn(me_flag, bit, total, theirs, prefix, last, [token])
        if square and bit == 0:
            relay = relayed(me_flag, arrived[1], arrived[2], [prefix])
            arrived[3] = lax.ppermute(relay, "ctx", [(2, 6), (0, 4), (5, 7), (7, 5)])
            carried = stage(1, carried, [relay], "chunks")
            token = carried[0]
        elif not square:
            carried = stage(bit + 1, carried, [prefix], "scratch")
            token = carried[0]
    prefix_other = swap(prefix)
    if not square:
        for distance in range(bits + 1, chips - 1):
            carried = stage(distance, carried, [], "scratch")

    linear, energy = linear_blocks(
        me_flag, terms, inside, sums, prefix, prefix_other, others, [carried[0]]
    )
    operands = (arrived[chips - 1], q_terms, *carried)
    theirs = last_stage(me_flag, chips - 1, *operands, [energy])
    step, other = 1, exchanged(energy, 1)
    while 2 * step < heads:
        step *= 2
        energy = plus(energy, other, [theirs])
        other = exchanged(energy, step)
    columns = q_lin.shape[1] * heads
    more = [swap(theirs), energy, other, lin_gain.reshape(1, -1), linear]
    return tuple(last_stage(me_flag, chips - 1, *operands, [], (columns, more)))


def solution(mesh):
    return jax.shard_map(
        body,
        mesh=mesh,
        in_specs=(
            P("ctx", "head"),
            P("ctx", "head"),
            P("ctx", "head"),
            P("head", "ctx"),
            P("head"),
            P("ctx", "head"),
            P("ctx", "head"),
            P("ctx", "head"),
        ),
        out_specs=(P("ctx", "head"), P("ctx", "head")),
        check_vma=False,
    )
```

```python
import functools
import math

import jax
import jax.numpy as jnp
from jax import lax
from jax.experimental import pallas as pl
from jax.experimental.pallas import tpu as pltpu
from jax.sharding import PartitionSpec as P

HD = 128
NEGATIVE = -1e30
EPSILON = 1e-05
ENERGY_ROWS = 64
F32 = jnp.float32
BF16 = jnp.bfloat16
NT = (((1,), (1,)), ((), ()))
VMEM_LIMIT = 32 * 1024 * 1024
VMEM = pl.BlockSpec(memory_space=pltpu.VMEM)
SMEM = pl.BlockSpec(memory_space=pltpu.SMEM)
ANY = pl.BlockSpec(memory_space=pl.ANY)
HBM = pl.BlockSpec(memory_space=pltpu.HBM)


def split(x):
    high = x.astype(BF16)
    low = (x - high.astype(F32)).astype(BF16)
    return high, low


def dot(a, b):
    return jnp.dot(a, b, preferred_element_type=F32)


def three_term(a, b):
    a_high, a_low = split(a)
    b_high, b_low = split(b)
    wide = dot(a_high, jnp.concatenate([b_high, b_low], axis=1))
    n = b.shape[1]
    return wide[:, :n] + wide[:, n:] + dot(a_low, b_high)


def call(kernel, in_specs, out_specs, out_shape, scratch=(), alias=None, after=()):
    count = len(in_specs)

    def ordered(*refs):
        kernel(*refs[:count], *refs[count + len(after) :])

    made = pl.pallas_call(
        ordered,
        in_specs=in_specs + [ANY] * len(after),
        out_specs=out_specs,
        out_shape=out_shape,
        scratch_shapes=list(scratch),
        input_output_aliases=alias or {},
        cost_estimate=pl.CostEstimate(flops=1, bytes_accessed=1, transcendentals=0),
        compiler_params=pltpu.CompilerParams(vmem_limit_bytes=VMEM_LIMIT),
    )
    return lambda *operands: made(*operands, *after)


def state_kernel(rate_ref, k_ref, v_ref, packed_ref, sums_ref):
    tokens = k_ref.shape[0]
    heads = rate_ref.shape[0]
    half = heads // 2
    upto = lax.broadcasted_iota(jnp.int32, (tokens, tokens), 0)
    upto = (upto <= lax.broadcasted_iota(jnp.int32, (tokens, tokens), 1)).astype(F32)
    sums = jnp.dot(
        rate_ref[...], upto, precision=lax.Precision.HIGHEST, preferred_element_type=F32
    )
    sums_ref[...] = sums
    totals = sums[:, tokens - 1 : tokens]
    trailing = jnp.exp(totals - sums)
    for side in range(2):
        packed_ref[side, half * HD :] = jnp.zeros((8, HD), F32)
    for h in range(heads):
        side, i = h // half, h % half
        at = slice(h * HD, (h + 1) * HD)
        packed_ref[side, i * HD : (i + 1) * HD] = three_term(
            k_ref[:, at].T * trailing[h : h + 1], v_ref[:, at]
        )
        packed_ref[side, half * HD + i : half * HD + i + 1] = jnp.broadcast_to(
            totals[h : h + 1], (1, HD)
        )


def local_states(rates, k_lin, v_lin, after):
    tokens = k_lin.shape[0]
    heads = rates.shape[0]
    return call(
        state_kernel,
        [VMEM] * 3,
        [VMEM] * 2,
        [
            jax.ShapeDtypeStruct((2, heads // 2 * HD + 8, HD), F32),
            jax.ShapeDtypeStruct((heads, tokens), F32),
        ],
        after=after,
    )(rates, k_lin, v_lin)


def join(half, first, second, out_ref):
    decay = jnp.exp(second[half * HD :, :])
    for i in range(half):
        at = slice(i * HD, (i + 1) * HD)
        out_ref[at] = first[at] * decay[i : i + 1] + second[at]
    out_ref[half * HD :] = first[half * HD :] + second[half * HD :]


def chip_kernel(half, me_ref, states_ref, others_ref, out_ref):
    core = me_ref[0] & 1

    @pl.when(core == 0)
    def _():
        join(half, states_ref[0], others_ref[0], out_ref)

    @pl.when(core == 1)
    def _():
        join(half, others_ref[1], states_ref[1], out_ref)


def chip_total(me, states, others, after):
    _, packed, _ = states.shape
    return call(
        functools.partial(chip_kernel, (packed - 8) // HD),
        [SMEM, VMEM, VMEM],
        VMEM,
        jax.ShapeDtypeStruct((packed, HD), F32),
        after=after,
    )(me, states, others)


def turn_kernel(half, bit, first, last, me_ref, total_ref, theirs_ref, *refs):
    refs = list(refs)
    before_ref = None if first else refs.pop(0)
    prefix_ref = refs.pop(0)
    total_out = None if last else refs.pop(0)
    late = (me_ref[0] >> (bit + 1)) & 1

    @pl.when(late == 0)
    def _():
        prefix_ref[...] = jnp.zeros_like(prefix_ref) if first else before_ref[...]
        if not last:
            join(half, total_ref[...], theirs_ref[...], total_out)

    @pl.when(late == 1)
    def _():
        if first:
            prefix_ref[...] = theirs_ref[...]
        else:
            join(half, theirs_ref[...], before_ref[...], prefix_ref)
        if not last:
            join(half, theirs_ref[...], total_ref[...], total_out)


def turn(me, bit, total, theirs, before, last, after):
    packed = total.shape[0]
    operands = [total, theirs] + ([] if before is None else [before])
    count = 1 if last else 2
    out = call(
        functools.partial(turn_kernel, (packed - 8) // HD, bit, before is None, last),
        [SMEM] + [VMEM] * len(operands),
        [VMEM] * count,
        [jax.ShapeDtypeStruct((packed, HD), F32)] * count,
        after=after,
    )(me, *operands)
    return out[0], (None if last else out[1])


def inside_kernel(q_ref, k_ref, v_ref, sums_ref, out_ref, terms_ref):
    tokens = q_ref.shape[0]
    heads = sums_ref.shape[0]
    causal = lax.broadcasted_iota(jnp.int32, (tokens, tokens), 0) >= lax.broadcasted_iota(
        jnp.int32, (tokens, tokens), 1
    )
    columns = sums_ref[...].T
    for h in range(heads):
        at = slice(h * HD, (h + 1) * HD)
        q_high, q_low = split(q_ref[:, at])
        k_high, k_low = split(k_ref[:, at])
        terms_ref[h, :, :HD] = q_high
        terms_ref[h, :, HD:] = q_low
        scores = lax.dot_general(
            jnp.concatenate([q_high, q_low, q_high], axis=1),
            jnp.concatenate([k_high, k_high, k_low], axis=1),
            NT,
            preferred_element_type=F32,
        )
        gaps = columns[:, h : h + 1] - sums_ref[h : h + 1, :]
        weights = jnp.where(causal, jnp.exp(jnp.where(causal, gaps, 0.0)), 0.0)
        out_ref[h] = three_term(scores * weights, v_ref[:, at])


def inside_blocks(q_lin, k_lin, v_lin, sums, after):
    tokens = q_lin.shape[0]
    heads = sums.shape[0]
    return call(
        inside_kernel,
        [VMEM] * 4,
        [VMEM] * 2,
        [
            jax.ShapeDtypeStruct((heads, tokens, HD), F32),
            jax.ShapeDtypeStruct((heads, tokens, 2 * HD), BF16),
        ],
        after=after,
    )(q_lin, k_lin, v_lin, sums)


def linear_kernel(me_ref, terms_ref, inside_ref, sums_ref, mine_ref, theirs_ref, other_ref, out_ref, energy_ref):
    heads, tokens, _ = out_ref.shape
    half = heads // 2
    core = me_ref[0] & 1
    leading = jnp.exp(sums_ref[...]).T
    squares = jnp.zeros((tokens, HD), F32)
    for side in range(2):
        decay = jnp.exp(other_ref[side, half * HD :])
        for i in range(half):
            h = side * half + i
            at = slice(i * HD, (i + 1) * HD)
            prior = jnp.where(core == side, mine_ref[at], theirs_ref[at])
            prior = jnp.where(core == 1, prior * decay[i : i + 1] + other_ref[side, at], prior)
            high, low = split(prior)
            wide = dot(terms_ref[h, :, :HD], jnp.concatenate([high, low], axis=1))
            carried = wide[:, :HD] + wide[:, HD:] + dot(terms_ref[h, :, HD:], high)
            linear = inside_ref[h] + leading[:, h : h + 1] * carried
            out_ref[h] = linear
            squares = squares + linear * linear
    energy_ref[...] = lax.dot_general(
        jnp.ones((energy_ref.shape[0], HD), F32),
        squares,
        NT,
        precision=lax.Precision.HIGHEST,
        preferred_element_type=F32,
    )


def linear_blocks(me, terms, inside, sums, mine, theirs, other, after):
    _, tokens, _ = inside.shape
    return call(
        linear_kernel,
        [SMEM] + [VMEM] * 6,
        [VMEM] * 2,
        [
            jax.ShapeDtypeStruct(inside.shape, F32),
            jax.ShapeDtypeStruct((ENERGY_ROWS, tokens), F32),
        ],
        after=after,
    )(me, terms, inside, sums, mine, theirs, other)


def halves(core, *arrays):
    early = [array[:, :HD] for array in arrays]
    late = [array[:, HD:] for array in arrays]
    mine = jnp.stack([jnp.where(core == 0, a, b) for a, b in zip(early, late)])
    theirs = jnp.stack([jnp.where(core == 0, b, a) for a, b in zip(early, late)])
    return mine, theirs


def pair_kernel(me_ref, mine_ref, other_ref, q_ref, out_ref, send_ref):
    tokens = mine_ref.shape[1]
    group = send_ref.shape[0]
    core = me_ref[0] & 1
    first = core == 0
    for side in range(2):
        mine, other = mine_ref[side], other_ref[side]
        out_ref[side, :tokens] = jnp.where(first, mine, other)
        out_ref[side, tokens:] = jnp.where(first, other, mine)
    for g in range(group):
        at = pl.ds(pl.multiple_of(((1 - core) * group + g) * HD, HD), HD)
        send_ref[g] = q_ref[:, at]


def pair_block(me, mine, other, q_soft, after):
    _, tokens, _ = mine.shape
    group = q_soft.shape[1] // (2 * HD)
    return call(
        pair_kernel,
        [SMEM] + [VMEM] * 3,
        [VMEM] * 2,
        [
            jax.ShapeDtypeStruct((2, 2 * tokens, HD), F32),
            jax.ShapeDtypeStruct((group, tokens, HD), F32),
        ],
        after=after,
    )(me, mine, other, q_soft)


def run(count, score, soften, gather):
    scores, before = score(0), None
    for i in range(count):
        following = score(i + 1) if i + 1 < count else None
        if before is not None:
            gather(i - 1, before)
        before = soften(i, scores)
        scores = following
    gather(count - 1, before)


def fill_terms(kv_ref, keys_ref, values_ref):
    k_high, k_low = split(kv_ref[0].T)
    keys_ref[:HD] = k_high
    keys_ref[HD : 2 * HD] = k_high
    keys_ref[2 * HD :] = k_low
    v_high, v_low = split(kv_ref[1])
    values_ref[:, :HD] = v_high
    values_ref[:, HD:] = v_low


def lane_max(array):
    peak = array[:, :HD]
    for c in range(1, array.shape[1] // HD):
        peak = jnp.maximum(peak, array[:, c * HD : (c + 1) * HD])
    return peak


def score_terms(pair):
    return jnp.concatenate([pair, pair[:, :HD]], axis=1)


def weigh(scores, peak, total):
    high, low = [], []
    for c in range(scores.shape[1] // HD):
        w = jnp.exp2(scores[:, c * HD : (c + 1) * HD] - peak)
        total = total + w
        pair = split(w)
        high.append(pair[0])
        low.append(pair[1])
    return jnp.concatenate(high, axis=1), jnp.concatenate(low, axis=1), total


def summed(high, low, values):
    wide = dot(high, values)
    return wide[:, :HD] + wide[:, HD:] + dot(low, values[:, :HD])


def own_kernel(factor, me_ref, q_ref, q_other_ref, kv_ref, q_out, acc_out, peak_out, total_out, keys_ref, values_ref):
    group, tokens = q_out.shape[0], q_ref.shape[0]
    core = me_ref[0] & 1
    first = core == 0
    fill_terms(kv_ref, keys_ref, values_ref)
    seen = lax.broadcasted_iota(jnp.int32, (tokens, tokens), 1)
    seen = seen <= lax.broadcasted_iota(jnp.int32, (tokens, tokens), 0)

    def where(i):
        t = i % 2
        return i // 2, slice(t * tokens, (t + 1) * tokens), slice(0, (t + 1) * tokens)

    def score(i):
        g, rows, keys = where(i)
        at = pl.ds(pl.multiple_of((core * group + g) * HD, HD), HD)
        mine, other = q_ref[:, at], q_other_ref[g]
        queries = jnp.where(first, mine, other) if i % 2 == 0 else jnp.where(first, other, mine)
        pair = jnp.concatenate(split(queries * factor), axis=1)
        q_out[g, rows] = pair
        s = dot(score_terms(pair), keys_ref[:, keys])
        edge = jnp.where(seen, s[:, rows], NEGATIVE)
        return edge if i % 2 == 0 else jnp.concatenate([s[:, :tokens], edge], axis=1)

    def soften(i, s):
        g, rows, _ = where(i)
        peak = jnp.max(lane_max(s), axis=1, keepdims=True)
        peak_out[g, rows] = jnp.broadcast_to(peak, (tokens, HD))
        high, low, total_out[g, rows] = weigh(s, peak, jnp.zeros((tokens, HD), F32))
        return high, low

    def gather(i, terms):
        g, rows, keys = where(i)
        acc_out[g, rows] = summed(*terms, values_ref[keys])

    run(2 * group, score, soften, gather)


def term_scratch(keys):
    return [pltpu.VMEM((3 * HD, keys), BF16), pltpu.VMEM((keys, 2 * HD), BF16)]


def own_stage(me, q_soft, q_other, kv, after):
    tokens, width = q_soft.shape
    group = width // (2 * HD)
    stat = jax.ShapeDtypeStruct((group, 2 * tokens, HD), F32)
    return call(
        functools.partial(own_kernel, math.log2(math.e) / math.sqrt(HD)),
        [SMEM] + [VMEM] * 3,
        [VMEM] * 4,
        [jax.ShapeDtypeStruct((group, 2 * tokens, 2 * HD), BF16), stat, stat, stat],
        term_scratch(2 * tokens),
        after=after,
    )(me, q_soft, q_other, kv)


def later_kernel(distance, parts, me_ref, kv_ref, q_ref, acc_ref, peak_ref, total_ref, acc_out, peak_out, total_out, keys_ref, values_ref):
    group, rows, _ = q_ref.shape
    size = rows // parts
    chip = me_ref[0] >> 1

    def where(i):
        return i // parts, slice(i % parts * size, (i % parts + 1) * size)

    def score(i):
        return dot(score_terms(q_ref[where(i)]), keys_ref[...])

    def soften(i, s):
        at = where(i)
        old = peak_ref[at]
        peak = jnp.maximum(jnp.max(lane_max(s), axis=1, keepdims=True), old)
        shrink = jnp.exp2(old - peak)
        peak_out[at] = peak
        high, low, total_out[at] = weigh(s, peak, total_ref[at] * shrink)
        return high, low, shrink

    def gather(i, terms):
        at = where(i)
        acc_out[at] = acc_ref[at] * terms[2] + summed(*terms[:2], values_ref[...])

    @pl.when(lax.bitwise_xor(chip, distance) < chip)
    def _():
        fill_terms(kv_ref, keys_ref, values_ref)
        run(parts * group, score, soften, gather)


def later_stage(me, distance, kv, q_terms, acc, peak, total, after, parts):
    return call(
        functools.partial(later_kernel, distance, parts),
        [SMEM] + [VMEM] * 5,
        [VMEM] * 3,
        [jax.ShapeDtypeStruct(acc.shape, F32)] * 3,
        term_scratch(kv.shape[1]),
        alias={3: 0, 4: 1, 5: 2},
        after=after,
    )(me, kv, q_terms, acc, peak, total)


def last_kernel(distance, whose, heads, columns, me_ref, kv_ref, q_ref, acc_ref, peak_ref, total_ref, *refs):
    if columns is None:
        out_ref, keys_ref, values_ref = refs
    else:
        theirs_ref, done_ref, energy_ref, energy_other_ref, gain_ref, linear_ref = refs[:6]
        lin_hbm, soft_hbm, lin_ref, out_ref, sems, keys_ref, values_ref = refs[6:]
    group, rows, _ = q_ref.shape
    tokens = rows // 2
    core, chip = me_ref[0] & 1, me_ref[0] >> 1
    side = core if whose == "own" else 1 - core
    at = pl.ds(pl.multiple_of(side * tokens, tokens), tokens)
    copies = []

    def copy_soft(source, whose, g):
        to = pl.ds(pl.multiple_of((whose * group + g) * HD, HD), HD)
        copies.append(pltpu.make_async_copy(source, soft_hbm.at[:, to], sems.at[len(copies)]))
        return copies[-1]

    if columns is not None:
        for g in range(group):
            copy_soft(theirs_ref.at[g], 1 - core, g).start()
        for g in range(done_ref.shape[0]):
            copy_soft(done_ref.at[g], core, g).start()
        factor = lax.rsqrt((energy_ref[:8] + energy_other_ref[:8]) / columns + EPSILON)
        factor = factor.T[:, 0:1]
        for h in range(linear_ref.shape[0]):
            to = slice(h * HD, (h + 1) * HD)
            lin_ref[h] = linear_ref[h] * factor * gain_ref[:, to]
            copies.append(
                pltpu.make_async_copy(lin_ref.at[h], lin_hbm.at[:, to], sems.at[len(copies)])
            )
            copies[-1].start()
        own_copies = [copy_soft(out_ref.at[n], core, g) for n, g in enumerate(heads)]

    def finish(n, acc, total):
        out_ref[n] = acc / jnp.sum(total, axis=1, keepdims=True)
        if columns is not None:
            own_copies[n].start()

    def score(n):
        return dot(score_terms(q_ref[heads[n], at]), keys_ref[...])

    def soften(n, s):
        old = peak_ref[heads[n], at]
        peak = jnp.maximum(jnp.max(lane_max(s), axis=1, keepdims=True), old)
        shrink = jnp.exp2(old - peak)
        return *weigh(s, peak, total_ref[heads[n], at] * shrink), shrink

    def gather(n, terms):
        high, low, total, shrink = terms
        new = summed(high, low, values_ref[...])
        finish(n, acc_ref[heads[n], at] * shrink + new, total)

    visible = lax.bitwise_xor(chip, distance) < chip

    @pl.when(visible)
    def _():
        fill_terms(kv_ref, keys_ref, values_ref)
        run(len(heads), score, soften, gather)

    @pl.when(jnp.logical_not(visible))
    def _():
        for n, g in enumerate(heads):
            finish(n, acc_ref[g, at], total_ref[g, at])

    for copy in copies:
        copy.wait()


def last_stage(me, distance, whose, heads, operands, after, extra=None):
    group, rows, _ = operands[1].shape
    tokens = rows // 2
    part = jax.ShapeDtypeStruct((len(heads), tokens, HD), F32)
    scratch = term_scratch(operands[0].shape[1])
    out_shape, out_spec, columns = part, VMEM, None
    if extra is not None:
        columns, more = extra
        operands = [*operands, *more]
        count = more[-1].shape[0]
        out_shape = [
            jax.ShapeDtypeStruct((tokens, count * HD), F32),
            jax.ShapeDtypeStruct((tokens, 2 * group * HD), F32),
        ]
        out_spec = [HBM] * 2
        scratch = [
            pltpu.VMEM((count, tokens, HD), F32),
            pltpu.VMEM(part.shape, F32),
            pltpu.SemaphoreType.DMA((2 * group + count,)),
        ] + scratch
    return call(
        functools.partial(last_kernel, distance, whose, heads, columns),
        [SMEM] + [VMEM] * len(operands),
        out_spec,
        out_shape,
        scratch,
        after=after,
    )(me, *operands)


def plus_kernel(a_ref, b_ref, out_ref):
    out_ref[...] = a_ref[...] + b_ref[...]


def plus(a, b, after):
    return call(
        plus_kernel, [VMEM] * 2, VMEM, jax.ShapeDtypeStruct(a.shape, F32), after=after
    )(a, b)


def copy_kernel(source_ref, out_ref):
    out_ref[...] = source_ref[...]


def copied(array, after):
    return call(copy_kernel, [VMEM], VMEM, jax.ShapeDtypeStruct(array.shape, F32), after=after)(
        array
    )


def relay_kernel(me_ref, beside_ref, across_ref, out_ref):
    @pl.when((me_ref[0] & 1) == 0)
    def _():
        out_ref[...] = beside_ref[...]

    @pl.when((me_ref[0] & 1) == 1)
    def _():
        out_ref[...] = across_ref[...]


def relayed(me, beside, across, after):
    return call(
        relay_kernel,
        [SMEM, VMEM, VMEM],
        VMEM,
        jax.ShapeDtypeStruct(beside.shape, F32),
        after=after,
    )(me, beside, across)


def body(q_lin, k_lin, v_lin, log_decay, lin_gain, q_soft, k_soft, v_soft):
    chips = lax.axis_size("ctx") // 2
    heads = lax.axis_size("head")
    me = lax.axis_index("ctx")
    me_flag = me.reshape(1).astype(jnp.int32)
    assert k_soft.shape[1] == 2 * HD
    swap_pairs = [(2 * c + e, 2 * c + 1 - e) for c in range(chips) for e in range(2)]

    def swap(array):
        return lax.ppermute(array, "ctx", swap_pairs)

    def across(array, distance, wanted=lambda c, e: True):
        pairs = [
            (2 * (c ^ distance) + e, 2 * c + e)
            for c in range(chips)
            for e in range(2)
            if wanted(c, e)
        ]
        return lax.ppermute(array, "ctx", pairs)

    square = chips == 4
    kv_mine, kv_send = halves(me & 1, k_soft, v_soft)
    kv_other = swap(kv_send)
    states, sums = local_states(log_decay, k_lin, v_lin, [kv_mine])
    others = swap(states)
    kv, q_send = pair_block(me_flag, kv_mine, kv_other, q_soft, [sums])
    q_other = swap(q_send)
    total, prefix = chip_total(me_flag, states, others, [q_send]), None
    inside, terms = inside_blocks(q_lin, k_lin, v_lin, sums, [total])

    def exchanged(array, step):
        return lax.ppermute(array, "head", [(i, i ^ step) for i in range(heads)])

    def sent(distance, array):
        return across(
            array,
            distance,
            lambda c, e: c ^ distance < c or (square and distance == 1 and c == 0 and e == 0),
        )

    def stage(distance, carried, after, parts=2):
        return later_stage(
            me_flag, distance, arrived[distance], q_terms, *carried, after, parts
        )

    bits = chips.bit_length() - 1
    arrived = {}
    if square:
        arrived[2] = sent(2, kv)
        arrived[1] = sent(1, copied(kv, [inside]))
    else:
        for distance in range(1, chips):
            arrived[distance] = sent(distance, kv)
    q_terms, *carried = own_stage(me_flag, q_soft, q_other, kv, [inside])
    token = carried[0]
    for bit in range(bits):
        last = bit == bits - 1
        theirs = across(total, 1 << bit, lambda c, e: not last or c ^ (1 << bit) < c)
        prefix, total = turn(me_flag, bit, total, theirs, prefix, last, [token])
        distance = 2 if square else bit + 1
        if not (square and last):
            carried = stage(distance, carried, [prefix], 1)
            token = carried[0]
    prefix_other = swap(prefix)
    token = prefix
    if square:
        relay = relayed(me_flag, arrived[1], arrived[2], [prefix])
        arrived[3] = lax.ppermute(relay, "ctx", [(2, 6), (0, 4), (5, 7), (7, 5)])
        token = relay
    linear, energy = linear_blocks(
        me_flag, terms, inside, sums, prefix, prefix_other, others, [token]
    )
    energies, step = [], 1
    while step < heads:
        energies.append(step)
        step *= 2
    other = exchanged(energy, energies[0])
    for distance in [1] if square else range(bits + 1, chips - 1):
        carried = stage(distance, carried, [energy])
    for step in energies[1:]:
        energy = plus(energy, other, [carried[0]])
        other = exchanged(energy, step)

    operands = [arrived[chips - 1], q_terms, *carried]
    group = q_terms.shape[0]
    theirs = last_stage(me_flag, chips - 1, "other", range(group), operands, [energy])
    done = last_stage(me_flag, chips - 1, "own", range(group // 2), operands, [theirs])
    columns = q_lin.shape[1] * heads
    more = [swap(theirs), done, energy, other, lin_gain.reshape(1, -1), linear]
    return tuple(
        last_stage(
            me_flag, chips - 1, "own", range(group // 2, group), operands, [], (columns, more)
        )
    )


def solution(mesh):
    return jax.shard_map(
        body,
        mesh=mesh,
        in_specs=(
            P("ctx", "head"),
            P("ctx", "head"),
            P("ctx", "head"),
            P("head", "ctx"),
            P("head"),
            P("ctx", "head"),
            P("ctx", "head"),
            P("ctx", "head"),
        ),
        out_specs=(P("ctx", "head"), P("ctx", "head")),
        check_vma=False,
    )
```

```python
import functools
import math

import jax
import jax.numpy as jnp
from jax import lax
from jax.experimental import pallas as pl
from jax.experimental.pallas import tpu as pltpu
from jax.sharding import PartitionSpec as P

HD = 128
NEGATIVE = -1e30
EPSILON = 1e-05
ENERGY_ROWS = 16
F32 = jnp.float32
BF16 = jnp.bfloat16
NT = (((1,), (1,)), ((), ()))
VMEM_LIMIT = 32 * 1024 * 1024
VMEM = pl.BlockSpec(memory_space=pltpu.VMEM)
SMEM = pl.BlockSpec(memory_space=pltpu.SMEM)
ANY = pl.BlockSpec(memory_space=pl.ANY)
HBM = pl.BlockSpec(memory_space=pltpu.HBM)


def split(x):
    high = x.astype(BF16)
    low = (x - high.astype(F32)).astype(BF16)
    return high, low


def dot(a, b):
    return jnp.dot(a, b, preferred_element_type=F32)


def three_term(a, b):
    a_high, a_low = split(a)
    b_high, b_low = split(b)
    wide = dot(a_high, jnp.concatenate([b_high, b_low], axis=1))
    n = b.shape[1]
    return wide[:, :n] + wide[:, n:] + dot(a_low, b_high)


def call(kernel, in_specs, out_specs, out_shape, scratch=(), alias=None, after=()):
    count = len(in_specs)

    def ordered(*refs):
        kernel(*refs[:count], *refs[count + len(after) :])

    made = pl.pallas_call(
        ordered,
        in_specs=in_specs + [ANY] * len(after),
        out_specs=out_specs,
        out_shape=out_shape,
        scratch_shapes=list(scratch),
        input_output_aliases=alias or {},
        cost_estimate=pl.CostEstimate(flops=1, bytes_accessed=1, transcendentals=0),
        compiler_params=pltpu.CompilerParams(vmem_limit_bytes=VMEM_LIMIT),
    )
    return lambda *operands: made(*operands, *after)


def state_kernel(rate_ref, k_ref, v_ref, packed_ref, sums_ref):
    tokens = k_ref.shape[0]
    heads = rate_ref.shape[0]
    half = heads // 2
    upto = lax.broadcasted_iota(jnp.int32, (tokens, tokens), 0)
    upto = (upto <= lax.broadcasted_iota(jnp.int32, (tokens, tokens), 1)).astype(F32)
    sums = jnp.dot(
        rate_ref[...], upto, precision=lax.Precision.HIGHEST, preferred_element_type=F32
    )
    sums_ref[...] = sums
    totals = sums[:, tokens - 1 : tokens]
    trailing = jnp.exp(totals - sums)
    for side in range(2):
        packed_ref[side, half * HD :] = jnp.zeros((8, HD), F32)
    for h in range(heads):
        side, i = h // half, h % half
        at = slice(h * HD, (h + 1) * HD)
        packed_ref[side, i * HD : (i + 1) * HD] = three_term(
            k_ref[:, at].T * trailing[h : h + 1], v_ref[:, at]
        )
        packed_ref[side, half * HD + i : half * HD + i + 1] = jnp.broadcast_to(
            totals[h : h + 1], (1, HD)
        )


def local_states(rates, k_lin, v_lin, after):
    tokens = k_lin.shape[0]
    heads = rates.shape[0]
    return call(
        state_kernel,
        [VMEM] * 3,
        [VMEM] * 2,
        [
            jax.ShapeDtypeStruct((2, heads // 2 * HD + 8, HD), F32),
            jax.ShapeDtypeStruct((heads, tokens), F32),
        ],
        after=after,
    )(rates, k_lin, v_lin)


def join(half, first, second, out_ref):
    decay = jnp.exp(second[half * HD :, :])
    for i in range(half):
        at = slice(i * HD, (i + 1) * HD)
        out_ref[at] = first[at] * decay[i : i + 1] + second[at]
    out_ref[half * HD :] = first[half * HD :] + second[half * HD :]


def chip_kernel(half, me_ref, states_ref, others_ref, out_ref):
    core = me_ref[0] & 1

    @pl.when(core == 0)
    def _():
        join(half, states_ref[0], others_ref[0], out_ref)

    @pl.when(core == 1)
    def _():
        join(half, others_ref[1], states_ref[1], out_ref)


def chip_total(me, states, others, after):
    _, packed, _ = states.shape
    return call(
        functools.partial(chip_kernel, (packed - 8) // HD),
        [SMEM, VMEM, VMEM],
        VMEM,
        jax.ShapeDtypeStruct((packed, HD), F32),
        after=after,
    )(me, states, others)


def turn_kernel(half, bit, first, last, me_ref, total_ref, theirs_ref, *refs):
    refs = list(refs)
    before_ref = None if first else refs.pop(0)
    prefix_ref = refs.pop(0)
    total_out = None if last else refs.pop(0)
    late = (me_ref[0] >> (bit + 1)) & 1

    @pl.when(late == 0)
    def _():
        prefix_ref[...] = jnp.zeros_like(prefix_ref) if first else before_ref[...]
        if not last:
            join(half, total_ref[...], theirs_ref[...], total_out)

    @pl.when(late == 1)
    def _():
        if first:
            prefix_ref[...] = theirs_ref[...]
        else:
            join(half, theirs_ref[...], before_ref[...], prefix_ref)
        if not last:
            join(half, theirs_ref[...], total_ref[...], total_out)


def turn(me, bit, total, theirs, before, last, after):
    packed = total.shape[0]
    operands = [total, theirs] + ([] if before is None else [before])
    count = 1 if last else 2
    out = call(
        functools.partial(turn_kernel, (packed - 8) // HD, bit, before is None, last),
        [SMEM] + [VMEM] * len(operands),
        [VMEM] * count,
        [jax.ShapeDtypeStruct((packed, HD), F32)] * count,
        after=after,
    )(me, *operands)
    return out[0], (None if last else out[1])


def inside_kernel(q_ref, k_ref, v_ref, sums_ref, out_ref, terms_ref):
    tokens = q_ref.shape[0]
    heads = sums_ref.shape[0]
    causal = lax.broadcasted_iota(jnp.int32, (tokens, tokens), 0) >= lax.broadcasted_iota(
        jnp.int32, (tokens, tokens), 1
    )
    columns = sums_ref[...].T
    for h in range(heads):
        at = slice(h * HD, (h + 1) * HD)
        q_high, q_low = split(q_ref[:, at])
        k_high, k_low = split(k_ref[:, at])
        terms_ref[h, :, :HD] = q_high
        terms_ref[h, :, HD:] = q_low
        scores = lax.dot_general(
            jnp.concatenate([q_high, q_low, q_high], axis=1),
            jnp.concatenate([k_high, k_high, k_low], axis=1),
            NT,
            preferred_element_type=F32,
        )
        gaps = columns[:, h : h + 1] - sums_ref[h : h + 1, :]
        weights = jnp.where(causal, jnp.exp(jnp.where(causal, gaps, 0.0)), 0.0)
        out_ref[h] = three_term(scores * weights, v_ref[:, at])


def inside_blocks(q_lin, k_lin, v_lin, sums, after):
    tokens = q_lin.shape[0]
    heads = sums.shape[0]
    return call(
        inside_kernel,
        [VMEM] * 4,
        [VMEM] * 2,
        [
            jax.ShapeDtypeStruct((heads, tokens, HD), F32),
            jax.ShapeDtypeStruct((heads, tokens, 2 * HD), BF16),
        ],
        after=after,
    )(q_lin, k_lin, v_lin, sums)


def linear_kernel(me_ref, terms_ref, inside_ref, sums_ref, mine_ref, theirs_ref, other_ref, out_ref, energy_ref):
    heads, tokens, _ = out_ref.shape
    half = heads // 2
    core = me_ref[0] & 1
    leading = jnp.exp(sums_ref[...]).T
    squares = jnp.zeros((tokens, HD), F32)
    for side in range(2):
        decay = jnp.exp(other_ref[side, half * HD :])
        for i in range(half):
            h = side * half + i
            at = slice(i * HD, (i + 1) * HD)
            prior = jnp.where(core == side, mine_ref[at], theirs_ref[at])
            prior = jnp.where(core == 1, prior * decay[i : i + 1] + other_ref[side, at], prior)
            high, low = split(prior)
            wide = dot(terms_ref[h, :, :HD], jnp.concatenate([high, low], axis=1))
            carried = wide[:, :HD] + wide[:, HD:] + dot(terms_ref[h, :, HD:], high)
            linear = inside_ref[h] + leading[:, h : h + 1] * carried
            out_ref[h] = linear
            squares = squares + linear * linear
    energy_ref[...] = lax.dot_general(
        jnp.ones((energy_ref.shape[0], HD), F32),
        squares,
        NT,
        precision=lax.Precision.HIGHEST,
        preferred_element_type=F32,
    )


def linear_blocks(me, terms, inside, sums, mine, theirs, other, after):
    _, tokens, _ = inside.shape
    return call(
        linear_kernel,
        [SMEM] + [VMEM] * 6,
        [VMEM] * 2,
        [
            jax.ShapeDtypeStruct(inside.shape, F32),
            jax.ShapeDtypeStruct((ENERGY_ROWS, tokens), F32),
        ],
        after=after,
    )(me, terms, inside, sums, mine, theirs, other)


def halves(core, *arrays):
    early = [array[:, :HD] for array in arrays]
    late = [array[:, HD:] for array in arrays]
    mine = jnp.stack([jnp.where(core == 0, a, b) for a, b in zip(early, late)])
    theirs = jnp.stack([jnp.where(core == 0, b, a) for a, b in zip(early, late)])
    return mine, theirs


def pair_kernel(me_ref, mine_ref, other_ref, q_ref, out_ref, send_ref):
    tokens = mine_ref.shape[1]
    group = send_ref.shape[0]
    core = me_ref[0] & 1
    first = core == 0
    for side in range(2):
        mine, other = mine_ref[side], other_ref[side]
        out_ref[side, :tokens] = jnp.where(first, mine, other)
        out_ref[side, tokens:] = jnp.where(first, other, mine)
    for g in range(group):
        at = pl.ds(pl.multiple_of(((1 - core) * group + g) * HD, HD), HD)
        send_ref[g] = q_ref[:, at]


def pair_block(me, mine, other, q_soft, after):
    _, tokens, _ = mine.shape
    group = q_soft.shape[1] // (2 * HD)
    return call(
        pair_kernel,
        [SMEM] + [VMEM] * 3,
        [VMEM] * 2,
        [
            jax.ShapeDtypeStruct((2, 2 * tokens, HD), F32),
            jax.ShapeDtypeStruct((group, tokens, HD), F32),
        ],
        after=after,
    )(me, mine, other, q_soft)


def run(count, score, soften, gather):
    scores, before = score(0), None
    for i in range(count):
        following = score(i + 1) if i + 1 < count else None
        if before is not None:
            gather(i - 1, before)
        before = soften(i, scores)
        scores = following
    gather(count - 1, before)


def fill_terms(kv_ref, keys_ref, values_ref):
    k_high, k_low = split(kv_ref[0].T)
    keys_ref[:HD] = k_high
    keys_ref[HD : 2 * HD] = k_high
    keys_ref[2 * HD :] = k_low
    v_high, v_low = split(kv_ref[1])
    values_ref[:, :HD] = v_high
    values_ref[:, HD:] = v_low


def lane_max(array):
    peak = array[:, :HD]
    for c in range(1, array.shape[1] // HD):
        peak = jnp.maximum(peak, array[:, c * HD : (c + 1) * HD])
    return peak


def score_terms(pair):
    return jnp.concatenate([pair, pair[:, :HD]], axis=1)


def weigh(scores, peak, total):
    high, low = [], []
    for c in range(scores.shape[1] // HD):
        w = jnp.exp2(scores[:, c * HD : (c + 1) * HD] - peak)
        total = total + w
        pair = split(w)
        high.append(pair[0])
        low.append(pair[1])
    return jnp.concatenate(high, axis=1), jnp.concatenate(low, axis=1), total


def summed(high, low, values):
    wide = dot(high, values)
    return wide[:, :HD] + wide[:, HD:] + dot(low, values[:, :HD])


def own_kernel(factor, me_ref, q_ref, q_other_ref, kv_ref, q_out, acc_out, peak_out, total_out, keys_ref, values_ref):
    group, tokens = q_out.shape[0], q_ref.shape[0]
    core = me_ref[0] & 1
    first = core == 0
    fill_terms(kv_ref, keys_ref, values_ref)
    seen = lax.broadcasted_iota(jnp.int32, (tokens, tokens), 1)
    seen = seen <= lax.broadcasted_iota(jnp.int32, (tokens, tokens), 0)

    def where(i):
        t = i % 2
        return i // 2, slice(t * tokens, (t + 1) * tokens), slice(0, (t + 1) * tokens)

    def score(i):
        g, rows, keys = where(i)
        at = pl.ds(pl.multiple_of((core * group + g) * HD, HD), HD)
        mine, other = q_ref[:, at], q_other_ref[g]
        queries = jnp.where(first, mine, other) if i % 2 == 0 else jnp.where(first, other, mine)
        pair = jnp.concatenate(split(queries * factor), axis=1)
        q_out[g, rows] = pair
        s = dot(score_terms(pair), keys_ref[:, keys])
        edge = jnp.where(seen, s[:, rows], NEGATIVE)
        return edge if i % 2 == 0 else jnp.concatenate([s[:, :tokens], edge], axis=1)

    def soften(i, s):
        g, rows, _ = where(i)
        peak = jnp.max(lane_max(s), axis=1, keepdims=True)
        peak_out[g, rows] = jnp.broadcast_to(peak, (tokens, HD))
        high, low, total_out[g, rows] = weigh(s, peak, jnp.zeros((tokens, HD), F32))
        return high, low

    def gather(i, terms):
        g, rows, keys = where(i)
        acc_out[g, rows] = summed(*terms, values_ref[keys])

    run(2 * group, score, soften, gather)


def term_scratch(keys):
    return [pltpu.VMEM((3 * HD, keys), BF16), pltpu.VMEM((keys, 2 * HD), BF16)]


def own_stage(me, q_soft, q_other, kv, after):
    tokens, width = q_soft.shape
    group = width // (2 * HD)
    stat = jax.ShapeDtypeStruct((group, 2 * tokens, HD), F32)
    return call(
        functools.partial(own_kernel, math.log2(math.e) / math.sqrt(HD)),
        [SMEM] + [VMEM] * 3,
        [VMEM] * 4,
        [jax.ShapeDtypeStruct((group, 2 * tokens, 2 * HD), BF16), stat, stat, stat],
        term_scratch(2 * tokens),
        after=after,
    )(me, q_soft, q_other, kv)


def later_kernel(distance, parts, me_ref, kv_ref, q_ref, acc_ref, peak_ref, total_ref, acc_out, peak_out, total_out, keys_ref, values_ref):
    group, rows, _ = q_ref.shape
    size = rows // parts
    chip = me_ref[0] >> 1

    def where(i):
        return i // parts, slice(i % parts * size, (i % parts + 1) * size)

    def score(i):
        return dot(score_terms(q_ref[where(i)]), keys_ref[...])

    def soften(i, s):
        at = where(i)
        old = peak_ref[at]
        peak = jnp.maximum(jnp.max(lane_max(s), axis=1, keepdims=True), old)
        shrink = jnp.exp2(old - peak)
        peak_out[at] = peak
        high, low, total_out[at] = weigh(s, peak, total_ref[at] * shrink)
        return high, low, shrink

    def gather(i, terms):
        at = where(i)
        acc_out[at] = acc_ref[at] * terms[2] + summed(*terms[:2], values_ref[...])

    @pl.when(lax.bitwise_xor(chip, distance) < chip)
    def _():
        fill_terms(kv_ref, keys_ref, values_ref)
        run(parts * group, score, soften, gather)


def later_stage(me, distance, kv, q_terms, acc, peak, total, after, parts):
    return call(
        functools.partial(later_kernel, distance, parts),
        [SMEM] + [VMEM] * 5,
        [VMEM] * 3,
        [jax.ShapeDtypeStruct(acc.shape, F32)] * 3,
        term_scratch(kv.shape[1]),
        alias={3: 0, 4: 1, 5: 2},
        after=after,
    )(me, kv, q_terms, acc, peak, total)


def last_kernel(distance, whose, heads, columns, me_ref, kv_ref, q_ref, acc_ref, peak_ref, total_ref, *refs):
    if columns is None:
        out_ref, keys_ref, values_ref = refs
    else:
        theirs_ref, done_ref, energy_ref, energy_other_ref, gain_ref, linear_ref = refs[:6]
        lin_hbm, soft_hbm, lin_ref, out_ref, sems, keys_ref, values_ref = refs[6:]
    group, rows, _ = q_ref.shape
    tokens = rows // 2
    core, chip = me_ref[0] & 1, me_ref[0] >> 1
    side = core if whose == "own" else 1 - core
    at = pl.ds(pl.multiple_of(side * tokens, tokens), tokens)
    copies = []

    def copy_soft(source, whose, g):
        to = pl.ds(pl.multiple_of((whose * group + g) * HD, HD), HD)
        copies.append(pltpu.make_async_copy(source, soft_hbm.at[:, to], sems.at[len(copies)]))
        return copies[-1]

    if columns is not None:
        for g in range(group):
            copy_soft(theirs_ref.at[g], 1 - core, g).start()
        for g in range(done_ref.shape[0]):
            copy_soft(done_ref.at[g], core, g).start()
        factor = lax.rsqrt((energy_ref[:8] + energy_other_ref[:8]) / columns + EPSILON)
        factor = factor.T[:, 0:1]
        for h in range(linear_ref.shape[0]):
            to = slice(h * HD, (h + 1) * HD)
            lin_ref[h] = linear_ref[h] * factor * gain_ref[:, to]
            copies.append(
                pltpu.make_async_copy(lin_ref.at[h], lin_hbm.at[:, to], sems.at[len(copies)])
            )
            copies[-1].start()
        own_copies = [copy_soft(out_ref.at[n], core, g) for n, g in enumerate(heads)]

    def finish(n, acc, total):
        out_ref[n] = acc / jnp.sum(total, axis=1, keepdims=True)
        if columns is not None:
            own_copies[n].start()

    def score(n):
        return dot(score_terms(q_ref[heads[n], at]), keys_ref[...])

    def soften(n, s):
        old = peak_ref[heads[n], at]
        peak = jnp.maximum(jnp.max(lane_max(s), axis=1, keepdims=True), old)
        shrink = jnp.exp2(old - peak)
        return *weigh(s, peak, total_ref[heads[n], at] * shrink), shrink

    def gather(n, terms):
        high, low, total, shrink = terms
        new = summed(high, low, values_ref[...])
        finish(n, acc_ref[heads[n], at] * shrink + new, total)

    visible = lax.bitwise_xor(chip, distance) < chip

    @pl.when(visible)
    def _():
        fill_terms(kv_ref, keys_ref, values_ref)
        run(len(heads), score, soften, gather)

    @pl.when(jnp.logical_not(visible))
    def _():
        for n, g in enumerate(heads):
            finish(n, acc_ref[g, at], total_ref[g, at])

    for copy in copies:
        copy.wait()


def last_stage(me, distance, whose, heads, operands, after, extra=None):
    group, rows, _ = operands[1].shape
    tokens = rows // 2
    part = jax.ShapeDtypeStruct((len(heads), tokens, HD), F32)
    scratch = term_scratch(operands[0].shape[1])
    out_shape, out_spec, columns = part, VMEM, None
    if extra is not None:
        columns, more = extra
        operands = [*operands, *more]
        count = more[-1].shape[0]
        out_shape = [
            jax.ShapeDtypeStruct((tokens, count * HD), F32),
            jax.ShapeDtypeStruct((tokens, 2 * group * HD), F32),
        ]
        out_spec = [HBM] * 2
        scratch = [
            pltpu.VMEM((count, tokens, HD), F32),
            pltpu.VMEM(part.shape, F32),
            pltpu.SemaphoreType.DMA((2 * group + count,)),
        ] + scratch
    return call(
        functools.partial(last_kernel, distance, whose, heads, columns),
        [SMEM] + [VMEM] * len(operands),
        out_spec,
        out_shape,
        scratch,
        after=after,
    )(me, *operands)


def plus_kernel(a_ref, b_ref, out_ref):
    out_ref[...] = a_ref[...] + b_ref[...]


def plus(a, b, after):
    return call(
        plus_kernel, [VMEM] * 2, VMEM, jax.ShapeDtypeStruct(a.shape, F32), after=after
    )(a, b)


def copy_kernel(source_ref, out_ref):
    out_ref[...] = source_ref[...]


def copied(array, after):
    return call(copy_kernel, [VMEM], VMEM, jax.ShapeDtypeStruct(array.shape, F32), after=after)(
        array
    )


def relay_kernel(me_ref, own_ref, across_ref, out_ref):
    @pl.when((me_ref[0] & 1) == 0)
    def _():
        out_ref[...] = own_ref[...]

    @pl.when((me_ref[0] & 1) == 1)
    def _():
        out_ref[...] = across_ref[...]


def relayed(me, own, across, after):
    return call(
        relay_kernel,
        [SMEM, VMEM, VMEM],
        VMEM,
        jax.ShapeDtypeStruct(own.shape, F32),
        after=after,
    )(me, own, across)


def body(q_lin, k_lin, v_lin, log_decay, lin_gain, q_soft, k_soft, v_soft):
    chips = lax.axis_size("ctx") // 2
    heads = lax.axis_size("head")
    me = lax.axis_index("ctx")
    me_flag = me.reshape(1).astype(jnp.int32)
    assert k_soft.shape[1] == 2 * HD
    swap_pairs = [(2 * c + e, 2 * c + 1 - e) for c in range(chips) for e in range(2)]

    def swap(array):
        return lax.ppermute(array, "ctx", swap_pairs)

    def across(array, distance, wanted=lambda c, e: True):
        pairs = [
            (2 * (c ^ distance) + e, 2 * c + e)
            for c in range(chips)
            for e in range(2)
            if wanted(c, e)
        ]
        return lax.ppermute(array, "ctx", pairs)

    square = chips == 4
    kv_mine, kv_send = halves(me & 1, k_soft, v_soft)
    kv_other = swap(kv_send)
    states, sums = local_states(log_decay, k_lin, v_lin, [kv_mine])
    others = swap(states)
    kv, q_send = pair_block(me_flag, kv_mine, kv_other, q_soft, [sums])
    q_other = swap(q_send)
    total, prefix = chip_total(me_flag, states, others, [q_send]), None
    inside, terms = inside_blocks(q_lin, k_lin, v_lin, sums, [total])

    def exchanged(array, step):
        return lax.ppermute(array, "head", [(i, i ^ step) for i in range(heads)])

    def sent(distance, array):
        return across(array, distance, lambda c, e: c ^ distance < c)

    def stage(distance, carried, after, parts=2):
        return later_stage(
            me_flag, distance, arrived[distance], q_terms, *carried, after, parts
        )

    bits = chips.bit_length() - 1
    arrived, token = {}, inside
    if square:
        arrived[2] = sent(2, kv)
        token = copied(kv, [inside])
        arrived[1] = sent(1, token)
    else:
        for distance in range(1, chips):
            arrived[distance] = sent(distance, kv)
    q_terms, *carried = own_stage(me_flag, q_soft, q_other, kv, [token])
    token = carried[0]
    if square:
        relay = relayed(me_flag, kv, arrived[2], [token])
        arrived[3] = lax.ppermute(relay, "ctx", [(0, 6), (2, 4), (5, 7), (7, 5)])
    for bit in range(bits):
        last = bit == bits - 1
        theirs = across(total, 1 << bit, lambda c, e: not last or c ^ (1 << bit) < c)
        prefix, total = turn(me_flag, bit, total, theirs, prefix, last, [token])
        distance = 2 if square else bit + 1
        if not (square and last):
            carried = stage(distance, carried, [prefix, relay] if square else [prefix], 4)
            token = carried[0]
    prefix_other = swap(prefix)
    linear, energy = linear_blocks(
        me_flag, terms, inside, sums, prefix, prefix_other, others, []
    )
    energies, step = [], 1
    while step < heads:
        energies.append(step)
        step *= 2
    other = exchanged(energy, energies[0])
    for distance in [1] if square else range(bits + 1, chips - 1):
        carried = stage(distance, carried, [energy])
    for step in energies[1:]:
        energy = plus(energy, other, [carried[0]])
        other = exchanged(energy, step)

    operands = [arrived[chips - 1], q_terms, *carried]
    group = q_terms.shape[0]
    theirs = last_stage(me_flag, chips - 1, "other", range(group), operands, [energy])
    done = last_stage(me_flag, chips - 1, "own", range(group // 2), operands, [theirs])
    columns = q_lin.shape[1] * heads
    more = [swap(theirs), done, energy, other, lin_gain.reshape(1, -1), linear]
    return tuple(
        last_stage(
            me_flag, chips - 1, "own", range(group // 2, group), operands, [], (columns, more)
        )
    )


def solution(mesh):
    return jax.shard_map(
        body,
        mesh=mesh,
        in_specs=(
            P("ctx", "head"),
            P("ctx", "head"),
            P("ctx", "head"),
            P("head", "ctx"),
            P("head"),
            P("ctx", "head"),
            P("ctx", "head"),
            P("ctx", "head"),
        ),
        out_specs=(P("ctx", "head"), P("ctx", "head")),
        check_vma=False,
    )
```

```python
import functools
import math

import jax
import jax.numpy as jnp
from jax import lax
from jax.experimental import pallas as pl
from jax.experimental.pallas import tpu as pltpu
from jax.sharding import PartitionSpec as P

HD = 128
NEGATIVE = -1e30
EPSILON = 1e-05
ENERGY_ROWS = 16
F32 = jnp.float32
BF16 = jnp.bfloat16
NT = (((1,), (1,)), ((), ()))
VMEM_LIMIT = 32 * 1024 * 1024
VMEM = pl.BlockSpec(memory_space=pltpu.VMEM)
SMEM = pl.BlockSpec(memory_space=pltpu.SMEM)
ANY = pl.BlockSpec(memory_space=pl.ANY)
HBM = pl.BlockSpec(memory_space=pltpu.HBM)


def split(x):
    high = x.astype(BF16)
    low = (x - high.astype(F32)).astype(BF16)
    return high, low


def dot(a, b):
    return jnp.dot(a, b, preferred_element_type=F32)


def three_term(a, b):
    a_high, a_low = split(a)
    b_high, b_low = split(b)
    wide = dot(a_high, jnp.concatenate([b_high, b_low], axis=1))
    n = b.shape[1]
    return wide[:, :n] + wide[:, n:] + dot(a_low, b_high)


def call(kernel, in_specs, out_specs, out_shape, scratch=(), alias=None, after=()):
    count = len(in_specs)

    def ordered(*refs):
        kernel(*refs[:count], *refs[count + len(after) :])

    made = pl.pallas_call(
        ordered,
        in_specs=in_specs + [ANY] * len(after),
        out_specs=out_specs,
        out_shape=out_shape,
        scratch_shapes=list(scratch),
        input_output_aliases=alias or {},
        cost_estimate=pl.CostEstimate(flops=1, bytes_accessed=1, transcendentals=0),
        compiler_params=pltpu.CompilerParams(vmem_limit_bytes=VMEM_LIMIT),
    )
    return lambda *operands: made(*operands, *after)


def state_kernel(rate_ref, k_ref, v_ref, packed_ref, sums_ref):
    tokens = k_ref.shape[0]
    heads = rate_ref.shape[0]
    half = heads // 2
    upto = lax.broadcasted_iota(jnp.int32, (tokens, tokens), 0)
    upto = (upto <= lax.broadcasted_iota(jnp.int32, (tokens, tokens), 1)).astype(F32)
    sums = jnp.dot(
        rate_ref[...], upto, precision=lax.Precision.HIGHEST, preferred_element_type=F32
    )
    sums_ref[...] = sums
    totals = sums[:, tokens - 1 : tokens]
    trailing = jnp.exp(totals - sums)
    for side in range(2):
        packed_ref[side, half * HD :] = jnp.zeros((8, HD), F32)
    for h in range(heads):
        side, i = h // half, h % half
        at = slice(h * HD, (h + 1) * HD)
        packed_ref[side, i * HD : (i + 1) * HD] = three_term(
            k_ref[:, at].T * trailing[h : h + 1], v_ref[:, at]
        )
        packed_ref[side, half * HD + i : half * HD + i + 1] = jnp.broadcast_to(
            totals[h : h + 1], (1, HD)
        )


def local_states(rates, k_lin, v_lin, after):
    tokens = k_lin.shape[0]
    heads = rates.shape[0]
    return call(
        state_kernel,
        [VMEM] * 3,
        [VMEM] * 2,
        [
            jax.ShapeDtypeStruct((2, heads // 2 * HD + 8, HD), F32),
            jax.ShapeDtypeStruct((heads, tokens), F32),
        ],
        after=after,
    )(rates, k_lin, v_lin)


def join(half, first, second, out_ref):
    decay = jnp.exp(second[half * HD :, :])
    for i in range(half):
        at = slice(i * HD, (i + 1) * HD)
        out_ref[at] = first[at] * decay[i : i + 1] + second[at]
    out_ref[half * HD :] = first[half * HD :] + second[half * HD :]


def chip_kernel(half, me_ref, states_ref, others_ref, out_ref):
    core = me_ref[0] & 1

    @pl.when(core == 0)
    def _():
        join(half, states_ref[0], others_ref[0], out_ref)

    @pl.when(core == 1)
    def _():
        join(half, others_ref[1], states_ref[1], out_ref)


def chip_total(me, states, others, after):
    _, packed, _ = states.shape
    return call(
        functools.partial(chip_kernel, (packed - 8) // HD),
        [SMEM, VMEM, VMEM],
        VMEM,
        jax.ShapeDtypeStruct((packed, HD), F32),
        after=after,
    )(me, states, others)


def turn_kernel(half, bit, first, last, me_ref, total_ref, theirs_ref, *refs):
    refs = list(refs)
    before_ref = None if first else refs.pop(0)
    prefix_ref = refs.pop(0)
    total_out = None if last else refs.pop(0)
    late = (me_ref[0] >> (bit + 1)) & 1

    @pl.when(late == 0)
    def _():
        prefix_ref[...] = jnp.zeros_like(prefix_ref) if first else before_ref[...]
        if not last:
            join(half, total_ref[...], theirs_ref[...], total_out)

    @pl.when(late == 1)
    def _():
        if first:
            prefix_ref[...] = theirs_ref[...]
        else:
            join(half, theirs_ref[...], before_ref[...], prefix_ref)
        if not last:
            join(half, theirs_ref[...], total_ref[...], total_out)


def turn(me, bit, total, theirs, before, last, after):
    packed = total.shape[0]
    operands = [total, theirs] + ([] if before is None else [before])
    count = 1 if last else 2
    out = call(
        functools.partial(turn_kernel, (packed - 8) // HD, bit, before is None, last),
        [SMEM] + [VMEM] * len(operands),
        [VMEM] * count,
        [jax.ShapeDtypeStruct((packed, HD), F32)] * count,
        after=after,
    )(me, *operands)
    return out[0], (None if last else out[1])


def inside_kernel(q_ref, k_ref, v_ref, sums_ref, out_ref, terms_ref):
    tokens = q_ref.shape[0]
    heads = sums_ref.shape[0]
    causal = lax.broadcasted_iota(jnp.int32, (tokens, tokens), 0) >= lax.broadcasted_iota(
        jnp.int32, (tokens, tokens), 1
    )
    columns = sums_ref[...].T
    for h in range(heads):
        at = slice(h * HD, (h + 1) * HD)
        q_high, q_low = split(q_ref[:, at])
        k_high, k_low = split(k_ref[:, at])
        terms_ref[h, :, :HD] = q_high
        terms_ref[h, :, HD:] = q_low
        scores = lax.dot_general(
            jnp.concatenate([q_high, q_low, q_high], axis=1),
            jnp.concatenate([k_high, k_high, k_low], axis=1),
            NT,
            preferred_element_type=F32,
        )
        gaps = columns[:, h : h + 1] - sums_ref[h : h + 1, :]
        weights = jnp.where(causal, jnp.exp(jnp.where(causal, gaps, 0.0)), 0.0)
        out_ref[h] = three_term(scores * weights, v_ref[:, at])


def inside_blocks(q_lin, k_lin, v_lin, sums, after):
    tokens = q_lin.shape[0]
    heads = sums.shape[0]
    return call(
        inside_kernel,
        [VMEM] * 4,
        [VMEM] * 2,
        [
            jax.ShapeDtypeStruct((heads, tokens, HD), F32),
            jax.ShapeDtypeStruct((heads, tokens, 2 * HD), BF16),
        ],
        after=after,
    )(q_lin, k_lin, v_lin, sums)


def linear_kernel(me_ref, terms_ref, inside_ref, sums_ref, mine_ref, theirs_ref, other_ref, out_ref, energy_ref):
    heads, tokens, _ = out_ref.shape
    half = heads // 2
    core = me_ref[0] & 1
    leading = jnp.exp(sums_ref[...]).T
    squares = jnp.zeros((tokens, HD), F32)
    for side in range(2):
        decay = jnp.exp(other_ref[side, half * HD :])
        for i in range(half):
            h = side * half + i
            at = slice(i * HD, (i + 1) * HD)
            prior = jnp.where(core == side, mine_ref[at], theirs_ref[at])
            prior = jnp.where(core == 1, prior * decay[i : i + 1] + other_ref[side, at], prior)
            high, low = split(prior)
            wide = dot(terms_ref[h, :, :HD], jnp.concatenate([high, low], axis=1))
            carried = wide[:, :HD] + wide[:, HD:] + dot(terms_ref[h, :, HD:], high)
            linear = inside_ref[h] + leading[:, h : h + 1] * carried
            out_ref[h] = linear
            squares = squares + linear * linear
    energy_ref[...] = lax.dot_general(
        jnp.ones((energy_ref.shape[0], HD), F32),
        squares,
        NT,
        precision=lax.Precision.HIGHEST,
        preferred_element_type=F32,
    )


def linear_blocks(me, terms, inside, sums, mine, theirs, other, after):
    _, tokens, _ = inside.shape
    return call(
        linear_kernel,
        [SMEM] + [VMEM] * 6,
        [VMEM] * 2,
        [
            jax.ShapeDtypeStruct(inside.shape, F32),
            jax.ShapeDtypeStruct((ENERGY_ROWS, tokens), F32),
        ],
        after=after,
    )(me, terms, inside, sums, mine, theirs, other)


def halves(core, *arrays):
    early = [array[:, :HD] for array in arrays]
    late = [array[:, HD:] for array in arrays]
    mine = jnp.stack([jnp.where(core == 0, a, b) for a, b in zip(early, late)])
    theirs = jnp.stack([jnp.where(core == 0, b, a) for a, b in zip(early, late)])
    return mine, theirs


def pair_kernel(me_ref, mine_ref, other_ref, q_ref, out_ref, send_ref):
    tokens = mine_ref.shape[1]
    group = send_ref.shape[0]
    core = me_ref[0] & 1
    first = core == 0
    for side in range(2):
        mine, other = mine_ref[side], other_ref[side]
        out_ref[side, :tokens] = jnp.where(first, mine, other)
        out_ref[side, tokens:] = jnp.where(first, other, mine)
    for g in range(group):
        at = pl.ds(pl.multiple_of(((1 - core) * group + g) * HD, HD), HD)
        send_ref[g] = q_ref[:, at]


def pair_block(me, mine, other, q_soft, after):
    _, tokens, _ = mine.shape
    group = q_soft.shape[1] // (2 * HD)
    return call(
        pair_kernel,
        [SMEM] + [VMEM] * 3,
        [VMEM] * 2,
        [
            jax.ShapeDtypeStruct((2, 2 * tokens, HD), F32),
            jax.ShapeDtypeStruct((group, tokens, HD), F32),
        ],
        after=after,
    )(me, mine, other, q_soft)


def run(count, score, soften, gather):
    scores, before = score(0), None
    for i in range(count):
        following = score(i + 1) if i + 1 < count else None
        if before is not None:
            gather(i - 1, before)
        before = soften(i, scores)
        scores = following
    gather(count - 1, before)


def fill_terms(kv_ref, keys_ref, values_ref):
    k_high, k_low = split(kv_ref[0].T)
    keys_ref[:HD] = k_high
    keys_ref[HD : 2 * HD] = k_high
    keys_ref[2 * HD :] = k_low
    v_high, v_low = split(kv_ref[1])
    values_ref[:, :HD] = v_high
    values_ref[:, HD:] = v_low


def lane_max(array):
    peak = array[:, :HD]
    for c in range(1, array.shape[1] // HD):
        peak = jnp.maximum(peak, array[:, c * HD : (c + 1) * HD])
    return peak


def score_terms(pair):
    return jnp.concatenate([pair, pair[:, :HD]], axis=1)


def weigh(scores, peak, total):
    high, low = [], []
    for c in range(scores.shape[1] // HD):
        w = jnp.exp2(scores[:, c * HD : (c + 1) * HD] - peak)
        total = total + w
        pair = split(w)
        high.append(pair[0])
        low.append(pair[1])
    return jnp.concatenate(high, axis=1), jnp.concatenate(low, axis=1), total


def summed(high, low, values):
    wide = dot(high, values)
    return wide[:, :HD] + wide[:, HD:] + dot(low, values[:, :HD])


def own_kernel(factor, me_ref, q_ref, q_other_ref, kv_ref, q_out, acc_out, peak_out, total_out, keys_ref, values_ref):
    group, tokens = q_out.shape[0], q_ref.shape[0]
    core = me_ref[0] & 1
    first = core == 0
    fill_terms(kv_ref, keys_ref, values_ref)
    seen = lax.broadcasted_iota(jnp.int32, (tokens, tokens), 1)
    seen = seen <= lax.broadcasted_iota(jnp.int32, (tokens, tokens), 0)

    def where(i):
        t = i % 2
        return i // 2, slice(t * tokens, (t + 1) * tokens), slice(0, (t + 1) * tokens)

    def score(i):
        g, rows, keys = where(i)
        at = pl.ds(pl.multiple_of((core * group + g) * HD, HD), HD)
        mine, other = q_ref[:, at], q_other_ref[g]
        queries = jnp.where(first, mine, other) if i % 2 == 0 else jnp.where(first, other, mine)
        pair = jnp.concatenate(split(queries * factor), axis=1)
        q_out[g, rows] = pair
        s = dot(score_terms(pair), keys_ref[:, keys])
        edge = jnp.where(seen, s[:, rows], NEGATIVE)
        return edge if i % 2 == 0 else jnp.concatenate([s[:, :tokens], edge], axis=1)

    def soften(i, s):
        g, rows, _ = where(i)
        peak = jnp.max(lane_max(s), axis=1, keepdims=True)
        peak_out[g, rows] = jnp.broadcast_to(peak, (tokens, HD))
        high, low, total_out[g, rows] = weigh(s, peak, jnp.zeros((tokens, HD), F32))
        return high, low

    def gather(i, terms):
        g, rows, keys = where(i)
        acc_out[g, rows] = summed(*terms, values_ref[keys])

    run(2 * group, score, soften, gather)


def term_scratch(keys):
    return [pltpu.VMEM((3 * HD, keys), BF16), pltpu.VMEM((keys, 2 * HD), BF16)]


def own_stage(me, q_soft, q_other, kv, after):
    tokens, width = q_soft.shape
    group = width // (2 * HD)
    stat = jax.ShapeDtypeStruct((group, 2 * tokens, HD), F32)
    return call(
        functools.partial(own_kernel, math.log2(math.e) / math.sqrt(HD)),
        [SMEM] + [VMEM] * 3,
        [VMEM] * 4,
        [jax.ShapeDtypeStruct((group, 2 * tokens, 2 * HD), BF16), stat, stat, stat],
        term_scratch(2 * tokens),
        after=after,
    )(me, q_soft, q_other, kv)


def later_kernel(distance, parts, me_ref, kv_ref, q_ref, acc_ref, peak_ref, total_ref, acc_out, peak_out, total_out, keys_ref, values_ref):
    group, rows, _ = q_ref.shape
    size = rows // parts
    chip = me_ref[0] >> 1

    def where(i):
        return i // parts, slice(i % parts * size, (i % parts + 1) * size)

    def score(i):
        return dot(score_terms(q_ref[where(i)]), keys_ref[...])

    def soften(i, s):
        at = where(i)
        old = peak_ref[at]
        peak = jnp.maximum(jnp.max(lane_max(s), axis=1, keepdims=True), old)
        shrink = jnp.exp2(old - peak)
        peak_out[at] = peak
        high, low, total_out[at] = weigh(s, peak, total_ref[at] * shrink)
        return high, low, shrink

    def gather(i, terms):
        at = where(i)
        acc_out[at] = acc_ref[at] * terms[2] + summed(*terms[:2], values_ref[...])

    @pl.when(lax.bitwise_xor(chip, distance) < chip)
    def _():
        fill_terms(kv_ref, keys_ref, values_ref)
        run(parts * group, score, soften, gather)


def later_stage(me, distance, kv, q_terms, acc, peak, total, after, parts):
    return call(
        functools.partial(later_kernel, distance, parts),
        [SMEM] + [VMEM] * 5,
        [VMEM] * 3,
        [jax.ShapeDtypeStruct(acc.shape, F32)] * 3,
        term_scratch(kv.shape[1]),
        alias={3: 0, 4: 1, 5: 2},
        after=after,
    )(me, kv, q_terms, acc, peak, total)


def last_kernel(distance, whose, heads, columns, me_ref, kv_ref, q_ref, acc_ref, peak_ref, total_ref, *refs):
    if columns is None:
        out_ref, keys_ref, values_ref = refs
    else:
        theirs_ref, done_ref, energy_ref, energy_other_ref, gain_ref, linear_ref = refs[:6]
        lin_hbm, soft_hbm, lin_ref, out_ref, sems, keys_ref, values_ref = refs[6:]
    group, rows, _ = q_ref.shape
    tokens = rows // 2
    core, chip = me_ref[0] & 1, me_ref[0] >> 1
    side = core if whose == "own" else 1 - core
    at = pl.ds(pl.multiple_of(side * tokens, tokens), tokens)
    copies = []

    def copy_soft(source, whose, g):
        to = pl.ds(pl.multiple_of((whose * group + g) * HD, HD), HD)
        copies.append(pltpu.make_async_copy(source, soft_hbm.at[:, to], sems.at[len(copies)]))
        return copies[-1]

    if columns is not None:
        for g in range(group):
            copy_soft(theirs_ref.at[g], 1 - core, g).start()
        for g in range(done_ref.shape[0]):
            copy_soft(done_ref.at[g], core, g).start()
        factor = lax.rsqrt((energy_ref[:8] + energy_other_ref[:8]) / columns + EPSILON)
        factor = factor.T[:, 0:1]
        for h in range(linear_ref.shape[0]):
            to = slice(h * HD, (h + 1) * HD)
            lin_ref[h] = linear_ref[h] * factor * gain_ref[:, to]
            copies.append(
                pltpu.make_async_copy(lin_ref.at[h], lin_hbm.at[:, to], sems.at[len(copies)])
            )
            copies[-1].start()
        own_copies = [copy_soft(out_ref.at[n], core, g) for n, g in enumerate(heads)]

    def finish(n, acc, total):
        out_ref[n] = acc / jnp.sum(total, axis=1, keepdims=True)
        if columns is not None:
            own_copies[n].start()

    def score(n):
        return dot(score_terms(q_ref[heads[n], at]), keys_ref[...])

    def soften(n, s):
        old = peak_ref[heads[n], at]
        peak = jnp.maximum(jnp.max(lane_max(s), axis=1, keepdims=True), old)
        shrink = jnp.exp2(old - peak)
        return *weigh(s, peak, total_ref[heads[n], at] * shrink), shrink

    def gather(n, terms):
        high, low, total, shrink = terms
        new = summed(high, low, values_ref[...])
        finish(n, acc_ref[heads[n], at] * shrink + new, total)

    visible = lax.bitwise_xor(chip, distance) < chip

    @pl.when(visible)
    def _():
        fill_terms(kv_ref, keys_ref, values_ref)
        run(len(heads), score, soften, gather)

    @pl.when(jnp.logical_not(visible))
    def _():
        for n, g in enumerate(heads):
            finish(n, acc_ref[g, at], total_ref[g, at])

    for copy in copies:
        copy.wait()


def last_stage(me, distance, whose, heads, operands, after, extra=None):
    group, rows, _ = operands[1].shape
    tokens = rows // 2
    part = jax.ShapeDtypeStruct((len(heads), tokens, HD), F32)
    scratch = term_scratch(operands[0].shape[1])
    out_shape, out_spec, columns = part, VMEM, None
    if extra is not None:
        columns, more = extra
        operands = [*operands, *more]
        count = more[-1].shape[0]
        out_shape = [
            jax.ShapeDtypeStruct((tokens, count * HD), F32),
            jax.ShapeDtypeStruct((tokens, 2 * group * HD), F32),
        ]
        out_spec = [HBM] * 2
        scratch = [
            pltpu.VMEM((count, tokens, HD), F32),
            pltpu.VMEM(part.shape, F32),
            pltpu.SemaphoreType.DMA((2 * group + count,)),
        ] + scratch
    return call(
        functools.partial(last_kernel, distance, whose, heads, columns),
        [SMEM] + [VMEM] * len(operands),
        out_spec,
        out_shape,
        scratch,
        after=after,
    )(me, *operands)


def plus_kernel(a_ref, b_ref, out_ref):
    out_ref[...] = a_ref[...] + b_ref[...]


def plus(a, b, after):
    return call(
        plus_kernel, [VMEM] * 2, VMEM, jax.ShapeDtypeStruct(a.shape, F32), after=after
    )(a, b)


def copy_kernel(source_ref, out_ref):
    out_ref[...] = source_ref[...]


def copied(array, after):
    return call(copy_kernel, [VMEM], VMEM, jax.ShapeDtypeStruct(array.shape, F32), after=after)(
        array
    )


def relay_kernel(me_ref, own_ref, across_ref, out_ref):
    @pl.when((me_ref[0] & 1) == 0)
    def _():
        out_ref[...] = own_ref[...]

    @pl.when((me_ref[0] & 1) == 1)
    def _():
        out_ref[...] = across_ref[...]


def relayed(me, own, across, after):
    return call(
        relay_kernel,
        [SMEM, VMEM, VMEM],
        VMEM,
        jax.ShapeDtypeStruct(own.shape, F32),
        after=after,
    )(me, own, across)


def body(q_lin, k_lin, v_lin, log_decay, lin_gain, q_soft, k_soft, v_soft):
    chips = lax.axis_size("ctx") // 2
    heads = lax.axis_size("head")
    me = lax.axis_index("ctx")
    me_flag = me.reshape(1).astype(jnp.int32)
    assert k_soft.shape[1] == 2 * HD
    swap_pairs = [(2 * c + e, 2 * c + 1 - e) for c in range(chips) for e in range(2)]

    def swap(array):
        return lax.ppermute(array, "ctx", swap_pairs)

    def across(array, distance, wanted=lambda c, e: True):
        pairs = [
            (2 * (c ^ distance) + e, 2 * c + e)
            for c in range(chips)
            for e in range(2)
            if wanted(c, e)
        ]
        return lax.ppermute(array, "ctx", pairs)

    square = chips == 4
    kv_mine, kv_send = halves(me & 1, k_soft, v_soft)
    kv_other = swap(kv_send)
    states, sums = local_states(log_decay, k_lin, v_lin, [kv_mine])
    others = swap(states)
    kv, q_send = pair_block(me_flag, kv_mine, kv_other, q_soft, [sums])
    q_other = swap(q_send)
    total, prefix = chip_total(me_flag, states, others, [q_send]), None
    inside, terms = inside_blocks(q_lin, k_lin, v_lin, sums, [total])

    def exchanged(array, step):
        return lax.ppermute(array, "head", [(i, i ^ step) for i in range(heads)])

    def sent(distance, array):
        return across(array, distance, lambda c, e: c ^ distance < c)

    def stage(distance, carried, after, parts=2):
        return later_stage(
            me_flag, distance, arrived[distance], q_terms, *carried, after, parts
        )

    bits = chips.bit_length() - 1
    arrived, token = {}, inside
    if square:
        arrived[2] = sent(2, kv)
        token = copied(kv, [inside])
        arrived[1] = sent(1, token)
    else:
        for distance in range(1, chips):
            arrived[distance] = sent(distance, kv)
    q_terms, *carried = own_stage(me_flag, q_soft, q_other, kv, [token])
    token = carried[0]
    if square:
        relay = relayed(me_flag, kv, arrived[2], [token])
        arrived[3] = lax.ppermute(relay, "ctx", [(0, 6), (2, 4), (5, 7), (7, 5)])
    for bit in range(bits):
        last = bit == bits - 1
        theirs = across(total, 1 << bit, lambda c, e: not last or c ^ (1 << bit) < c)
        prefix, total = turn(me_flag, bit, total, theirs, prefix, last, [token] + ([arrived[1]] if square and last else []))
        distance = 2 if square else bit + 1
        if not (square and last):
            carried = stage(distance, carried, [prefix, relay] if square else [prefix], 4)
            token = carried[0]
    prefix_other = swap(prefix)
    for distance in [1] if square else range(bits + 1, chips - 1):
        carried = stage(distance, carried, [prefix], 4)
    linear, energy = linear_blocks(
        me_flag, terms, inside, sums, prefix, prefix_other, others, [carried[0]]
    )
    energies, step = [], 1
    while step < heads:
        energies.append(step)
        step *= 2
    other = exchanged(energy, energies[0])
    operands = [arrived[chips - 1], q_terms, *carried]
    group = q_terms.shape[0]
    theirs = last_stage(me_flag, chips - 1, "other", range(group), operands, [energy])
    for step in energies[1:]:
        energy = plus(energy, other, [theirs])
        other = exchanged(energy, step)

    done = last_stage(me_flag, chips - 1, "own", range(group // 2), operands, [theirs])
    columns = q_lin.shape[1] * heads
    more = [swap(theirs), done, energy, other, lin_gain.reshape(1, -1), linear]
    return tuple(
        last_stage(
            me_flag, chips - 1, "own", range(group // 2, group), operands, [], (columns, more)
        )
    )


def solution(mesh):
    return jax.shard_map(
        body,
        mesh=mesh,
        in_specs=(
            P("ctx", "head"),
            P("ctx", "head"),
            P("ctx", "head"),
            P("head", "ctx"),
            P("head"),
            P("ctx", "head"),
            P("ctx", "head"),
            P("ctx", "head"),
        ),
        out_specs=(P("ctx", "head"), P("ctx", "head")),
        check_vma=False,
    )
```

```python
import functools
import math

import jax
import jax.numpy as jnp
from jax import lax
from jax.experimental import pallas as pl
from jax.experimental.pallas import tpu as pltpu
from jax.sharding import PartitionSpec as P

HD = 128
NEGATIVE = -1e30
EPSILON = 1e-05
ENERGY_ROWS = 16
F32 = jnp.float32
BF16 = jnp.bfloat16
NT = (((1,), (1,)), ((), ()))
VMEM_LIMIT = 32 * 1024 * 1024
VMEM = pl.BlockSpec(memory_space=pltpu.VMEM)
SMEM = pl.BlockSpec(memory_space=pltpu.SMEM)
ANY = pl.BlockSpec(memory_space=pl.ANY)
HBM = pl.BlockSpec(memory_space=pltpu.HBM)


def split(x):
    high = x.astype(BF16)
    low = (x - high.astype(F32)).astype(BF16)
    return high, low


def dot(a, b):
    return jnp.dot(a, b, preferred_element_type=F32)


def three_term(a, b):
    a_high, a_low = split(a)
    b_high, b_low = split(b)
    wide = dot(a_high, jnp.concatenate([b_high, b_low], axis=1))
    n = b.shape[1]
    return wide[:, :n] + wide[:, n:] + dot(a_low, b_high)


def call(kernel, in_specs, out_specs, out_shape, scratch=(), alias=None, after=()):
    count = len(in_specs)

    def ordered(*refs):
        kernel(*refs[:count], *refs[count + len(after) :])

    made = pl.pallas_call(
        ordered,
        in_specs=in_specs + [ANY] * len(after),
        out_specs=out_specs,
        out_shape=out_shape,
        scratch_shapes=list(scratch),
        input_output_aliases=alias or {},
        cost_estimate=pl.CostEstimate(flops=1, bytes_accessed=1, transcendentals=0),
        compiler_params=pltpu.CompilerParams(vmem_limit_bytes=VMEM_LIMIT),
    )
    return lambda *operands: made(*operands, *after)


def state_kernel(rate_ref, k_ref, v_ref, packed_ref, sums_ref):
    tokens = k_ref.shape[0]
    heads = rate_ref.shape[0]
    half = heads // 2
    upto = lax.broadcasted_iota(jnp.int32, (tokens, tokens), 0)
    upto = (upto <= lax.broadcasted_iota(jnp.int32, (tokens, tokens), 1)).astype(F32)
    sums = jnp.dot(
        rate_ref[...], upto, precision=lax.Precision.HIGHEST, preferred_element_type=F32
    )
    sums_ref[...] = sums
    totals = sums[:, tokens - 1 : tokens]
    trailing = jnp.exp(totals - sums)
    for side in range(2):
        packed_ref[side, half * HD :] = jnp.zeros((8, HD), F32)
    for h in range(heads):
        side, i = h // half, h % half
        at = slice(h * HD, (h + 1) * HD)
        packed_ref[side, i * HD : (i + 1) * HD] = three_term(
            k_ref[:, at].T * trailing[h : h + 1], v_ref[:, at]
        )
        packed_ref[side, half * HD + i : half * HD + i + 1] = jnp.broadcast_to(
            totals[h : h + 1], (1, HD)
        )


def local_states(rates, k_lin, v_lin, after):
    tokens = k_lin.shape[0]
    heads = rates.shape[0]
    return call(
        state_kernel,
        [VMEM] * 3,
        [VMEM] * 2,
        [
            jax.ShapeDtypeStruct((2, heads // 2 * HD + 8, HD), F32),
            jax.ShapeDtypeStruct((heads, tokens), F32),
        ],
        after=after,
    )(rates, k_lin, v_lin)


def join(half, first, second, out_ref):
    decay = jnp.exp(second[half * HD :, :])
    for i in range(half):
        at = slice(i * HD, (i + 1) * HD)
        out_ref[at] = first[at] * decay[i : i + 1] + second[at]
    out_ref[half * HD :] = first[half * HD :] + second[half * HD :]


def chip_kernel(half, me_ref, states_ref, others_ref, out_ref):
    core = me_ref[0] & 1

    @pl.when(core == 0)
    def _():
        join(half, states_ref[0], others_ref[0], out_ref)

    @pl.when(core == 1)
    def _():
        join(half, others_ref[1], states_ref[1], out_ref)


def chip_total(me, states, others, after):
    _, packed, _ = states.shape
    return call(
        functools.partial(chip_kernel, (packed - 8) // HD),
        [SMEM, VMEM, VMEM],
        VMEM,
        jax.ShapeDtypeStruct((packed, HD), F32),
        after=after,
    )(me, states, others)


def turn_kernel(half, bit, first, last, me_ref, total_ref, theirs_ref, *refs):
    refs = list(refs)
    before_ref = None if first else refs.pop(0)
    prefix_ref = refs.pop(0)
    total_out = None if last else refs.pop(0)
    late = (me_ref[0] >> (bit + 1)) & 1

    @pl.when(late == 0)
    def _():
        prefix_ref[...] = jnp.zeros_like(prefix_ref) if first else before_ref[...]
        if not last:
            join(half, total_ref[...], theirs_ref[...], total_out)

    @pl.when(late == 1)
    def _():
        if first:
            prefix_ref[...] = theirs_ref[...]
        else:
            join(half, theirs_ref[...], before_ref[...], prefix_ref)
        if not last:
            join(half, theirs_ref[...], total_ref[...], total_out)


def turn(me, bit, total, theirs, before, last, after):
    packed = total.shape[0]
    operands = [total, theirs] + ([] if before is None else [before])
    count = 1 if last else 2
    out = call(
        functools.partial(turn_kernel, (packed - 8) // HD, bit, before is None, last),
        [SMEM] + [VMEM] * len(operands),
        [VMEM] * count,
        [jax.ShapeDtypeStruct((packed, HD), F32)] * count,
        after=after,
    )(me, *operands)
    return out[0], (None if last else out[1])


def inside_kernel(q_ref, k_ref, v_ref, sums_ref, out_ref, terms_ref):
    tokens = q_ref.shape[0]
    heads = sums_ref.shape[0]
    causal = lax.broadcasted_iota(jnp.int32, (tokens, tokens), 0) >= lax.broadcasted_iota(
        jnp.int32, (tokens, tokens), 1
    )
    columns = sums_ref[...].T
    for h in range(heads):
        at = slice(h * HD, (h + 1) * HD)
        q_high, q_low = split(q_ref[:, at])
        k_high, k_low = split(k_ref[:, at])
        terms_ref[h, :, :HD] = q_high
        terms_ref[h, :, HD:] = q_low
        scores = lax.dot_general(
            jnp.concatenate([q_high, q_low, q_high], axis=1),
            jnp.concatenate([k_high, k_high, k_low], axis=1),
            NT,
            preferred_element_type=F32,
        )
        gaps = columns[:, h : h + 1] - sums_ref[h : h + 1, :]
        weights = jnp.where(causal, jnp.exp(jnp.where(causal, gaps, 0.0)), 0.0)
        out_ref[h] = three_term(scores * weights, v_ref[:, at])


def inside_blocks(q_lin, k_lin, v_lin, sums, after):
    tokens = q_lin.shape[0]
    heads = sums.shape[0]
    return call(
        inside_kernel,
        [VMEM] * 4,
        [VMEM] * 2,
        [
            jax.ShapeDtypeStruct((heads, tokens, HD), F32),
            jax.ShapeDtypeStruct((heads, tokens, 2 * HD), BF16),
        ],
        after=after,
    )(q_lin, k_lin, v_lin, sums)


def linear_kernel(me_ref, terms_ref, inside_ref, sums_ref, mine_ref, theirs_ref, other_ref, out_ref, energy_ref):
    heads, tokens, _ = inside_ref.shape
    half = heads // 2
    core = me_ref[0] & 1
    leading = jnp.exp(sums_ref[...]).T
    squares = jnp.zeros((tokens, HD), F32)
    for side in range(2):
        decay = jnp.exp(other_ref[side, half * HD :])
        for i in range(half):
            h = side * half + i
            at = slice(i * HD, (i + 1) * HD)
            prior = jnp.where(core == side, mine_ref[at], theirs_ref[at])
            prior = jnp.where(core == 1, prior * decay[i : i + 1] + other_ref[side, at], prior)
            high, low = split(prior)
            wide = dot(terms_ref[h, :, :HD], jnp.concatenate([high, low], axis=1))
            carried = wide[:, :HD] + wide[:, HD:] + dot(terms_ref[h, :, HD:], high)
            linear = inside_ref[h] + leading[:, h : h + 1] * carried
            out_ref[:, h * HD : (h + 1) * HD] = linear
            squares = squares + linear * linear
    energy_ref[...] = lax.dot_general(
        jnp.ones((energy_ref.shape[0], HD), F32),
        squares,
        NT,
        precision=lax.Precision.HIGHEST,
        preferred_element_type=F32,
    )


def linear_blocks(me, terms, inside, sums, mine, theirs, other, after):
    heads, tokens, _ = inside.shape
    return call(
        linear_kernel,
        [SMEM] + [VMEM] * 6,
        [VMEM] * 2,
        [
            jax.ShapeDtypeStruct((tokens, heads * HD), F32),
            jax.ShapeDtypeStruct((ENERGY_ROWS, tokens), F32),
        ],
        after=after,
    )(me, terms, inside, sums, mine, theirs, other)


def halves(core, *arrays):
    early = [array[:, :HD] for array in arrays]
    late = [array[:, HD:] for array in arrays]
    mine = jnp.stack([jnp.where(core == 0, a, b) for a, b in zip(early, late)])
    theirs = jnp.stack([jnp.where(core == 0, b, a) for a, b in zip(early, late)])
    return mine, theirs


def pair_kernel(me_ref, mine_ref, other_ref, q_ref, out_ref, send_ref):
    tokens = mine_ref.shape[1]
    group = send_ref.shape[0]
    core = me_ref[0] & 1
    first = core == 0
    for side in range(2):
        mine, other = mine_ref[side], other_ref[side]
        out_ref[side, :tokens] = jnp.where(first, mine, other)
        out_ref[side, tokens:] = jnp.where(first, other, mine)
    for g in range(group):
        at = pl.ds(pl.multiple_of(((1 - core) * group + g) * HD, HD), HD)
        send_ref[g] = q_ref[:, at]


def pair_block(me, mine, other, q_soft, after):
    _, tokens, _ = mine.shape
    group = q_soft.shape[1] // (2 * HD)
    return call(
        pair_kernel,
        [SMEM] + [VMEM] * 3,
        [VMEM] * 2,
        [
            jax.ShapeDtypeStruct((2, 2 * tokens, HD), F32),
            jax.ShapeDtypeStruct((group, tokens, HD), F32),
        ],
        after=after,
    )(me, mine, other, q_soft)


def run(count, score, soften, gather):
    scores, before = score(0), None
    for i in range(count):
        following = score(i + 1) if i + 1 < count else None
        if before is not None:
            gather(i - 1, before)
        before = soften(i, scores)
        scores = following
    gather(count - 1, before)


def fill_terms(kv_ref, keys_ref, values_ref):
    k_high, k_low = split(kv_ref[0].T)
    keys_ref[:HD] = k_high
    keys_ref[HD : 2 * HD] = k_high
    keys_ref[2 * HD :] = k_low
    v_high, v_low = split(kv_ref[1])
    values_ref[:, :HD] = v_high
    values_ref[:, HD:] = v_low


def lane_max(array):
    peak = array[:, :HD]
    for c in range(1, array.shape[1] // HD):
        peak = jnp.maximum(peak, array[:, c * HD : (c + 1) * HD])
    return peak


def score_terms(pair):
    return jnp.concatenate([pair, pair[:, :HD]], axis=1)


def weigh(scores, peak, total):
    high, low = [], []
    for c in range(scores.shape[1] // HD):
        w = jnp.exp2(scores[:, c * HD : (c + 1) * HD] - peak)
        total = total + w
        pair = split(w)
        high.append(pair[0])
        low.append(pair[1])
    return jnp.concatenate(high, axis=1), jnp.concatenate(low, axis=1), total


def summed(high, low, values):
    wide = dot(high, values)
    return wide[:, :HD] + wide[:, HD:] + dot(low, values[:, :HD])


def own_kernel(factor, me_ref, q_ref, q_other_ref, kv_ref, q_out, acc_out, peak_out, total_out, keys_ref, values_ref):
    group, tokens = q_out.shape[0], q_ref.shape[0]
    core = me_ref[0] & 1
    first = core == 0
    fill_terms(kv_ref, keys_ref, values_ref)
    seen = lax.broadcasted_iota(jnp.int32, (tokens, tokens), 1)
    seen = seen <= lax.broadcasted_iota(jnp.int32, (tokens, tokens), 0)

    def where(i):
        t = i % 2
        return i // 2, slice(t * tokens, (t + 1) * tokens), slice(0, (t + 1) * tokens)

    def score(i):
        g, rows, keys = where(i)
        at = pl.ds(pl.multiple_of((core * group + g) * HD, HD), HD)
        mine, other = q_ref[:, at], q_other_ref[g]
        queries = jnp.where(first, mine, other) if i % 2 == 0 else jnp.where(first, other, mine)
        pair = jnp.concatenate(split(queries * factor), axis=1)
        q_out[g, rows] = pair
        s = dot(score_terms(pair), keys_ref[:, keys])
        edge = jnp.where(seen, s[:, rows], NEGATIVE)
        return edge if i % 2 == 0 else jnp.concatenate([s[:, :tokens], edge], axis=1)

    def soften(i, s):
        g, rows, _ = where(i)
        peak = jnp.max(lane_max(s), axis=1, keepdims=True)
        peak_out[g, rows] = jnp.broadcast_to(peak, (tokens, HD))
        high, low, total_out[g, rows] = weigh(s, peak, jnp.zeros((tokens, HD), F32))
        return high, low

    def gather(i, terms):
        g, rows, keys = where(i)
        acc_out[g, rows] = summed(*terms, values_ref[keys])

    run(2 * group, score, soften, gather)


def term_scratch(keys):
    return [pltpu.VMEM((3 * HD, keys), BF16), pltpu.VMEM((keys, 2 * HD), BF16)]


def own_stage(me, q_soft, q_other, kv, after):
    tokens, width = q_soft.shape
    group = width // (2 * HD)
    stat = jax.ShapeDtypeStruct((group, 2 * tokens, HD), F32)
    return call(
        functools.partial(own_kernel, math.log2(math.e) / math.sqrt(HD)),
        [SMEM] + [VMEM] * 3,
        [VMEM] * 4,
        [jax.ShapeDtypeStruct((group, 2 * tokens, 2 * HD), BF16), stat, stat, stat],
        term_scratch(2 * tokens),
        after=after,
    )(me, q_soft, q_other, kv)


def later_kernel(distance, parts, heads, me_ref, kv_ref, q_ref, acc_ref, peak_ref, total_ref, acc_out, peak_out, total_out, keys_ref, values_ref):
    size = q_ref.shape[1] // parts
    chip = me_ref[0] >> 1

    def where(i):
        return heads[i // parts], slice(i % parts * size, (i % parts + 1) * size)

    def score(i):
        return dot(score_terms(q_ref[where(i)]), keys_ref[...])

    def soften(i, s):
        at = where(i)
        old = peak_ref[at]
        peak = jnp.maximum(jnp.max(lane_max(s), axis=1, keepdims=True), old)
        shrink = jnp.exp2(old - peak)
        peak_out[at] = peak
        high, low, total_out[at] = weigh(s, peak, total_ref[at] * shrink)
        return high, low, shrink

    def gather(i, terms):
        at = where(i)
        acc_out[at] = acc_ref[at] * terms[2] + summed(*terms[:2], values_ref[...])

    @pl.when(lax.bitwise_xor(chip, distance) < chip)
    def _():
        fill_terms(kv_ref, keys_ref, values_ref)
        run(parts * len(heads), score, soften, gather)


def later_stage(me, distance, heads, kv, q_terms, acc, peak, total, after, parts=4):
    return call(
        functools.partial(later_kernel, distance, parts, heads),
        [SMEM] + [VMEM] * 5,
        [VMEM] * 3,
        [jax.ShapeDtypeStruct(acc.shape, F32)] * 3,
        term_scratch(kv.shape[1]),
        alias={3: 0, 4: 1, 5: 2},
        after=after,
    )(me, kv, q_terms, acc, peak, total)


def last_kernel(distance, whose, heads, columns, me_ref, kv_ref, q_ref, acc_ref, peak_ref, total_ref, *refs):
    if columns is None:
        out_ref, keys_ref, values_ref = refs
    else:
        theirs_ref, done_ref, energy_ref, energy_other_ref, gain_ref, linear_ref = refs[:6]
        lin_hbm, soft_hbm, lin_ref, out_ref, sems, keys_ref, values_ref = refs[6:]
    group, rows, _ = q_ref.shape
    tokens = rows // 2
    core, chip = me_ref[0] & 1, me_ref[0] >> 1
    side = core if whose == "own" else 1 - core
    at = pl.ds(pl.multiple_of(side * tokens, tokens), tokens)
    copies = []

    def copy(source, target):
        copies.append(pltpu.make_async_copy(source, target, sems.at[len(copies)]))
        return copies[-1]

    def columns_of(whose, g, count):
        return pl.ds(pl.multiple_of((whose * group + g) * HD, HD), count * HD)

    if columns is not None:
        blocks = [pl.ds(n * (tokens // 4), tokens // 4) for n in range(4)]
        for block in blocks:
            to = soft_hbm.at[block, columns_of(1 - core, 0, group)]
            copy(theirs_ref.at[block], to).start()
        factor = lax.rsqrt((energy_ref[:8] + energy_other_ref[:8]) / columns + EPSILON)
        factor = factor.T[:, 0:1]
        for n, block in enumerate(blocks):
            rows = slice(n * (tokens // 4), (n + 1) * (tokens // 4))
            lin_ref[rows] = linear_ref[rows] * factor[rows] * gain_ref[...]
            copy(lin_ref.at[block], lin_hbm.at[block]).start()
        for block in blocks:
            to = soft_hbm.at[block, columns_of(core, 0, group - len(heads))]
            copy(done_ref.at[block], to).start()
        own_copies = [
            copy(out_ref.at[:, pl.ds(n * HD, HD)], soft_hbm.at[:, columns_of(core, g, 1)])
            for n, g in enumerate(heads)
        ]

    def finish(n, acc, total):
        out_ref[:, n * HD : (n + 1) * HD] = acc / jnp.sum(total, axis=1, keepdims=True)
        if columns is not None:
            own_copies[n].start()

    def score(n):
        return dot(score_terms(q_ref[heads[n], at]), keys_ref[...])

    def soften(n, s):
        old = peak_ref[heads[n], at]
        peak = jnp.maximum(jnp.max(lane_max(s), axis=1, keepdims=True), old)
        shrink = jnp.exp2(old - peak)
        return *weigh(s, peak, total_ref[heads[n], at] * shrink), shrink

    def gather(n, terms):
        high, low, total, shrink = terms
        new = summed(high, low, values_ref[...])
        finish(n, acc_ref[heads[n], at] * shrink + new, total)

    visible = lax.bitwise_xor(chip, distance) < chip

    @pl.when(visible)
    def _():
        fill_terms(kv_ref, keys_ref, values_ref)
        run(len(heads), score, soften, gather)

    @pl.when(jnp.logical_not(visible))
    def _():
        for n, g in enumerate(heads):
            finish(n, acc_ref[g, at], total_ref[g, at])

    for each in copies:
        each.wait()


def last_stage(me, distance, whose, heads, operands, after, extra=None):
    group, rows, _ = operands[1].shape
    tokens = rows // 2
    part = jax.ShapeDtypeStruct((tokens, len(heads) * HD), F32)
    scratch = term_scratch(operands[0].shape[1])
    out_shape, out_spec, columns = part, VMEM, None
    if extra is not None:
        columns, more = extra
        operands = [*operands, *more]
        linear = more[-1]
        out_shape = [
            jax.ShapeDtypeStruct(linear.shape, F32),
            jax.ShapeDtypeStruct((tokens, 2 * group * HD), F32),
        ]
        out_spec = [HBM] * 2
        scratch = [
            pltpu.VMEM(linear.shape, F32),
            pltpu.VMEM(part.shape, F32),
            pltpu.SemaphoreType.DMA((12 + len(heads),)),
        ] + scratch
    return call(
        functools.partial(last_kernel, distance, whose, heads, columns),
        [SMEM] + [VMEM] * len(operands),
        out_spec,
        out_shape,
        scratch,
        after=after,
    )(me, *operands)


def plus_kernel(a_ref, b_ref, out_ref):
    out_ref[...] = a_ref[...] + b_ref[...]


def plus(a, b, after):
    return call(
        plus_kernel, [VMEM] * 2, VMEM, jax.ShapeDtypeStruct(a.shape, F32), after=after
    )(a, b)


def copy_kernel(source_ref, out_ref):
    out_ref[...] = source_ref[...]


def copied(array, after):
    return call(copy_kernel, [VMEM], VMEM, jax.ShapeDtypeStruct(array.shape, F32), after=after)(
        array
    )


def relay_kernel(me_ref, own_ref, across_ref, out_ref):
    @pl.when((me_ref[0] & 1) == 0)
    def _():
        out_ref[...] = own_ref[...]

    @pl.when((me_ref[0] & 1) == 1)
    def _():
        out_ref[...] = across_ref[...]


def relayed(me, own, across, after):
    return call(
        relay_kernel,
        [SMEM, VMEM, VMEM],
        VMEM,
        jax.ShapeDtypeStruct(own.shape, F32),
        after=after,
    )(me, own, across)


def body(q_lin, k_lin, v_lin, log_decay, lin_gain, q_soft, k_soft, v_soft):
    chips = lax.axis_size("ctx") // 2
    heads = lax.axis_size("head")
    me = lax.axis_index("ctx")
    me_flag = me.reshape(1).astype(jnp.int32)
    assert k_soft.shape[1] == 2 * HD
    swap_pairs = [(2 * c + e, 2 * c + 1 - e) for c in range(chips) for e in range(2)]

    def swap(array):
        return lax.ppermute(array, "ctx", swap_pairs)

    def across(array, distance, wanted=lambda c, e: True):
        pairs = [
            (2 * (c ^ distance) + e, 2 * c + e)
            for c in range(chips)
            for e in range(2)
            if wanted(c, e)
        ]
        return lax.ppermute(array, "ctx", pairs)

    square = chips == 4
    kv_mine, kv_send = halves(me & 1, k_soft, v_soft)
    kv_other = swap(kv_send)
    states, sums = local_states(log_decay, k_lin, v_lin, [kv_mine])
    others = swap(states)
    kv, q_send = pair_block(me_flag, kv_mine, kv_other, q_soft, [sums])
    q_other = swap(q_send)
    total, prefix = chip_total(me_flag, states, others, [q_send]), None
    inside, terms = inside_blocks(q_lin, k_lin, v_lin, sums, [total])

    def exchanged(array, step):
        return lax.ppermute(array, "head", [(i, i ^ step) for i in range(heads)])

    def sent(distance, array):
        return across(array, distance, lambda c, e: c ^ distance < c)

    def stage(distance, heads, carried, after):
        return later_stage(
            me_flag, distance, heads, arrived[distance], q_terms, *carried, after
        )

    bits = chips.bit_length() - 1
    arrived, token = {}, inside
    if square:
        arrived[2] = sent(2, kv)
        token = copied(kv, [inside])
        arrived[1] = sent(1, token)
    else:
        for distance in range(1, chips):
            arrived[distance] = sent(distance, kv)
    q_terms, *carried = own_stage(me_flag, q_soft, q_other, kv, [token])
    group = q_terms.shape[0]
    all_heads, front, back = range(group), range(group // 2), range(group // 2, group)
    token = carried[0]
    if square:
        relay = relayed(me_flag, kv, arrived[2], [token])
        arrived[3] = lax.ppermute(relay, "ctx", [(0, 6), (2, 4), (5, 7), (7, 5)])
    for bit in range(bits):
        last = bit == bits - 1
        theirs = across(total, 1 << bit, lambda c, e: not last or c ^ (1 << bit) < c)
        prefix, total = turn(me_flag, bit, total, theirs, prefix, last, [token] + ([arrived[1]] if square and last else []))
        distance = 2 if square else bit + 1
        if not (square and last):
            carried = stage(distance, all_heads, carried, [prefix, relay] if square else [prefix])
            token = carried[0]
    prefix_other = swap(prefix)
    left = [1] if square else range(bits + 1, chips - 1)
    for distance in left[:-1]:
        carried = stage(distance, all_heads, carried, [prefix])
    carried = stage(left[-1], front, carried, [prefix])
    linear, energy = linear_blocks(
        me_flag, terms, inside, sums, prefix, prefix_other, others, [carried[0]]
    )
    energies, step = [], 1
    while step < heads:
        energies.append(step)
        step *= 2
    other = exchanged(energy, energies[0])
    carried = stage(left[-1], back, carried, [energy])
    operands = [arrived[chips - 1], q_terms, *carried]
    for step in energies[1:]:
        energy = plus(energy, other, [carried[0]])
        other = exchanged(energy, step)

    theirs = last_stage(me_flag, chips - 1, "other", all_heads, operands, [energy])
    done = last_stage(me_flag, chips - 1, "own", front, operands, [theirs])
    columns = q_lin.shape[1] * heads
    more = [swap(theirs), done, energy, other, lin_gain.reshape(1, -1), linear]
    return tuple(
        last_stage(me_flag, chips - 1, "own", back, operands, [], (columns, more))
    )


def solution(mesh):
    return jax.shard_map(
        body,
        mesh=mesh,
        in_specs=(
            P("ctx", "head"),
            P("ctx", "head"),
            P("ctx", "head"),
            P("head", "ctx"),
            P("head"),
            P("ctx", "head"),
            P("ctx", "head"),
            P("ctx", "head"),
        ),
        out_specs=(P("ctx", "head"), P("ctx", "head")),
        check_vma=False,
    )
```

```python
import functools
import math

import jax
import jax.numpy as jnp
from jax import lax
from jax.experimental import pallas as pl
from jax.experimental.pallas import tpu as pltpu
from jax.sharding import PartitionSpec as P

HD = 128
NEGATIVE = -1e30
EPSILON = 1e-05
ENERGY_ROWS = 16
HEADROOM = 60.0
F32 = jnp.float32
BF16 = jnp.bfloat16
NT = (((1,), (1,)), ((), ()))
VMEM_LIMIT = 32 * 1024 * 1024
VMEM = pl.BlockSpec(memory_space=pltpu.VMEM)
SMEM = pl.BlockSpec(memory_space=pltpu.SMEM)
ANY = pl.BlockSpec(memory_space=pl.ANY)
HBM = pl.BlockSpec(memory_space=pltpu.HBM)


def split(x):
    high = x.astype(BF16)
    low = (x - high.astype(F32)).astype(BF16)
    return high, low


def dot(a, b):
    return jnp.dot(a, b, preferred_element_type=F32)


def three_term(a, b):
    a_high, a_low = split(a)
    b_high, b_low = split(b)
    wide = dot(a_high, jnp.concatenate([b_high, b_low], axis=1))
    n = b.shape[1]
    return wide[:, :n] + wide[:, n:] + dot(a_low, b_high)


def call(kernel, in_specs, out_specs, out_shape, scratch=(), alias=None, after=()):
    count = len(in_specs)

    def ordered(*refs):
        kernel(*refs[:count], *refs[count + len(after) :])

    made = pl.pallas_call(
        ordered,
        in_specs=in_specs + [ANY] * len(after),
        out_specs=out_specs,
        out_shape=out_shape,
        scratch_shapes=list(scratch),
        input_output_aliases=alias or {},
        cost_estimate=pl.CostEstimate(flops=1, bytes_accessed=1, transcendentals=0),
        compiler_params=pltpu.CompilerParams(vmem_limit_bytes=VMEM_LIMIT),
    )
    return lambda *operands: made(*operands, *after)


def state_kernel(rate_ref, k_ref, v_ref, packed_ref, sums_ref):
    tokens = k_ref.shape[0]
    heads = rate_ref.shape[0]
    half = heads // 2
    upto = lax.broadcasted_iota(jnp.int32, (tokens, tokens), 0)
    upto = (upto <= lax.broadcasted_iota(jnp.int32, (tokens, tokens), 1)).astype(F32)
    sums = jnp.dot(
        rate_ref[...], upto, precision=lax.Precision.HIGHEST, preferred_element_type=F32
    )
    sums_ref[...] = sums
    totals = sums[:, tokens - 1 : tokens]
    trailing = jnp.exp(totals - sums)
    for side in range(2):
        packed_ref[side, half * HD :] = jnp.zeros((8, HD), F32)
    for h in range(heads):
        side, i = h // half, h % half
        at = slice(h * HD, (h + 1) * HD)
        packed_ref[side, i * HD : (i + 1) * HD] = three_term(
            k_ref[:, at].T * trailing[h : h + 1], v_ref[:, at]
        )
        packed_ref[side, half * HD + i : half * HD + i + 1] = jnp.broadcast_to(
            totals[h : h + 1], (1, HD)
        )


def local_states(rates, k_lin, v_lin, after):
    tokens = k_lin.shape[0]
    heads = rates.shape[0]
    return call(
        state_kernel,
        [VMEM] * 3,
        [VMEM] * 2,
        [
            jax.ShapeDtypeStruct((2, heads // 2 * HD + 8, HD), F32),
            jax.ShapeDtypeStruct((heads, tokens), F32),
        ],
        after=after,
    )(rates, k_lin, v_lin)


def join(half, first, second, out_ref):
    decay = jnp.exp(second[half * HD :, :])
    for i in range(half):
        at = slice(i * HD, (i + 1) * HD)
        out_ref[at] = first[at] * decay[i : i + 1] + second[at]
    out_ref[half * HD :] = first[half * HD :] + second[half * HD :]


def chip_kernel(half, me_ref, states_ref, others_ref, out_ref):
    core = me_ref[0] & 1

    @pl.when(core == 0)
    def _():
        join(half, states_ref[0], others_ref[0], out_ref)

    @pl.when(core == 1)
    def _():
        join(half, others_ref[1], states_ref[1], out_ref)


def chip_total(me, states, others, after):
    _, packed, _ = states.shape
    return call(
        functools.partial(chip_kernel, (packed - 8) // HD),
        [SMEM, VMEM, VMEM],
        VMEM,
        jax.ShapeDtypeStruct((packed, HD), F32),
        after=after,
    )(me, states, others)


def turn_kernel(half, bit, first, last, me_ref, total_ref, theirs_ref, *refs):
    refs = list(refs)
    before_ref = None if first else refs.pop(0)
    prefix_ref = refs.pop(0)
    total_out = None if last else refs.pop(0)
    late = (me_ref[0] >> (bit + 1)) & 1

    @pl.when(late == 0)
    def _():
        prefix_ref[...] = jnp.zeros_like(prefix_ref) if first else before_ref[...]
        if not last:
            join(half, total_ref[...], theirs_ref[...], total_out)

    @pl.when(late == 1)
    def _():
        if first:
            prefix_ref[...] = theirs_ref[...]
        else:
            join(half, theirs_ref[...], before_ref[...], prefix_ref)
        if not last:
            join(half, theirs_ref[...], total_ref[...], total_out)


def turn(me, bit, total, theirs, before, last, after):
    packed = total.shape[0]
    operands = [total, theirs] + ([] if before is None else [before])
    count = 1 if last else 2
    out = call(
        functools.partial(turn_kernel, (packed - 8) // HD, bit, before is None, last),
        [SMEM] + [VMEM] * len(operands),
        [VMEM] * count,
        [jax.ShapeDtypeStruct((packed, HD), F32)] * count,
        after=after,
    )(me, *operands)
    return out[0], (None if last else out[1])


def inside_kernel(q_ref, k_ref, v_ref, sums_ref, out_ref, terms_ref):
    tokens = q_ref.shape[0]
    heads = sums_ref.shape[0]
    causal = lax.broadcasted_iota(jnp.int32, (tokens, tokens), 0) >= lax.broadcasted_iota(
        jnp.int32, (tokens, tokens), 1
    )
    columns = sums_ref[...].T
    for h in range(heads):
        at = slice(h * HD, (h + 1) * HD)
        q_high, q_low = split(q_ref[:, at])
        k_high, k_low = split(k_ref[:, at])
        terms_ref[h, :, :HD] = q_high
        terms_ref[h, :, HD:] = q_low
        scores = lax.dot_general(
            jnp.concatenate([q_high, q_low, q_high], axis=1),
            jnp.concatenate([k_high, k_high, k_low], axis=1),
            NT,
            preferred_element_type=F32,
        )
        gaps = columns[:, h : h + 1] - sums_ref[h : h + 1, :]
        weights = jnp.where(causal, jnp.exp(jnp.where(causal, gaps, 0.0)), 0.0)
        out_ref[h] = three_term(scores * weights, v_ref[:, at])


def inside_blocks(q_lin, k_lin, v_lin, sums, after):
    tokens = q_lin.shape[0]
    heads = sums.shape[0]
    return call(
        inside_kernel,
        [VMEM] * 4,
        [VMEM] * 2,
        [
            jax.ShapeDtypeStruct((heads, tokens, HD), F32),
            jax.ShapeDtypeStruct((heads, tokens, 2 * HD), BF16),
        ],
        after=after,
    )(q_lin, k_lin, v_lin, sums)


def linear_kernel(me_ref, terms_ref, inside_ref, sums_ref, mine_ref, theirs_ref, other_ref, out_ref, energy_ref):
    heads, tokens, _ = inside_ref.shape
    half = heads // 2
    core = me_ref[0] & 1
    leading = jnp.exp(sums_ref[...]).T
    squares = jnp.zeros((tokens, HD), F32)
    for side in range(2):
        decay = jnp.exp(other_ref[side, half * HD :])
        for i in range(half):
            h = side * half + i
            at = slice(i * HD, (i + 1) * HD)
            prior = jnp.where(core == side, mine_ref[at], theirs_ref[at])
            prior = jnp.where(core == 1, prior * decay[i : i + 1] + other_ref[side, at], prior)
            high, low = split(prior)
            wide = dot(terms_ref[h, :, :HD], jnp.concatenate([high, low], axis=1))
            carried = wide[:, :HD] + wide[:, HD:] + dot(terms_ref[h, :, HD:], high)
            linear = inside_ref[h] + leading[:, h : h + 1] * carried
            out_ref[:, h * HD : (h + 1) * HD] = linear
            squares = squares + linear * linear
    energy_ref[...] = lax.dot_general(
        jnp.ones((energy_ref.shape[0], HD), F32),
        squares,
        NT,
        precision=lax.Precision.HIGHEST,
        preferred_element_type=F32,
    )


def linear_blocks(me, terms, inside, sums, mine, theirs, other, after):
    heads, tokens, _ = inside.shape
    return call(
        linear_kernel,
        [SMEM] + [VMEM] * 6,
        [VMEM] * 2,
        [
            jax.ShapeDtypeStruct((tokens, heads * HD), F32),
            jax.ShapeDtypeStruct((ENERGY_ROWS, tokens), F32),
        ],
        after=after,
    )(me, terms, inside, sums, mine, theirs, other)


def halves(core, *arrays):
    early = [array[:, :HD] for array in arrays]
    late = [array[:, HD:] for array in arrays]
    mine = jnp.stack([jnp.where(core == 0, a, b) for a, b in zip(early, late)])
    theirs = jnp.stack([jnp.where(core == 0, b, a) for a, b in zip(early, late)])
    return mine, theirs


def pair_kernel(me_ref, mine_ref, other_ref, q_ref, out_ref, send_ref):
    tokens = mine_ref.shape[1]
    group = send_ref.shape[0]
    core = me_ref[0] & 1
    first = core == 0
    for side in range(2):
        mine, other = mine_ref[side], other_ref[side]
        out_ref[side, :tokens] = jnp.where(first, mine, other)
        out_ref[side, tokens:] = jnp.where(first, other, mine)
    for g in range(group):
        at = pl.ds(pl.multiple_of(((1 - core) * group + g) * HD, HD), HD)
        send_ref[g] = q_ref[:, at]


def pair_block(me, mine, other, q_soft, after):
    _, tokens, _ = mine.shape
    group = q_soft.shape[1] // (2 * HD)
    return call(
        pair_kernel,
        [SMEM] + [VMEM] * 3,
        [VMEM] * 2,
        [
            jax.ShapeDtypeStruct((2, 2 * tokens, HD), F32),
            jax.ShapeDtypeStruct((group, tokens, HD), F32),
        ],
        after=after,
    )(me, mine, other, q_soft)


def run(count, score, soften, gather):
    scores, before = score(0), None
    for i in range(count):
        following = score(i + 1) if i + 1 < count else None
        if before is not None:
            gather(i - 1, before)
        before = soften(i, scores)
        scores = following
    gather(count - 1, before)


def fill_terms(kv_ref, keys_ref, values_ref):
    keys = kv_ref[0].T
    k_high, k_low = split(keys)
    keys_ref[:HD] = k_high
    keys_ref[HD : 2 * HD] = k_high
    keys_ref[2 * HD :] = k_low
    v_high, v_low = split(kv_ref[1])
    values_ref[:, :HD] = v_high
    values_ref[:, HD:] = v_low
    return keys


def bounded(keys, limit_ref):
    longest = jnp.max(jnp.sum(keys * keys, axis=0, keepdims=True)) * jnp.max(limit_ref[0:1])
    room = jnp.max(limit_ref[1:2])
    return jnp.logical_and(room > 0.0, longest <= room * room)


def lane_max(array):
    peak = array[:, :HD]
    for c in range(1, array.shape[1] // HD):
        peak = jnp.maximum(peak, array[:, c * HD : (c + 1) * HD])
    return peak


def score_terms(pair):
    return jnp.concatenate([pair, pair[:, :HD]], axis=1)


def weigh(scores, peak, total):
    high, low = [], []
    for c in range(scores.shape[1] // HD):
        w = jnp.exp2(scores[:, c * HD : (c + 1) * HD] - peak)
        total = total + w
        pair = split(w)
        high.append(pair[0])
        low.append(pair[1])
    return jnp.concatenate(high, axis=1), jnp.concatenate(low, axis=1), total


def summed(high, low, values):
    wide = dot(high, values)
    return wide[:, :HD] + wide[:, HD:] + dot(low, values[:, :HD])


def own_kernel(factor, me_ref, q_ref, q_other_ref, kv_ref, q_out, acc_out, peak_out, total_out, limit_ref, keys_ref, values_ref):
    group, tokens = q_out.shape[0], q_ref.shape[0]
    core = me_ref[0] & 1
    first = core == 0
    fill_terms(kv_ref, keys_ref, values_ref)
    seen = lax.broadcasted_iota(jnp.int32, (tokens, tokens), 1)
    seen = seen <= lax.broadcasted_iota(jnp.int32, (tokens, tokens), 0)

    def where(i):
        t = i % 2
        return i // 2, slice(t * tokens, (t + 1) * tokens), slice(0, (t + 1) * tokens)

    def score(i):
        g, rows, keys = where(i)
        at = pl.ds(pl.multiple_of((core * group + g) * HD, HD), HD)
        mine, other = q_ref[:, at], q_other_ref[g]
        queries = jnp.where(first, mine, other) if i % 2 == 0 else jnp.where(first, other, mine)
        queries = queries * factor
        lengths.append(jnp.sum(queries * queries, axis=1, keepdims=True))
        pair = jnp.concatenate(split(queries), axis=1)
        q_out[g, rows] = pair
        s = dot(score_terms(pair), keys_ref[:, keys])
        edge = jnp.where(seen, s[:, rows], NEGATIVE)
        return edge if i % 2 == 0 else jnp.concatenate([s[:, :tokens], edge], axis=1)

    def soften(i, s):
        g, rows, _ = where(i)
        peak = jnp.max(lane_max(s), axis=1, keepdims=True)
        lowest.append(peak)
        peak_out[g, rows] = jnp.broadcast_to(peak, (tokens, HD))
        high, low, total_out[g, rows] = weigh(s, peak, jnp.zeros((tokens, HD), F32))
        return high, low

    def gather(i, terms):
        g, rows, keys = where(i)
        acc_out[g, rows] = summed(*terms, values_ref[keys])

    lengths, lowest = [], []
    run(2 * group, score, soften, gather)
    longest = jnp.max(functools.reduce(jnp.maximum, lengths))
    room = HEADROOM + jnp.min(functools.reduce(jnp.minimum, lowest))
    row = lax.broadcasted_iota(jnp.int32, limit_ref.shape, 0)
    limit_ref[...] = jnp.where(row == 0, longest, room)


def term_scratch(keys):
    return [pltpu.VMEM((3 * HD, keys), BF16), pltpu.VMEM((keys, 2 * HD), BF16)]


def own_stage(me, q_soft, q_other, kv, after):
    tokens, width = q_soft.shape
    group = width // (2 * HD)
    stat = jax.ShapeDtypeStruct((group, 2 * tokens, HD), F32)
    return call(
        functools.partial(own_kernel, math.log2(math.e) / math.sqrt(HD)),
        [SMEM] + [VMEM] * 3,
        [VMEM] * 5,
        [
            jax.ShapeDtypeStruct((group, 2 * tokens, 2 * HD), BF16),
            stat,
            stat,
            stat,
            jax.ShapeDtypeStruct((8, HD), F32),
        ],
        term_scratch(2 * tokens),
        after=after,
    )(me, q_soft, q_other, kv)


def later_kernel(distance, parts, heads, me_ref, kv_ref, q_ref, acc_ref, peak_ref, total_ref, limit_ref, acc_out, peak_out, total_out, keys_ref, values_ref):
    size = q_ref.shape[1] // parts
    chip = me_ref[0] >> 1

    def where(i):
        return heads[i // parts], slice(i % parts * size, (i % parts + 1) * size)

    def score(i):
        return dot(score_terms(q_ref[where(i)]), keys_ref[...])

    def soften(i, s):
        at = where(i)
        old = peak_ref[at]
        peak = jnp.maximum(jnp.max(lane_max(s), axis=1, keepdims=True), old)
        shrink = jnp.exp2(old - peak)
        peak_out[at] = peak
        high, low, total_out[at] = weigh(s, peak, total_ref[at] * shrink)
        return high, low, shrink

    def gather(i, terms):
        at = where(i)
        acc_out[at] = acc_ref[at] * terms[2] + summed(*terms[:2], values_ref[...])

    def soften_same(i, s):
        at = where(i)
        high, low, total_out[at] = weigh(s, peak_ref[at], total_ref[at])
        return high, low

    def gather_same(i, terms):
        at = where(i)
        acc_out[at] = acc_ref[at] + summed(*terms, values_ref[...])

    @pl.when(lax.bitwise_xor(chip, distance) < chip)
    def _():
        same = bounded(fill_terms(kv_ref, keys_ref, values_ref), limit_ref)

        @pl.when(same)
        def _():
            run(parts * len(heads), score, soften_same, gather_same)

        @pl.when(jnp.logical_not(same))
        def _():
            run(parts * len(heads), score, soften, gather)


def later_stage(me, distance, heads, kv, q_terms, acc, peak, total, limit, after, parts=4):
    return call(
        functools.partial(later_kernel, distance, parts, heads),
        [SMEM] + [VMEM] * 6,
        [VMEM] * 3,
        [jax.ShapeDtypeStruct(acc.shape, F32)] * 3,
        term_scratch(kv.shape[1]),
        alias={3: 0, 4: 1, 5: 2},
        after=after,
    )(me, kv, q_terms, acc, peak, total, limit)


def last_kernel(distance, whose, heads, columns, me_ref, kv_ref, q_ref, acc_ref, peak_ref, total_ref, limit_ref, *refs):
    if columns is None:
        out_ref, keys_ref, values_ref = refs
    else:
        theirs_ref, done_ref, energy_ref, energy_other_ref, gain_ref, linear_ref = refs[:6]
        lin_hbm, soft_hbm, lin_ref, out_ref, sems, keys_ref, values_ref = refs[6:]
    group, rows, _ = q_ref.shape
    tokens = rows // 2
    core, chip = me_ref[0] & 1, me_ref[0] >> 1
    side = core if whose == "own" else 1 - core
    at = pl.ds(pl.multiple_of(side * tokens, tokens), tokens)
    copies = []

    def copy(source, target):
        copies.append(pltpu.make_async_copy(source, target, sems.at[len(copies)]))
        return copies[-1]

    def columns_of(whose, g, count):
        return pl.ds(pl.multiple_of((whose * group + g) * HD, HD), count * HD)

    if columns is not None:
        blocks = [pl.ds(n * (tokens // 4), tokens // 4) for n in range(4)]
        for block in blocks:
            to = soft_hbm.at[block, columns_of(1 - core, 0, group)]
            copy(theirs_ref.at[block], to).start()
        factor = lax.rsqrt((energy_ref[:8] + energy_other_ref[:8]) / columns + EPSILON)
        factor = factor.T[:, 0:1]
        for n, block in enumerate(blocks):
            rows = slice(n * (tokens // 4), (n + 1) * (tokens // 4))
            lin_ref[rows] = linear_ref[rows] * factor[rows] * gain_ref[...]
            copy(lin_ref.at[block], lin_hbm.at[block]).start()
        for block in blocks:
            to = soft_hbm.at[block, columns_of(core, 0, group - len(heads))]
            copy(done_ref.at[block], to).start()
        own_copies = [
            copy(out_ref.at[:, pl.ds(n * HD, HD)], soft_hbm.at[:, columns_of(core, g, 1)])
            for n, g in enumerate(heads)
        ]

    def finish(n, acc, total):
        out_ref[:, n * HD : (n + 1) * HD] = acc / jnp.sum(total, axis=1, keepdims=True)
        if columns is not None:
            own_copies[n].start()

    def score(n):
        return dot(score_terms(q_ref[heads[n], at]), keys_ref[...])

    def soften(n, s):
        old = peak_ref[heads[n], at]
        peak = jnp.maximum(jnp.max(lane_max(s), axis=1, keepdims=True), old)
        shrink = jnp.exp2(old - peak)
        return *weigh(s, peak, total_ref[heads[n], at] * shrink), shrink

    def gather(n, terms):
        high, low, total, shrink = terms
        new = summed(high, low, values_ref[...])
        finish(n, acc_ref[heads[n], at] * shrink + new, total)

    def soften_same(n, s):
        return weigh(s, peak_ref[heads[n], at], total_ref[heads[n], at])

    def gather_same(n, terms):
        high, low, total = terms
        finish(n, acc_ref[heads[n], at] + summed(high, low, values_ref[...]), total)

    visible = lax.bitwise_xor(chip, distance) < chip

    @pl.when(visible)
    def _():
        same = bounded(fill_terms(kv_ref, keys_ref, values_ref), limit_ref)

        @pl.when(same)
        def _():
            run(len(heads), score, soften_same, gather_same)

        @pl.when(jnp.logical_not(same))
        def _():
            run(len(heads), score, soften, gather)

    @pl.when(jnp.logical_not(visible))
    def _():
        for n, g in enumerate(heads):
            finish(n, acc_ref[g, at], total_ref[g, at])

    for each in copies:
        each.wait()


def last_stage(me, distance, whose, heads, operands, after, extra=None):
    group, rows, _ = operands[1].shape
    tokens = rows // 2
    part = jax.ShapeDtypeStruct((tokens, len(heads) * HD), F32)
    scratch = term_scratch(operands[0].shape[1])
    out_shape, out_spec, columns = part, VMEM, None
    if extra is not None:
        columns, more = extra
        operands = [*operands, *more]
        linear = more[-1]
        out_shape = [
            jax.ShapeDtypeStruct(linear.shape, F32),
            jax.ShapeDtypeStruct((tokens, 2 * group * HD), F32),
        ]
        out_spec = [HBM] * 2
        scratch = [
            pltpu.VMEM(linear.shape, F32),
            pltpu.VMEM(part.shape, F32),
            pltpu.SemaphoreType.DMA((12 + len(heads),)),
        ] + scratch
    return call(
        functools.partial(last_kernel, distance, whose, heads, columns),
        [SMEM] + [VMEM] * len(operands),
        out_spec,
        out_shape,
        scratch,
        after=after,
    )(me, *operands)


def plus_kernel(a_ref, b_ref, out_ref):
    out_ref[...] = a_ref[...] + b_ref[...]


def plus(a, b, after):
    return call(
        plus_kernel, [VMEM] * 2, VMEM, jax.ShapeDtypeStruct(a.shape, F32), after=after
    )(a, b)


def copy_kernel(source_ref, out_ref):
    out_ref[...] = source_ref[...]


def copied(array, after):
    return call(copy_kernel, [VMEM], VMEM, jax.ShapeDtypeStruct(array.shape, F32), after=after)(
        array
    )


def relay_kernel(me_ref, own_ref, across_ref, out_ref):
    @pl.when((me_ref[0] & 1) == 0)
    def _():
        out_ref[...] = own_ref[...]

    @pl.when((me_ref[0] & 1) == 1)
    def _():
        out_ref[...] = across_ref[...]


def relayed(me, own, across, after):
    return call(
        relay_kernel,
        [SMEM, VMEM, VMEM],
        VMEM,
        jax.ShapeDtypeStruct(own.shape, F32),
        after=after,
    )(me, own, across)


def body(q_lin, k_lin, v_lin, log_decay, lin_gain, q_soft, k_soft, v_soft):
    chips = lax.axis_size("ctx") // 2
    heads = lax.axis_size("head")
    me = lax.axis_index("ctx")
    me_flag = me.reshape(1).astype(jnp.int32)
    assert k_soft.shape[1] == 2 * HD
    swap_pairs = [(2 * c + e, 2 * c + 1 - e) for c in range(chips) for e in range(2)]

    def swap(array):
        return lax.ppermute(array, "ctx", swap_pairs)

    def across(array, distance, wanted=lambda c, e: True):
        pairs = [
            (2 * (c ^ distance) + e, 2 * c + e)
            for c in range(chips)
            for e in range(2)
            if wanted(c, e)
        ]
        return lax.ppermute(array, "ctx", pairs)

    square = chips == 4
    kv_mine, kv_send = halves(me & 1, k_soft, v_soft)
    kv_other = swap(kv_send)
    states, sums = local_states(log_decay, k_lin, v_lin, [kv_mine])
    others = swap(states)
    kv, q_send = pair_block(me_flag, kv_mine, kv_other, q_soft, [sums])
    q_other = swap(q_send)
    total, prefix = chip_total(me_flag, states, others, [q_send]), None
    inside, terms = inside_blocks(q_lin, k_lin, v_lin, sums, [total])

    def exchanged(array, step):
        return lax.ppermute(array, "head", [(i, i ^ step) for i in range(heads)])

    def sent(distance, array):
        return across(array, distance, lambda c, e: c ^ distance < c)

    def stage(distance, heads, carried, after):
        return later_stage(
            me_flag, distance, heads, arrived[distance], q_terms, *carried, limit, after
        )

    bits = chips.bit_length() - 1
    arrived, token = {}, inside
    if square:
        arrived[2] = sent(2, kv)
        token = copied(kv, [inside])
        arrived[1] = sent(1, token)
    else:
        for distance in range(1, chips):
            arrived[distance] = sent(distance, kv)
    q_terms, *carried, limit = own_stage(me_flag, q_soft, q_other, kv, [token])
    group = q_terms.shape[0]
    all_heads, front, back = range(group), range(group // 2), range(group // 2, group)
    token = carried[0]
    if square:
        relay = relayed(me_flag, kv, arrived[2], [token])
        arrived[3] = lax.ppermute(relay, "ctx", [(0, 6), (2, 4), (5, 7), (7, 5)])
    for bit in range(bits):
        last = bit == bits - 1
        theirs = across(total, 1 << bit, lambda c, e: not last or c ^ (1 << bit) < c)
        prefix, total = turn(me_flag, bit, total, theirs, prefix, last, [token] + ([arrived[1]] if square and last else []))
        distance = 2 if square else bit + 1
        if not (square and last):
            carried = stage(distance, all_heads, carried, [prefix, relay] if square else [prefix])
            token = carried[0]
    prefix_other = swap(prefix)
    left = [1] if square else range(bits + 1, chips - 1)
    for distance in left[:-1]:
        carried = stage(distance, all_heads, carried, [prefix])
    carried = stage(left[-1], front, carried, [prefix])
    linear, energy = linear_blocks(
        me_flag, terms, inside, sums, prefix, prefix_other, others, [carried[0]]
    )
    energies, step = [], 1
    while step < heads:
        energies.append(step)
        step *= 2
    other = exchanged(energy, energies[0])
    carried = stage(left[-1], back, carried, [energy])
    operands = [arrived[chips - 1], q_terms, *carried, limit]
    for step in energies[1:]:
        energy = plus(energy, other, [carried[0]])
        other = exchanged(energy, step)

    theirs = last_stage(me_flag, chips - 1, "other", all_heads, operands, [energy])
    done = last_stage(me_flag, chips - 1, "own", front, operands, [theirs])
    columns = q_lin.shape[1] * heads
    more = [swap(theirs), done, energy, other, lin_gain.reshape(1, -1), linear]
    return tuple(
        last_stage(me_flag, chips - 1, "own", back, operands, [], (columns, more))
    )


def solution(mesh):
    return jax.shard_map(
        body,
        mesh=mesh,
        in_specs=(
            P("ctx", "head"),
            P("ctx", "head"),
            P("ctx", "head"),
            P("head", "ctx"),
            P("head"),
            P("ctx", "head"),
            P("ctx", "head"),
            P("ctx", "head"),
        ),
        out_specs=(P("ctx", "head"), P("ctx", "head")),
        check_vma=False,
    )
```

```python
import functools
import math

import jax
import jax.numpy as jnp
from jax import lax
from jax.experimental import pallas as pl
from jax.experimental.pallas import tpu as pltpu
from jax.sharding import PartitionSpec as P

HD = 128
NEGATIVE = -1e30
EPSILON = 1e-05
ENERGY_ROWS = 16
F32 = jnp.float32
BF16 = jnp.bfloat16
NT = (((1,), (1,)), ((), ()))
VMEM_LIMIT = 32 * 1024 * 1024
VMEM = pl.BlockSpec(memory_space=pltpu.VMEM)
SMEM = pl.BlockSpec(memory_space=pltpu.SMEM)
ANY = pl.BlockSpec(memory_space=pl.ANY)
HBM = pl.BlockSpec(memory_space=pltpu.HBM)


def split(x):
    high = x.astype(BF16)
    low = (x - high.astype(F32)).astype(BF16)
    return high, low


def dot(a, b):
    return jnp.dot(a, b, preferred_element_type=F32)


def three_term(a, b):
    a_high, a_low = split(a)
    b_high, b_low = split(b)
    wide = dot(a_high, jnp.concatenate([b_high, b_low], axis=1))
    n = b.shape[1]
    return wide[:, :n] + wide[:, n:] + dot(a_low, b_high)


def call(kernel, in_specs, out_specs, out_shape, scratch=(), alias=None, after=()):
    count = len(in_specs)

    def ordered(*refs):
        kernel(*refs[:count], *refs[count + len(after) :])

    made = pl.pallas_call(
        ordered,
        in_specs=in_specs + [ANY] * len(after),
        out_specs=out_specs,
        out_shape=out_shape,
        scratch_shapes=list(scratch),
        input_output_aliases=alias or {},
        cost_estimate=pl.CostEstimate(flops=1, bytes_accessed=1, transcendentals=0),
        compiler_params=pltpu.CompilerParams(vmem_limit_bytes=VMEM_LIMIT),
    )
    return lambda *operands: made(*operands, *after)


def state_kernel(rate_ref, k_ref, v_ref, packed_ref, sums_ref):
    tokens = k_ref.shape[0]
    heads = rate_ref.shape[0]
    half = heads // 2
    upto = lax.broadcasted_iota(jnp.int32, (tokens, tokens), 0)
    upto = (upto <= lax.broadcasted_iota(jnp.int32, (tokens, tokens), 1)).astype(F32)
    sums = jnp.dot(
        rate_ref[...], upto, precision=lax.Precision.HIGHEST, preferred_element_type=F32
    )
    sums_ref[...] = sums
    totals = sums[:, tokens - 1 : tokens]
    trailing = jnp.exp(totals - sums)
    for side in range(2):
        packed_ref[side, half * HD :] = jnp.zeros((8, HD), F32)
    for h in range(heads):
        side, i = h // half, h % half
        at = slice(h * HD, (h + 1) * HD)
        packed_ref[side, i * HD : (i + 1) * HD] = three_term(
            k_ref[:, at].T * trailing[h : h + 1], v_ref[:, at]
        )
        packed_ref[side, half * HD + i : half * HD + i + 1] = jnp.broadcast_to(
            totals[h : h + 1], (1, HD)
        )


def local_states(rates, k_lin, v_lin, after):
    tokens = k_lin.shape[0]
    heads = rates.shape[0]
    return call(
        state_kernel,
        [VMEM] * 3,
        [VMEM] * 2,
        [
            jax.ShapeDtypeStruct((2, heads // 2 * HD + 8, HD), F32),
            jax.ShapeDtypeStruct((heads, tokens), F32),
        ],
        after=after,
    )(rates, k_lin, v_lin)


def join(half, first, second, out_ref):
    decay = jnp.exp(second[half * HD :, :])
    for i in range(half):
        at = slice(i * HD, (i + 1) * HD)
        out_ref[at] = first[at] * decay[i : i + 1] + second[at]
    out_ref[half * HD :] = first[half * HD :] + second[half * HD :]


def chip_kernel(half, me_ref, states_ref, others_ref, out_ref):
    core = me_ref[0] & 1

    @pl.when(core == 0)
    def _():
        join(half, states_ref[0], others_ref[0], out_ref)

    @pl.when(core == 1)
    def _():
        join(half, others_ref[1], states_ref[1], out_ref)


def chip_total(me, states, others, after):
    _, packed, _ = states.shape
    return call(
        functools.partial(chip_kernel, (packed - 8) // HD),
        [SMEM, VMEM, VMEM],
        VMEM,
        jax.ShapeDtypeStruct((packed, HD), F32),
        after=after,
    )(me, states, others)


def turn_kernel(half, bit, first, last, me_ref, total_ref, theirs_ref, *refs):
    refs = list(refs)
    before_ref = None if first else refs.pop(0)
    prefix_ref = refs.pop(0)
    total_out = None if last else refs.pop(0)
    late = (me_ref[0] >> (bit + 1)) & 1

    @pl.when(late == 0)
    def _():
        prefix_ref[...] = jnp.zeros_like(prefix_ref) if first else before_ref[...]
        if not last:
            join(half, total_ref[...], theirs_ref[...], total_out)

    @pl.when(late == 1)
    def _():
        if first:
            prefix_ref[...] = theirs_ref[...]
        else:
            join(half, theirs_ref[...], before_ref[...], prefix_ref)
        if not last:
            join(half, theirs_ref[...], total_ref[...], total_out)


def turn(me, bit, total, theirs, before, last, after):
    packed = total.shape[0]
    operands = [total, theirs] + ([] if before is None else [before])
    count = 1 if last else 2
    out = call(
        functools.partial(turn_kernel, (packed - 8) // HD, bit, before is None, last),
        [SMEM] + [VMEM] * len(operands),
        [VMEM] * count,
        [jax.ShapeDtypeStruct((packed, HD), F32)] * count,
        after=after,
    )(me, *operands)
    return out[0], (None if last else out[1])


def inside_kernel(q_ref, k_ref, v_ref, sums_ref, out_ref, terms_ref):
    tokens = q_ref.shape[0]
    heads = sums_ref.shape[0]
    causal = lax.broadcasted_iota(jnp.int32, (tokens, tokens), 0) >= lax.broadcasted_iota(
        jnp.int32, (tokens, tokens), 1
    )
    columns = sums_ref[...].T
    for h in range(heads):
        at = slice(h * HD, (h + 1) * HD)
        q_high, q_low = split(q_ref[:, at])
        k_high, k_low = split(k_ref[:, at])
        terms_ref[h, :, :HD] = q_high
        terms_ref[h, :, HD:] = q_low
        scores = lax.dot_general(
            jnp.concatenate([q_high, q_low, q_high], axis=1),
            jnp.concatenate([k_high, k_high, k_low], axis=1),
            NT,
            preferred_element_type=F32,
        )
        gaps = columns[:, h : h + 1] - sums_ref[h : h + 1, :]
        weights = jnp.where(causal, jnp.exp(jnp.where(causal, gaps, 0.0)), 0.0)
        out_ref[h] = three_term(scores * weights, v_ref[:, at])


def inside_blocks(q_lin, k_lin, v_lin, sums, after):
    tokens = q_lin.shape[0]
    heads = sums.shape[0]
    return call(
        inside_kernel,
        [VMEM] * 4,
        [VMEM] * 2,
        [
            jax.ShapeDtypeStruct((heads, tokens, HD), F32),
            jax.ShapeDtypeStruct((heads, tokens, 2 * HD), BF16),
        ],
        after=after,
    )(q_lin, k_lin, v_lin, sums)


def linear_kernel(me_ref, terms_ref, inside_ref, sums_ref, mine_ref, theirs_ref, other_ref, out_ref, energy_ref):
    heads, tokens, _ = inside_ref.shape
    half = heads // 2
    core = me_ref[0] & 1
    leading = jnp.exp(sums_ref[...]).T
    squares = jnp.zeros((tokens, HD), F32)
    for side in range(2):
        decay = jnp.exp(other_ref[side, half * HD :])
        for i in range(half):
            h = side * half + i
            at = slice(i * HD, (i + 1) * HD)
            prior = jnp.where(core == side, mine_ref[at], theirs_ref[at])
            prior = jnp.where(core == 1, prior * decay[i : i + 1] + other_ref[side, at], prior)
            high, low = split(prior)
            wide = dot(terms_ref[h, :, :HD], jnp.concatenate([high, low], axis=1))
            carried = wide[:, :HD] + wide[:, HD:] + dot(terms_ref[h, :, HD:], high)
            linear = inside_ref[h] + leading[:, h : h + 1] * carried
            out_ref[:, h * HD : (h + 1) * HD] = linear
            squares = squares + linear * linear
    energy_ref[...] = lax.dot_general(
        jnp.ones((energy_ref.shape[0], HD), F32),
        squares,
        NT,
        precision=lax.Precision.HIGHEST,
        preferred_element_type=F32,
    )


def linear_blocks(me, terms, inside, sums, mine, theirs, other, after):
    heads, tokens, _ = inside.shape
    return call(
        linear_kernel,
        [SMEM] + [VMEM] * 6,
        [VMEM] * 2,
        [
            jax.ShapeDtypeStruct((tokens, heads * HD), F32),
            jax.ShapeDtypeStruct((ENERGY_ROWS, tokens), F32),
        ],
        after=after,
    )(me, terms, inside, sums, mine, theirs, other)


def halves(core, *arrays):
    early = [array[:, :HD] for array in arrays]
    late = [array[:, HD:] for array in arrays]
    mine = jnp.stack([jnp.where(core == 0, a, b) for a, b in zip(early, late)])
    theirs = jnp.stack([jnp.where(core == 0, b, a) for a, b in zip(early, late)])
    return mine, theirs


def pair_kernel(me_ref, mine_ref, other_ref, q_ref, early_ref, late_ref, send_ref):
    group = send_ref.shape[0]
    core = me_ref[0] & 1
    first = core == 0
    mine, other = mine_ref[...], other_ref[...]
    early_ref[...] = jnp.where(first, mine, other)
    late_ref[...] = jnp.where(first, other, mine)
    for g in range(group):
        at = pl.ds(pl.multiple_of(((1 - core) * group + g) * HD, HD), HD)
        send_ref[g] = q_ref[:, at]


def pair_block(me, mine, other, q_soft, after):
    tokens, width = q_soft.shape
    return call(
        pair_kernel,
        [SMEM] + [VMEM] * 3,
        [VMEM] * 3,
        [
            jax.ShapeDtypeStruct(mine.shape, F32),
            jax.ShapeDtypeStruct(mine.shape, F32),
            jax.ShapeDtypeStruct((width // (2 * HD), tokens, HD), F32),
        ],
        after=after,
    )(me, mine, other, q_soft)


def run(count, score, soften, gather):
    scores, before = score(0), None
    for i in range(count):
        following = score(i + 1) if i + 1 < count else None
        if before is not None:
            gather(i - 1, before)
        before = soften(i, scores)
        scores = following
    gather(count - 1, before)


def fill_terms(kv_refs, keys_ref, values_ref):
    start = 0
    for kv_ref in kv_refs:
        at = slice(start, start + kv_ref.shape[1])
        start = at.stop
        k_high, k_low = split(kv_ref[0].T)
        keys_ref[:HD, at] = k_high
        keys_ref[HD : 2 * HD, at] = k_high
        keys_ref[2 * HD :, at] = k_low
        v_high, v_low = split(kv_ref[1])
        values_ref[at, :HD] = v_high
        values_ref[at, HD:] = v_low


def lane_max(array):
    peak = array[:, :HD]
    for c in range(1, array.shape[1] // HD):
        peak = jnp.maximum(peak, array[:, c * HD : (c + 1) * HD])
    return peak


def score_terms(pair):
    return jnp.concatenate([pair, pair[:, :HD]], axis=1)


def weigh(scores, peak, total):
    high, low = [], []
    for c in range(scores.shape[1] // HD):
        w = jnp.exp2(scores[:, c * HD : (c + 1) * HD] - peak)
        total = total + w
        pair = split(w)
        high.append(pair[0])
        low.append(pair[1])
    return jnp.concatenate(high, axis=1), jnp.concatenate(low, axis=1), total


def summed(high, low, values):
    wide = dot(high, values)
    return wide[:, :HD] + wide[:, HD:] + dot(low, values[:, :HD])


def own_kernel(factor, me_ref, q_ref, q_other_ref, early_ref, late_ref, q_out, acc_out, peak_out, total_out, keys_ref, values_ref):
    group, tokens = q_out.shape[0], q_ref.shape[0]
    core = me_ref[0] & 1
    first = core == 0
    fill_terms([early_ref, late_ref], keys_ref, values_ref)
    seen = lax.broadcasted_iota(jnp.int32, (tokens, tokens), 1)
    seen = seen <= lax.broadcasted_iota(jnp.int32, (tokens, tokens), 0)

    def where(i):
        t = i % 2
        return i // 2, slice(t * tokens, (t + 1) * tokens), slice(0, (t + 1) * tokens)

    def score(i):
        g, rows, keys = where(i)
        at = pl.ds(pl.multiple_of((core * group + g) * HD, HD), HD)
        mine, other = q_ref[:, at], q_other_ref[g]
        queries = jnp.where(first, mine, other) if i % 2 == 0 else jnp.where(first, other, mine)
        pair = jnp.concatenate(split(queries * factor), axis=1)
        q_out[g, rows] = pair
        s = dot(score_terms(pair), keys_ref[:, keys])
        edge = jnp.where(seen, s[:, rows], NEGATIVE)
        return edge if i % 2 == 0 else jnp.concatenate([s[:, :tokens], edge], axis=1)

    def soften(i, s):
        g, rows, _ = where(i)
        peak = jnp.max(lane_max(s), axis=1, keepdims=True)
        peak_out[g, rows] = jnp.broadcast_to(peak, (tokens, HD))
        high, low, total_out[g, rows] = weigh(s, peak, jnp.zeros((tokens, HD), F32))
        return high, low

    def gather(i, terms):
        g, rows, keys = where(i)
        acc_out[g, rows] = summed(*terms, values_ref[keys])

    run(2 * group, score, soften, gather)


def term_scratch(keys):
    return [pltpu.VMEM((3 * HD, keys), BF16), pltpu.VMEM((keys, 2 * HD), BF16)]


def own_stage(me, q_soft, q_other, early, late, after):
    tokens, width = q_soft.shape
    group = width // (2 * HD)
    stat = jax.ShapeDtypeStruct((group, 2 * tokens, HD), F32)
    return call(
        functools.partial(own_kernel, math.log2(math.e) / math.sqrt(HD)),
        [SMEM] + [VMEM] * 4,
        [VMEM] * 4,
        [jax.ShapeDtypeStruct((group, 2 * tokens, 2 * HD), BF16), stat, stat, stat],
        term_scratch(2 * tokens),
        after=after,
    )(me, q_soft, q_other, early, late)


def later_kernel(distance, parts, heads, me_ref, kv_ref, q_ref, acc_ref, peak_ref, total_ref, acc_out, peak_out, total_out, keys_ref, values_ref):
    size = q_ref.shape[1] // parts
    chip = me_ref[0] >> 1

    def where(i):
        return heads[i // parts], slice(i % parts * size, (i % parts + 1) * size)

    def score(i):
        return dot(score_terms(q_ref[where(i)]), keys_ref[...])

    def soften(i, s):
        at = where(i)
        old = peak_ref[at]
        peak = jnp.maximum(jnp.max(lane_max(s), axis=1, keepdims=True), old)
        shrink = jnp.exp2(old - peak)
        peak_out[at] = peak
        high, low, total_out[at] = weigh(s, peak, total_ref[at] * shrink)
        return high, low, shrink

    def gather(i, terms):
        at = where(i)
        acc_out[at] = acc_ref[at] * terms[2] + summed(*terms[:2], values_ref[...])

    @pl.when(lax.bitwise_xor(chip, distance) < chip)
    def _():
        fill_terms([kv_ref], keys_ref, values_ref)
        run(parts * len(heads), score, soften, gather)


def later_stage(me, distance, heads, kv, q_terms, acc, peak, total, after, parts=4):
    return call(
        functools.partial(later_kernel, distance, parts, heads),
        [SMEM] + [VMEM] * 5,
        [VMEM] * 3,
        [jax.ShapeDtypeStruct(acc.shape, F32)] * 3,
        term_scratch(kv.shape[1]),
        alias={3: 0, 4: 1, 5: 2},
        after=after,
    )(me, kv, q_terms, acc, peak, total)


def last_kernel(distance, whose, heads, columns, me_ref, kv_ref, q_ref, acc_ref, peak_ref, total_ref, *refs):
    if columns is None:
        out_ref, keys_ref, values_ref = refs
    else:
        theirs_ref, done_ref, energy_ref, energy_other_ref, gain_ref, linear_ref = refs[:6]
        lin_hbm, soft_hbm, lin_ref, out_ref, sems, keys_ref, values_ref = refs[6:]
    group, rows, _ = q_ref.shape
    tokens = rows // 2
    core, chip = me_ref[0] & 1, me_ref[0] >> 1
    side = core if whose == "own" else 1 - core
    at = pl.ds(pl.multiple_of(side * tokens, tokens), tokens)
    copies = []

    def copy(source, target):
        copies.append(pltpu.make_async_copy(source, target, sems.at[len(copies)]))
        return copies[-1]

    def columns_of(whose, g, count):
        return pl.ds(pl.multiple_of((whose * group + g) * HD, HD), count * HD)

    if columns is not None:
        blocks = [pl.ds(n * (tokens // 4), tokens // 4) for n in range(4)]
        for block in blocks:
            to = soft_hbm.at[block, columns_of(1 - core, 0, group)]
            copy(theirs_ref.at[block], to).start()
        factor = lax.rsqrt((energy_ref[:8] + energy_other_ref[:8]) / columns + EPSILON)
        factor = factor.T[:, 0:1]
        for n, block in enumerate(blocks):
            rows = slice(n * (tokens // 4), (n + 1) * (tokens // 4))
            lin_ref[rows] = linear_ref[rows] * factor[rows] * gain_ref[...]
            copy(lin_ref.at[block], lin_hbm.at[block]).start()
        for block in blocks:
            to = soft_hbm.at[block, columns_of(core, 0, group - len(heads))]
            copy(done_ref.at[block], to).start()
        own_copies = [
            copy(out_ref.at[:, pl.ds(n * HD, HD)], soft_hbm.at[:, columns_of(core, g, 1)])
            for n, g in enumerate(heads)
        ]

    def finish(n, acc, total):
        out_ref[:, n * HD : (n + 1) * HD] = acc / jnp.sum(total, axis=1, keepdims=True)
        if columns is not None:
            own_copies[n].start()

    def score(n):
        return dot(score_terms(q_ref[heads[n], at]), keys_ref[...])

    def soften(n, s):
        old = peak_ref[heads[n], at]
        peak = jnp.maximum(jnp.max(lane_max(s), axis=1, keepdims=True), old)
        shrink = jnp.exp2(old - peak)
        return *weigh(s, peak, total_ref[heads[n], at] * shrink), shrink

    def gather(n, terms):
        high, low, total, shrink = terms
        new = summed(high, low, values_ref[...])
        finish(n, acc_ref[heads[n], at] * shrink + new, total)

    visible = lax.bitwise_xor(chip, distance) < chip

    @pl.when(visible)
    def _():
        fill_terms([kv_ref], keys_ref, values_ref)
        run(len(heads), score, soften, gather)

    @pl.when(jnp.logical_not(visible))
    def _():
        for n, g in enumerate(heads):
            finish(n, acc_ref[g, at], total_ref[g, at])

    for each in copies:
        each.wait()


def last_stage(me, distance, whose, heads, operands, after, extra=None):
    group, rows, _ = operands[1].shape
    tokens = rows // 2
    part = jax.ShapeDtypeStruct((tokens, len(heads) * HD), F32)
    scratch = term_scratch(operands[0].shape[1])
    out_shape, out_spec, columns = part, VMEM, None
    if extra is not None:
        columns, more = extra
        operands = [*operands, *more]
        linear = more[-1]
        out_shape = [
            jax.ShapeDtypeStruct(linear.shape, F32),
            jax.ShapeDtypeStruct((tokens, 2 * group * HD), F32),
        ]
        out_spec = [HBM] * 2
        scratch = [
            pltpu.VMEM(linear.shape, F32),
            pltpu.VMEM(part.shape, F32),
            pltpu.SemaphoreType.DMA((12 + len(heads),)),
        ] + scratch
    return call(
        functools.partial(last_kernel, distance, whose, heads, columns),
        [SMEM] + [VMEM] * len(operands),
        out_spec,
        out_shape,
        scratch,
        after=after,
    )(me, *operands)


def plus_kernel(a_ref, b_ref, out_ref):
    out_ref[...] = a_ref[...] + b_ref[...]


def plus(a, b, after):
    return call(
        plus_kernel, [VMEM] * 2, VMEM, jax.ShapeDtypeStruct(a.shape, F32), after=after
    )(a, b)


def copy_kernel(source_ref, out_ref):
    out_ref[...] = source_ref[...]


def copied(array, after):
    return call(copy_kernel, [VMEM], VMEM, jax.ShapeDtypeStruct(array.shape, F32), after=after)(
        array
    )


def relay_kernel(me_ref, early_ref, late_ref, across_early_ref, across_late_ref, out_ref):
    tokens = early_ref.shape[1]

    @pl.when((me_ref[0] & 1) == 0)
    def _():
        out_ref[:, :tokens] = early_ref[...]
        out_ref[:, tokens:] = late_ref[...]

    @pl.when((me_ref[0] & 1) == 1)
    def _():
        out_ref[:, :tokens] = across_early_ref[...]
        out_ref[:, tokens:] = across_late_ref[...]


def relayed(me, own, across, after):
    sides, tokens, _ = own[0].shape
    return call(
        relay_kernel,
        [SMEM] + [VMEM] * 4,
        VMEM,
        jax.ShapeDtypeStruct((sides, 2 * tokens, HD), F32),
        after=after,
    )(me, *own, *across)


def body(q_lin, k_lin, v_lin, log_decay, lin_gain, q_soft, k_soft, v_soft):
    chips = lax.axis_size("ctx") // 2
    heads = lax.axis_size("head")
    me = lax.axis_index("ctx")
    me_flag = me.reshape(1).astype(jnp.int32)
    assert k_soft.shape[1] == 2 * HD
    swap_pairs = [(2 * c + e, 2 * c + 1 - e) for c in range(chips) for e in range(2)]

    def swap(array):
        return lax.ppermute(array, "ctx", swap_pairs)

    def across(array, distance, wanted=lambda c, e: True):
        pairs = [
            (2 * (c ^ distance) + e, 2 * c + e)
            for c in range(chips)
            for e in range(2)
            if wanted(c, e)
        ]
        return lax.ppermute(array, "ctx", pairs)

    square = chips == 4
    kv_mine, kv_send = halves(me & 1, k_soft, v_soft)
    kv_other = swap(kv_send)
    states, sums = local_states(log_decay, k_lin, v_lin, [kv_mine])
    others = swap(states)
    early, late, q_send = pair_block(me_flag, kv_mine, kv_other, q_soft, [sums])
    kv = (early, late)
    q_other = swap(q_send)
    total, prefix = chip_total(me_flag, states, others, [q_send]), None
    inside, terms = inside_blocks(q_lin, k_lin, v_lin, sums, [total])

    def exchanged(array, step):
        return lax.ppermute(array, "head", [(i, i ^ step) for i in range(heads)])

    def sent(distance, array):
        return across(array, distance, lambda c, e: c ^ distance < c)

    def stage(distance, half, heads, carried, after):
        return later_stage(
            me_flag, distance, heads, arrived[distance][half], q_terms, *carried, after
        )

    bits = chips.bit_length() - 1
    arrived, token = {}, inside
    if square:
        first = sent(2, early)
        token = copied(late, [inside])
        arrived[2] = (first, sent(2, token))
        token = copied(early, [token])
        arrived[1] = (sent(1, token),)
    else:
        for distance in range(1, chips):
            arrived[distance] = tuple(sent(distance, array) for array in kv)
    q_terms, *carried = own_stage(me_flag, q_soft, q_other, *kv, [token])
    group = q_terms.shape[0]
    all_heads, front, back = range(group), range(group // 2), range(group // 2, group)

    token = carried[0]
    for bit in range(bits):
        last = bit == bits - 1
        theirs = across(total, 1 << bit, lambda c, e: not last or c ^ (1 << bit) < c)
        waits = [token] + ([arrived[1][1] if last else arrived[2][0]] if square else [])
        prefix, total = turn(me_flag, bit, total, theirs, prefix, last, waits)
        if square and bit == 0:
            carried = stage(2, 0, all_heads, carried, [prefix])
            token = copied(late, [carried[0]])
            arrived[1] += (sent(1, token),)
            relay = relayed(me_flag, kv, arrived[2], [token, arrived[1][0]])
            arrived[3] = lax.ppermute(relay, "ctx", [(0, 6), (2, 4), (5, 7), (7, 5)])
            carried = stage(2, 1, all_heads, carried, [relay, arrived[1][0]])
            carried = stage(1, 0, all_heads, carried, [])
            token = carried[0]
        elif not square:
            for half in range(2):
                carried = stage(bit + 1, half, all_heads, carried, [prefix])
            token = carried[0]
    prefix_other = swap(prefix)
    left = [(1, 1)] if square else [(d, h) for d in range(bits + 1, chips - 1) for h in range(2)]
    for distance, half in left[:-1]:
        carried = stage(distance, half, all_heads, carried, [prefix])
    carried = stage(*left[-1], front, carried, [prefix])
    linear, energy = linear_blocks(
        me_flag, terms, inside, sums, prefix, prefix_other, others, [carried[0]]
    )
    energies, step = [], 1
    while step < heads:
        energies.append(step)
        step *= 2
    other = exchanged(energy, energies[0])
    carried = stage(*left[-1], back, carried, [energy])
    for step in energies[1:]:
        energy = plus(energy, other, [carried[0]])
        other = exchanged(energy, step)

    if not square:
        relay = arrived[chips - 1]
        arrived[3] = relayed(me_flag, relay, relay, [])
    operands = [arrived[3], q_terms, *carried]
    theirs = last_stage(me_flag, chips - 1, "other", all_heads, operands, [energy])
    done = last_stage(me_flag, chips - 1, "own", front, operands, [theirs])
    columns = q_lin.shape[1] * heads
    more = [swap(theirs), done, energy, other, lin_gain.reshape(1, -1), linear]
    return tuple(
        last_stage(me_flag, chips - 1, "own", back, operands, [], (columns, more))
    )


def solution(mesh):
    return jax.shard_map(
        body,
        mesh=mesh,
        in_specs=(
            P("ctx", "head"),
            P("ctx", "head"),
            P("ctx", "head"),
            P("head", "ctx"),
            P("head"),
            P("ctx", "head"),
            P("ctx", "head"),
            P("ctx", "head"),
        ),
        out_specs=(P("ctx", "head"), P("ctx", "head")),
        check_vma=False,
    )
```

```python
import functools
import math

import jax
import jax.numpy as jnp
from jax import lax
from jax.experimental import pallas as pl
from jax.experimental.pallas import tpu as pltpu
from jax.sharding import PartitionSpec as P

HD = 128
NEGATIVE = -1e30
EPSILON = 1e-05
ENERGY_ROWS = 16
F32 = jnp.float32
BF16 = jnp.bfloat16
NT = (((1,), (1,)), ((), ()))
VMEM_LIMIT = 32 * 1024 * 1024
VMEM = pl.BlockSpec(memory_space=pltpu.VMEM)
SMEM = pl.BlockSpec(memory_space=pltpu.SMEM)
ANY = pl.BlockSpec(memory_space=pl.ANY)
HBM = pl.BlockSpec(memory_space=pltpu.HBM)


def split(x):
    high = x.astype(BF16)
    low = (x - high.astype(F32)).astype(BF16)
    return high, low


def dot(a, b):
    return jnp.dot(a, b, preferred_element_type=F32)


def three_term(a, b):
    a_high, a_low = split(a)
    b_high, b_low = split(b)
    wide = dot(a_high, jnp.concatenate([b_high, b_low], axis=1))
    n = b.shape[1]
    return wide[:, :n] + wide[:, n:] + dot(a_low, b_high)


def call(kernel, in_specs, out_specs, out_shape, scratch=(), alias=None, after=()):
    count = len(in_specs)

    def ordered(*refs):
        kernel(*refs[:count], *refs[count + len(after) :])

    made = pl.pallas_call(
        ordered,
        in_specs=in_specs + [ANY] * len(after),
        out_specs=out_specs,
        out_shape=out_shape,
        scratch_shapes=list(scratch),
        input_output_aliases=alias or {},
        cost_estimate=pl.CostEstimate(flops=1, bytes_accessed=1, transcendentals=0),
        compiler_params=pltpu.CompilerParams(vmem_limit_bytes=VMEM_LIMIT),
    )
    return lambda *operands: made(*operands, *after)


def state_kernel(rate_ref, k_ref, v_ref, packed_ref, sums_ref):
    tokens = k_ref.shape[0]
    heads = rate_ref.shape[0]
    half = heads // 2
    upto = lax.broadcasted_iota(jnp.int32, (tokens, tokens), 0)
    upto = (upto <= lax.broadcasted_iota(jnp.int32, (tokens, tokens), 1)).astype(F32)
    sums = jnp.dot(
        rate_ref[...], upto, precision=lax.Precision.HIGHEST, preferred_element_type=F32
    )
    sums_ref[...] = sums
    totals = sums[:, tokens - 1 : tokens]
    trailing = jnp.exp(totals - sums)
    for side in range(2):
        packed_ref[side, half * HD :] = jnp.zeros((8, HD), F32)
    for h in range(heads):
        side, i = h // half, h % half
        at = slice(h * HD, (h + 1) * HD)
        packed_ref[side, i * HD : (i + 1) * HD] = three_term(
            k_ref[:, at].T * trailing[h : h + 1], v_ref[:, at]
        )
        packed_ref[side, half * HD + i : half * HD + i + 1] = jnp.broadcast_to(
            totals[h : h + 1], (1, HD)
        )


def local_states(rates, k_lin, v_lin, after):
    tokens = k_lin.shape[0]
    heads = rates.shape[0]
    return call(
        state_kernel,
        [VMEM] * 3,
        [VMEM] * 2,
        [
            jax.ShapeDtypeStruct((2, heads // 2 * HD + 8, HD), F32),
            jax.ShapeDtypeStruct((heads, tokens), F32),
        ],
        after=after,
    )(rates, k_lin, v_lin)


def join(half, first, second, out_ref):
    decay = jnp.exp(second[half * HD :, :])
    for i in range(half):
        at = slice(i * HD, (i + 1) * HD)
        out_ref[at] = first[at] * decay[i : i + 1] + second[at]
    out_ref[half * HD :] = first[half * HD :] + second[half * HD :]


def chip_kernel(half, me_ref, states_ref, others_ref, out_ref):
    core = me_ref[0] & 1

    @pl.when(core == 0)
    def _():
        join(half, states_ref[0], others_ref[0], out_ref)

    @pl.when(core == 1)
    def _():
        join(half, others_ref[1], states_ref[1], out_ref)


def chip_total(me, states, others, after):
    _, packed, _ = states.shape
    return call(
        functools.partial(chip_kernel, (packed - 8) // HD),
        [SMEM, VMEM, VMEM],
        VMEM,
        jax.ShapeDtypeStruct((packed, HD), F32),
        after=after,
    )(me, states, others)


def turn_kernel(half, bit, first, last, me_ref, total_ref, theirs_ref, *refs):
    refs = list(refs)
    before_ref = None if first else refs.pop(0)
    prefix_ref = refs.pop(0)
    total_out = None if last else refs.pop(0)
    late = (me_ref[0] >> (bit + 1)) & 1

    @pl.when(late == 0)
    def _():
        prefix_ref[...] = jnp.zeros_like(prefix_ref) if first else before_ref[...]
        if not last:
            join(half, total_ref[...], theirs_ref[...], total_out)

    @pl.when(late == 1)
    def _():
        if first:
            prefix_ref[...] = theirs_ref[...]
        else:
            join(half, theirs_ref[...], before_ref[...], prefix_ref)
        if not last:
            join(half, theirs_ref[...], total_ref[...], total_out)


def turn(me, bit, total, theirs, before, last, after):
    packed = total.shape[0]
    operands = [total, theirs] + ([] if before is None else [before])
    count = 1 if last else 2
    out = call(
        functools.partial(turn_kernel, (packed - 8) // HD, bit, before is None, last),
        [SMEM] + [VMEM] * len(operands),
        [VMEM] * count,
        [jax.ShapeDtypeStruct((packed, HD), F32)] * count,
        after=after,
    )(me, *operands)
    return out[0], (None if last else out[1])


def inside_kernel(q_ref, k_ref, v_ref, sums_ref, out_ref, terms_ref):
    tokens = q_ref.shape[0]
    heads = sums_ref.shape[0]
    causal = lax.broadcasted_iota(jnp.int32, (tokens, tokens), 0) >= lax.broadcasted_iota(
        jnp.int32, (tokens, tokens), 1
    )
    columns = sums_ref[...].T
    for h in range(heads):
        at = slice(h * HD, (h + 1) * HD)
        q_high, q_low = split(q_ref[:, at])
        k_high, k_low = split(k_ref[:, at])
        terms_ref[h, :, :HD] = q_high
        terms_ref[h, :, HD:] = q_low
        scores = lax.dot_general(
            jnp.concatenate([q_high, q_low, q_high], axis=1),
            jnp.concatenate([k_high, k_high, k_low], axis=1),
            NT,
            preferred_element_type=F32,
        )
        gaps = columns[:, h : h + 1] - sums_ref[h : h + 1, :]
        weights = jnp.where(causal, jnp.exp(jnp.where(causal, gaps, 0.0)), 0.0)
        out_ref[h] = three_term(scores * weights, v_ref[:, at])


def inside_blocks(q_lin, k_lin, v_lin, sums, after):
    tokens = q_lin.shape[0]
    heads = sums.shape[0]
    return call(
        inside_kernel,
        [VMEM] * 4,
        [VMEM] * 2,
        [
            jax.ShapeDtypeStruct((heads, tokens, HD), F32),
            jax.ShapeDtypeStruct((heads, tokens, 2 * HD), BF16),
        ],
        after=after,
    )(q_lin, k_lin, v_lin, sums)


def linear_kernel(me_ref, terms_ref, inside_ref, sums_ref, mine_ref, theirs_ref, other_ref, out_ref, energy_ref):
    heads, tokens, _ = inside_ref.shape
    half = heads // 2
    core = me_ref[0] & 1
    leading = jnp.exp(sums_ref[...]).T
    squares = jnp.zeros((tokens, HD), F32)
    for side in range(2):
        decay = jnp.exp(other_ref[side, half * HD :])
        for i in range(half):
            h = side * half + i
            at = slice(i * HD, (i + 1) * HD)
            prior = jnp.where(core == side, mine_ref[at], theirs_ref[at])
            prior = jnp.where(core == 1, prior * decay[i : i + 1] + other_ref[side, at], prior)
            high, low = split(prior)
            wide = dot(terms_ref[h, :, :HD], jnp.concatenate([high, low], axis=1))
            carried = wide[:, :HD] + wide[:, HD:] + dot(terms_ref[h, :, HD:], high)
            linear = inside_ref[h] + leading[:, h : h + 1] * carried
            out_ref[:, h * HD : (h + 1) * HD] = linear
            squares = squares + linear * linear
    energy_ref[...] = lax.dot_general(
        jnp.ones((energy_ref.shape[0], HD), F32),
        squares,
        NT,
        precision=lax.Precision.HIGHEST,
        preferred_element_type=F32,
    )


def linear_blocks(me, terms, inside, sums, mine, theirs, other, after):
    heads, tokens, _ = inside.shape
    return call(
        linear_kernel,
        [SMEM] + [VMEM] * 6,
        [VMEM] * 2,
        [
            jax.ShapeDtypeStruct((tokens, heads * HD), F32),
            jax.ShapeDtypeStruct((ENERGY_ROWS, tokens), F32),
        ],
        after=after,
    )(me, terms, inside, sums, mine, theirs, other)


def halves(core, *arrays):
    early = [array[:, :HD] for array in arrays]
    late = [array[:, HD:] for array in arrays]
    mine = jnp.stack([jnp.where(core == 0, a, b) for a, b in zip(early, late)])
    theirs = jnp.stack([jnp.where(core == 0, b, a) for a, b in zip(early, late)])
    return mine, theirs


def pair_kernel(me_ref, mine_ref, other_ref, q_ref, out_ref, send_ref):
    tokens = mine_ref.shape[1]
    group = send_ref.shape[0]
    core = me_ref[0] & 1
    first = core == 0
    for side in range(2):
        mine, other = mine_ref[side], other_ref[side]
        out_ref[side, :tokens] = jnp.where(first, mine, other)
        out_ref[side, tokens:] = jnp.where(first, other, mine)
    for g in range(group):
        at = pl.ds(pl.multiple_of(((1 - core) * group + g) * HD, HD), HD)
        send_ref[g] = q_ref[:, at]


def pair_block(me, mine, other, q_soft, after):
    _, tokens, _ = mine.shape
    group = q_soft.shape[1] // (2 * HD)
    return call(
        pair_kernel,
        [SMEM] + [VMEM] * 3,
        [VMEM] * 2,
        [
            jax.ShapeDtypeStruct((2, 2 * tokens, HD), F32),
            jax.ShapeDtypeStruct((group, tokens, HD), F32),
        ],
        after=after,
    )(me, mine, other, q_soft)


def run(count, score, soften, gather):
    scores, before = score(0), None
    for i in range(count):
        following = score(i + 1) if i + 1 < count else None
        if before is not None:
            gather(i - 1, before)
        before = soften(i, scores)
        scores = following
    gather(count - 1, before)


def run_loop(trips, count, score, soften, gather):
    def trip(j, carry):
        run(
            count,
            lambda i: score((j, i)),
            lambda i, scores: soften((j, i), scores),
            lambda i, terms: gather((j, i), terms),
        )
        return carry

    lax.fori_loop(0, trips, trip, 0)


def fill_terms(kv_ref, keys_ref, values_ref):
    k_high, k_low = split(kv_ref[0].T)
    keys_ref[:HD] = k_high
    keys_ref[HD : 2 * HD] = k_high
    keys_ref[2 * HD :] = k_low
    v_high, v_low = split(kv_ref[1])
    values_ref[:, :HD] = v_high
    values_ref[:, HD:] = v_low


def lane_max(array):
    peak = array[:, :HD]
    for c in range(1, array.shape[1] // HD):
        peak = jnp.maximum(peak, array[:, c * HD : (c + 1) * HD])
    return peak


def score_terms(pair):
    return jnp.concatenate([pair, pair[:, :HD]], axis=1)


def weigh(scores, peak, total):
    high, low = [], []
    for c in range(scores.shape[1] // HD):
        w = jnp.exp2(scores[:, c * HD : (c + 1) * HD] - peak)
        total = total + w
        pair = split(w)
        high.append(pair[0])
        low.append(pair[1])
    return jnp.concatenate(high, axis=1), jnp.concatenate(low, axis=1), total


def summed(high, low, values):
    wide = dot(high, values)
    return wide[:, :HD] + wide[:, HD:] + dot(low, values[:, :HD])


def own_kernel(factor, me_ref, q_ref, q_other_ref, kv_ref, q_out, acc_out, peak_out, total_out, keys_ref, values_ref):
    group, tokens = q_out.shape[0], q_ref.shape[0]
    core = me_ref[0] & 1
    first = core == 0
    fill_terms(kv_ref, keys_ref, values_ref)
    seen = lax.broadcasted_iota(jnp.int32, (tokens, tokens), 1)
    seen = seen <= lax.broadcasted_iota(jnp.int32, (tokens, tokens), 0)

    def where(step):
        j, i = step
        t = i % 2
        return 2 * j + i // 2, slice(t * tokens, (t + 1) * tokens), slice(0, (t + 1) * tokens)

    def score(i):
        g, rows, keys = where(i)
        at = pl.ds(pl.multiple_of((core * group + g) * HD, HD), HD)
        mine, other = q_ref[:, at], q_other_ref[g]
        early = i[1] % 2 == 0
        queries = jnp.where(first, mine, other) if early else jnp.where(first, other, mine)
        pair = jnp.concatenate(split(queries * factor), axis=1)
        q_out[g, rows] = pair
        s = dot(score_terms(pair), keys_ref[:, keys])
        edge = jnp.where(seen, s[:, rows], NEGATIVE)
        return edge if early else jnp.concatenate([s[:, :tokens], edge], axis=1)

    def soften(i, s):
        g, rows, _ = where(i)
        peak = jnp.max(lane_max(s), axis=1, keepdims=True)
        peak_out[g, rows] = jnp.broadcast_to(peak, (tokens, HD))
        high, low, total_out[g, rows] = weigh(s, peak, jnp.zeros((tokens, HD), F32))
        return high, low

    def gather(i, terms):
        g, rows, keys = where(i)
        acc_out[g, rows] = summed(*terms, values_ref[keys])

    run_loop(group // 2, 4, score, soften, gather)


def term_scratch(keys):
    return [pltpu.VMEM((3 * HD, keys), BF16), pltpu.VMEM((keys, 2 * HD), BF16)]


def own_stage(me, q_soft, q_other, kv, after):
    tokens, width = q_soft.shape
    group = width // (2 * HD)
    stat = jax.ShapeDtypeStruct((group, 2 * tokens, HD), F32)
    return call(
        functools.partial(own_kernel, math.log2(math.e) / math.sqrt(HD)),
        [SMEM] + [VMEM] * 3,
        [VMEM] * 4,
        [jax.ShapeDtypeStruct((group, 2 * tokens, 2 * HD), BF16), stat, stat, stat],
        term_scratch(2 * tokens),
        after=after,
    )(me, q_soft, q_other, kv)


def later_kernel(distance, parts, heads, me_ref, kv_ref, q_ref, acc_ref, peak_ref, total_ref, acc_out, peak_out, total_out, keys_ref, values_ref):
    size = q_ref.shape[1] // parts
    per = 2 if len(heads) % 2 == 0 else 1
    chip = me_ref[0] >> 1

    def where(i):
        j, n = i
        head = heads[0] + j * per + n // parts
        return head, slice(n % parts * size, (n % parts + 1) * size)

    def score(i):
        return dot(score_terms(q_ref[where(i)]), keys_ref[...])

    def soften(i, s):
        at = where(i)
        old = peak_ref[at]
        peak = jnp.maximum(jnp.max(lane_max(s), axis=1, keepdims=True), old)
        shrink = jnp.exp2(old - peak)
        peak_out[at] = peak
        high, low, total_out[at] = weigh(s, peak, total_ref[at] * shrink)
        return high, low, shrink

    def gather(i, terms):
        at = where(i)
        acc_out[at] = acc_ref[at] * terms[2] + summed(*terms[:2], values_ref[...])

    @pl.when(lax.bitwise_xor(chip, distance) < chip)
    def _():
        fill_terms(kv_ref, keys_ref, values_ref)
        run_loop(len(heads) // per, parts * per, score, soften, gather)


def later_stage(me, distance, heads, kv, q_terms, acc, peak, total, after, parts=4):
    return call(
        functools.partial(later_kernel, distance, parts, heads),
        [SMEM] + [VMEM] * 5,
        [VMEM] * 3,
        [jax.ShapeDtypeStruct(acc.shape, F32)] * 3,
        term_scratch(kv.shape[1]),
        alias={3: 0, 4: 1, 5: 2},
        after=after,
    )(me, kv, q_terms, acc, peak, total)


def last_kernel(distance, whose, heads, columns, me_ref, kv_ref, q_ref, acc_ref, peak_ref, total_ref, *refs):
    if columns is None:
        out_ref, keys_ref, values_ref = refs
    else:
        theirs_ref, done_ref, energy_ref, energy_other_ref, gain_ref, linear_ref = refs[:6]
        lin_hbm, soft_hbm, lin_ref, out_ref, sems, keys_ref, values_ref = refs[6:]
    group, rows, _ = q_ref.shape
    tokens = rows // 2
    core, chip = me_ref[0] & 1, me_ref[0] >> 1
    side = core if whose == "own" else 1 - core
    at = pl.ds(pl.multiple_of(side * tokens, tokens), tokens)
    copies = []

    def copy(source, target):
        copies.append(pltpu.make_async_copy(source, target, sems.at[len(copies)]))
        return copies[-1]

    def columns_of(whose, g, count):
        return pl.ds(pl.multiple_of((whose * group + g) * HD, HD), count * HD)

    if columns is not None:
        blocks = [pl.ds(n * (tokens // 4), tokens // 4) for n in range(4)]
        for block in blocks:
            to = soft_hbm.at[block, columns_of(1 - core, 0, group)]
            copy(theirs_ref.at[block], to).start()
        factor = lax.rsqrt((energy_ref[:8] + energy_other_ref[:8]) / columns + EPSILON)
        factor = factor.T[:, 0:1]
        for n, block in enumerate(blocks):
            rows = slice(n * (tokens // 4), (n + 1) * (tokens // 4))
            lin_ref[rows] = linear_ref[rows] * factor[rows] * gain_ref[...]
            copy(lin_ref.at[block], lin_hbm.at[block]).start()
        for block in blocks:
            to = soft_hbm.at[block, columns_of(core, 0, group - len(heads))]
            copy(done_ref.at[block], to).start()
        own_copies = [
            copy(out_ref.at[:, pl.ds(n * HD, HD)], soft_hbm.at[:, columns_of(core, g, 1)])
            for n, g in enumerate(heads)
        ]

    def finish(n, acc, total):
        to = pl.ds(pl.multiple_of(n * HD, HD), HD)
        out_ref[:, to] = acc / jnp.sum(total, axis=1, keepdims=True)
        if columns is not None:
            own_copies[n].start()

    def score(n):
        return dot(score_terms(q_ref[heads[0] + n, at]), keys_ref[...])

    def soften(n, s):
        old = peak_ref[heads[0] + n, at]
        peak = jnp.maximum(jnp.max(lane_max(s), axis=1, keepdims=True), old)
        shrink = jnp.exp2(old - peak)
        return *weigh(s, peak, total_ref[heads[0] + n, at] * shrink), shrink

    def gather(n, terms):
        high, low, total, shrink = terms
        new = summed(high, low, values_ref[...])
        finish(n, acc_ref[heads[0] + n, at] * shrink + new, total)

    visible = lax.bitwise_xor(chip, distance) < chip

    @pl.when(visible)
    def _():
        fill_terms(kv_ref, keys_ref, values_ref)
        if columns is None and len(heads) % 2 == 0:
            run_loop(
                len(heads) // 2,
                2,
                lambda i: score(2 * i[0] + i[1]),
                lambda i, scores: soften(2 * i[0] + i[1], scores),
                lambda i, terms: gather(2 * i[0] + i[1], terms),
            )
        else:
            run(len(heads), score, soften, gather)

    @pl.when(jnp.logical_not(visible))
    def _():
        for n, g in enumerate(heads):
            finish(n, acc_ref[g, at], total_ref[g, at])

    for each in copies:
        each.wait()


def last_stage(me, distance, whose, heads, operands, after, extra=None):
    group, rows, _ = operands[1].shape
    tokens = rows // 2
    part = jax.ShapeDtypeStruct((tokens, len(heads) * HD), F32)
    scratch = term_scratch(operands[0].shape[1])
    out_shape, out_spec, columns = part, VMEM, None
    if extra is not None:
        columns, more = extra
        operands = [*operands, *more]
        linear = more[-1]
        out_shape = [
            jax.ShapeDtypeStruct(linear.shape, F32),
            jax.ShapeDtypeStruct((tokens, 2 * group * HD), F32),
        ]
        out_spec = [HBM] * 2
        scratch = [
            pltpu.VMEM(linear.shape, F32),
            pltpu.VMEM(part.shape, F32),
            pltpu.SemaphoreType.DMA((12 + len(heads),)),
        ] + scratch
    return call(
        functools.partial(last_kernel, distance, whose, heads, columns),
        [SMEM] + [VMEM] * len(operands),
        out_spec,
        out_shape,
        scratch,
        after=after,
    )(me, *operands)


def plus_kernel(a_ref, b_ref, out_ref):
    out_ref[...] = a_ref[...] + b_ref[...]


def plus(a, b, after):
    return call(
        plus_kernel, [VMEM] * 2, VMEM, jax.ShapeDtypeStruct(a.shape, F32), after=after
    )(a, b)


def copy_kernel(source_ref, out_ref):
    out_ref[...] = source_ref[...]


def copied(array, after):
    return call(copy_kernel, [VMEM], VMEM, jax.ShapeDtypeStruct(array.shape, F32), after=after)(
        array
    )


def relay_kernel(me_ref, own_ref, across_ref, out_ref):
    @pl.when((me_ref[0] & 1) == 0)
    def _():
        out_ref[...] = own_ref[...]

    @pl.when((me_ref[0] & 1) == 1)
    def _():
        out_ref[...] = across_ref[...]


def relayed(me, own, across, after):
    return call(
        relay_kernel,
        [SMEM, VMEM, VMEM],
        VMEM,
        jax.ShapeDtypeStruct(own.shape, F32),
        after=after,
    )(me, own, across)


def body(q_lin, k_lin, v_lin, log_decay, lin_gain, q_soft, k_soft, v_soft):
    chips = lax.axis_size("ctx") // 2
    heads = lax.axis_size("head")
    me = lax.axis_index("ctx")
    me_flag = me.reshape(1).astype(jnp.int32)
    assert k_soft.shape[1] == 2 * HD
    swap_pairs = [(2 * c + e, 2 * c + 1 - e) for c in range(chips) for e in range(2)]

    def swap(array):
        return lax.ppermute(array, "ctx", swap_pairs)

    def across(array, distance, wanted=lambda c, e: True):
        pairs = [
            (2 * (c ^ distance) + e, 2 * c + e)
            for c in range(chips)
            for e in range(2)
            if wanted(c, e)
        ]
        return lax.ppermute(array, "ctx", pairs)

    square = chips == 4
    kv_mine, kv_send = halves(me & 1, k_soft, v_soft)
    kv_other = swap(kv_send)
    states, sums = local_states(log_decay, k_lin, v_lin, [kv_mine])
    others = swap(states)
    kv, q_send = pair_block(me_flag, kv_mine, kv_other, q_soft, [sums])
    q_other = swap(q_send)
    total, prefix = chip_total(me_flag, states, others, [q_send]), None
    inside, terms = inside_blocks(q_lin, k_lin, v_lin, sums, [total])

    def exchanged(array, step):
        return lax.ppermute(array, "head", [(i, i ^ step) for i in range(heads)])

    def sent(distance, array):
        return across(array, distance, lambda c, e: c ^ distance < c)

    def stage(distance, heads, carried, after):
        return later_stage(
            me_flag, distance, heads, arrived[distance], q_terms, *carried, after
        )

    bits = chips.bit_length() - 1
    arrived, token = {}, inside
    if square:
        arrived[2] = sent(2, kv)
        token = copied(kv, [inside])
        arrived[1] = sent(1, token)
    else:
        for distance in range(1, chips):
            arrived[distance] = sent(distance, kv)
    q_terms, *carried = own_stage(me_flag, q_soft, q_other, kv, [token])
    group = q_terms.shape[0]
    all_heads, front, back = range(group), range(group // 2), range(group // 2, group)
    token = carried[0]
    if square:
        relay = relayed(me_flag, kv, arrived[2], [token])
        arrived[3] = lax.ppermute(relay, "ctx", [(0, 6), (2, 4), (5, 7), (7, 5)])
    for bit in range(bits):
        last = bit == bits - 1
        theirs = across(total, 1 << bit, lambda c, e: not last or c ^ (1 << bit) < c)
        prefix, total = turn(me_flag, bit, total, theirs, prefix, last, [token] + ([arrived[1]] if square and last else []))
        distance = 2 if square else bit + 1
        if not (square and last):
            carried = stage(distance, all_heads, carried, [prefix, relay] if square else [prefix])
            token = carried[0]
    prefix_other = swap(prefix)
    left = [1] if square else range(bits + 1, chips - 1)
    for distance in left[:-1]:
        carried = stage(distance, all_heads, carried, [prefix])
    carried = stage(left[-1], front, carried, [prefix])
    linear, energy = linear_blocks(
        me_flag, terms, inside, sums, prefix, prefix_other, others, [carried[0]]
    )
    energies, step = [], 1
    while step < heads:
        energies.append(step)
        step *= 2
    other = exchanged(energy, energies[0])
    carried = stage(left[-1], back, carried, [energy])
    operands = [arrived[chips - 1], q_terms, *carried]
    for step in energies[1:]:
        energy = plus(energy, other, [carried[0]])
        other = exchanged(energy, step)

    theirs = last_stage(me_flag, chips - 1, "other", all_heads, operands, [energy])
    done = last_stage(me_flag, chips - 1, "own", front, operands, [theirs])
    columns = q_lin.shape[1] * heads
    more = [swap(theirs), done, energy, other, lin_gain.reshape(1, -1), linear]
    return tuple(
        last_stage(me_flag, chips - 1, "own", back, operands, [], (columns, more))
    )


def solution(mesh):
    return jax.shard_map(
        body,
        mesh=mesh,
        in_specs=(
            P("ctx", "head"),
            P("ctx", "head"),
            P("ctx", "head"),
            P("head", "ctx"),
            P("head"),
            P("ctx", "head"),
            P("ctx", "head"),
            P("ctx", "head"),
        ),
        out_specs=(P("ctx", "head"), P("ctx", "head")),
        check_vma=False,
    )
```

```python
import functools
import math

import jax
import jax.numpy as jnp
from jax import lax
from jax.experimental import pallas as pl
from jax.experimental.pallas import tpu as pltpu
from jax.sharding import PartitionSpec as P

HD = 128
NEGATIVE = -1e30
EPSILON = 1e-05
ENERGY_ROWS = 16
F32 = jnp.float32
BF16 = jnp.bfloat16
NT = (((1,), (1,)), ((), ()))
VMEM_LIMIT = 32 * 1024 * 1024
VMEM = pl.BlockSpec(memory_space=pltpu.VMEM)
SMEM = pl.BlockSpec(memory_space=pltpu.SMEM)
ANY = pl.BlockSpec(memory_space=pl.ANY)
HBM = pl.BlockSpec(memory_space=pltpu.HBM)


def split(x):
    high = x.astype(BF16)
    low = (x - high.astype(F32)).astype(BF16)
    return high, low


def dot(a, b):
    return jnp.dot(a, b, preferred_element_type=F32)


def three_term(a, b):
    a_high, a_low = split(a)
    b_high, b_low = split(b)
    wide = dot(a_high, jnp.concatenate([b_high, b_low], axis=1))
    n = b.shape[1]
    return wide[:, :n] + wide[:, n:] + dot(a_low, b_high)


def call(kernel, in_specs, out_specs, out_shape, scratch=(), alias=None, after=()):
    count = len(in_specs)

    def ordered(*refs):
        kernel(*refs[:count], *refs[count + len(after) :])

    made = pl.pallas_call(
        ordered,
        in_specs=in_specs + [ANY] * len(after),
        out_specs=out_specs,
        out_shape=out_shape,
        scratch_shapes=list(scratch),
        input_output_aliases=alias or {},
        cost_estimate=pl.CostEstimate(flops=1, bytes_accessed=1, transcendentals=0),
        compiler_params=pltpu.CompilerParams(vmem_limit_bytes=VMEM_LIMIT),
    )
    return lambda *operands: made(*operands, *after)


def state_kernel(rate_ref, k_ref, v_ref, packed_ref, sums_ref):
    tokens = k_ref.shape[0]
    heads = rate_ref.shape[0]
    half = heads // 2
    upto = lax.broadcasted_iota(jnp.int32, (tokens, tokens), 0)
    upto = (upto <= lax.broadcasted_iota(jnp.int32, (tokens, tokens), 1)).astype(F32)
    sums = jnp.dot(
        rate_ref[...], upto, precision=lax.Precision.HIGHEST, preferred_element_type=F32
    )
    sums_ref[...] = sums
    totals = sums[:, tokens - 1 : tokens]
    trailing = jnp.exp(totals - sums)
    for side in range(2):
        packed_ref[side, half * HD :] = jnp.zeros((8, HD), F32)
    for h in range(heads):
        side, i = h // half, h % half
        at = slice(h * HD, (h + 1) * HD)
        packed_ref[side, i * HD : (i + 1) * HD] = three_term(
            k_ref[:, at].T * trailing[h : h + 1], v_ref[:, at]
        )
        packed_ref[side, half * HD + i : half * HD + i + 1] = jnp.broadcast_to(
            totals[h : h + 1], (1, HD)
        )


def local_states(rates, k_lin, v_lin, after):
    tokens = k_lin.shape[0]
    heads = rates.shape[0]
    return call(
        state_kernel,
        [VMEM] * 3,
        [VMEM] * 2,
        [
            jax.ShapeDtypeStruct((2, heads // 2 * HD + 8, HD), F32),
            jax.ShapeDtypeStruct((heads, tokens), F32),
        ],
        after=after,
    )(rates, k_lin, v_lin)


def join(half, first, second, out_ref):
    decay = jnp.exp(second[half * HD :, :])
    for i in range(half):
        at = slice(i * HD, (i + 1) * HD)
        out_ref[at] = first[at] * decay[i : i + 1] + second[at]
    out_ref[half * HD :] = first[half * HD :] + second[half * HD :]


def chip_kernel(half, me_ref, states_ref, others_ref, out_ref):
    core = me_ref[0] & 1

    @pl.when(core == 0)
    def _():
        join(half, states_ref[0], others_ref[0], out_ref)

    @pl.when(core == 1)
    def _():
        join(half, others_ref[1], states_ref[1], out_ref)


def chip_total(me, states, others, after):
    _, packed, _ = states.shape
    return call(
        functools.partial(chip_kernel, (packed - 8) // HD),
        [SMEM, VMEM, VMEM],
        VMEM,
        jax.ShapeDtypeStruct((packed, HD), F32),
        after=after,
    )(me, states, others)


def turn_kernel(half, bit, first, last, me_ref, total_ref, theirs_ref, *refs):
    refs = list(refs)
    before_ref = None if first else refs.pop(0)
    prefix_ref = refs.pop(0)
    total_out = None if last else refs.pop(0)
    late = (me_ref[0] >> (bit + 1)) & 1

    @pl.when(late == 0)
    def _():
        prefix_ref[...] = jnp.zeros_like(prefix_ref) if first else before_ref[...]
        if not last:
            join(half, total_ref[...], theirs_ref[...], total_out)

    @pl.when(late == 1)
    def _():
        if first:
            prefix_ref[...] = theirs_ref[...]
        else:
            join(half, theirs_ref[...], before_ref[...], prefix_ref)
        if not last:
            join(half, theirs_ref[...], total_ref[...], total_out)


def turn(me, bit, total, theirs, before, last, after):
    packed = total.shape[0]
    operands = [total, theirs] + ([] if before is None else [before])
    count = 1 if last else 2
    out = call(
        functools.partial(turn_kernel, (packed - 8) // HD, bit, before is None, last),
        [SMEM] + [VMEM] * len(operands),
        [VMEM] * count,
        [jax.ShapeDtypeStruct((packed, HD), F32)] * count,
        after=after,
    )(me, *operands)
    return out[0], (None if last else out[1])


def inside_kernel(q_ref, k_ref, v_ref, sums_ref, out_ref, terms_ref):
    tokens = q_ref.shape[0]
    heads = sums_ref.shape[0]
    causal = lax.broadcasted_iota(jnp.int32, (tokens, tokens), 0) >= lax.broadcasted_iota(
        jnp.int32, (tokens, tokens), 1
    )
    columns = sums_ref[...].T
    for h in range(heads):
        at = slice(h * HD, (h + 1) * HD)
        q_high, q_low = split(q_ref[:, at])
        k_high, k_low = split(k_ref[:, at])
        terms_ref[h, :, :HD] = q_high
        terms_ref[h, :, HD:] = q_low
        scores = lax.dot_general(
            jnp.concatenate([q_high, q_low, q_high], axis=1),
            jnp.concatenate([k_high, k_high, k_low], axis=1),
            NT,
            preferred_element_type=F32,
        )
        gaps = columns[:, h : h + 1] - sums_ref[h : h + 1, :]
        weights = jnp.where(causal, jnp.exp(jnp.where(causal, gaps, 0.0)), 0.0)
        out_ref[h] = three_term(scores * weights, v_ref[:, at])


def inside_blocks(q_lin, k_lin, v_lin, sums, after):
    tokens = q_lin.shape[0]
    heads = sums.shape[0]
    return call(
        inside_kernel,
        [VMEM] * 4,
        [VMEM] * 2,
        [
            jax.ShapeDtypeStruct((heads, tokens, HD), F32),
            jax.ShapeDtypeStruct((heads, tokens, 2 * HD), BF16),
        ],
        after=after,
    )(q_lin, k_lin, v_lin, sums)


def linear_kernel(me_ref, terms_ref, inside_ref, sums_ref, mine_ref, theirs_ref, other_ref, out_ref, energy_ref):
    heads, tokens, _ = inside_ref.shape
    half = heads // 2
    core = me_ref[0] & 1
    leading = jnp.exp(sums_ref[...]).T
    squares = jnp.zeros((tokens, HD), F32)
    for side in range(2):
        decay = jnp.exp(other_ref[side, half * HD :])
        for i in range(half):
            h = side * half + i
            at = slice(i * HD, (i + 1) * HD)
            prior = jnp.where(core == side, mine_ref[at], theirs_ref[at])
            prior = jnp.where(core == 1, prior * decay[i : i + 1] + other_ref[side, at], prior)
            high, low = split(prior)
            wide = dot(terms_ref[h, :, :HD], jnp.concatenate([high, low], axis=1))
            carried = wide[:, :HD] + wide[:, HD:] + dot(terms_ref[h, :, HD:], high)
            linear = inside_ref[h] + leading[:, h : h + 1] * carried
            out_ref[:, h * HD : (h + 1) * HD] = linear
            squares = squares + linear * linear
    energy_ref[...] = lax.dot_general(
        jnp.ones((energy_ref.shape[0], HD), F32),
        squares,
        NT,
        precision=lax.Precision.HIGHEST,
        preferred_element_type=F32,
    )


def linear_blocks(me, terms, inside, sums, mine, theirs, other, after):
    heads, tokens, _ = inside.shape
    return call(
        linear_kernel,
        [SMEM] + [VMEM] * 6,
        [VMEM] * 2,
        [
            jax.ShapeDtypeStruct((tokens, heads * HD), F32),
            jax.ShapeDtypeStruct((ENERGY_ROWS, tokens), F32),
        ],
        after=after,
    )(me, terms, inside, sums, mine, theirs, other)


def halves(core, *arrays):
    early = [array[:, :HD] for array in arrays]
    late = [array[:, HD:] for array in arrays]
    mine = jnp.stack([jnp.where(core == 0, a, b) for a, b in zip(early, late)])
    theirs = jnp.stack([jnp.where(core == 0, b, a) for a, b in zip(early, late)])
    return mine, theirs


def pair_kernel(me_ref, mine_ref, other_ref, q_ref, out_ref, send_ref):
    tokens = mine_ref.shape[1]
    group = send_ref.shape[0]
    core = me_ref[0] & 1
    first = core == 0
    for side in range(2):
        mine, other = mine_ref[side], other_ref[side]
        out_ref[side, :tokens] = jnp.where(first, mine, other)
        out_ref[side, tokens:] = jnp.where(first, other, mine)
    for g in range(group):
        at = pl.ds(pl.multiple_of(((1 - core) * group + g) * HD, HD), HD)
        send_ref[g] = q_ref[:, at]


def pair_block(me, mine, other, q_soft, after):
    _, tokens, _ = mine.shape
    group = q_soft.shape[1] // (2 * HD)
    return call(
        pair_kernel,
        [SMEM] + [VMEM] * 3,
        [VMEM] * 2,
        [
            jax.ShapeDtypeStruct((2, 2 * tokens, HD), F32),
            jax.ShapeDtypeStruct((group, tokens, HD), F32),
        ],
        after=after,
    )(me, mine, other, q_soft)


def run(count, score, soften, gather):
    scores, before = score(0), None
    for i in range(count):
        following = score(i + 1) if i + 1 < count else None
        if before is not None:
            gather(i - 1, before)
        before = soften(i, scores)
        scores = following
    gather(count - 1, before)


def fill_terms(kv_ref, keys_ref, values_ref):
    k_high, k_low = split(kv_ref[0].T)
    keys_ref[:HD] = k_high
    keys_ref[HD : 2 * HD] = k_high
    keys_ref[2 * HD : 3 * HD] = k_low
    keys_ref[3 * HD :] = k_low
    v_high, v_low = split(kv_ref[1])
    values_ref[:, :HD] = v_high
    values_ref[:, HD:] = v_low


def lane_max(array):
    peak = array[:, :HD]
    for c in range(1, array.shape[1] // HD):
        peak = jnp.maximum(peak, array[:, c * HD : (c + 1) * HD])
    return peak


def deep_terms(pair):
    return jnp.concatenate([pair, pair], axis=1)


def score_terms(pair):
    return jnp.concatenate([pair, pair[:, :HD]], axis=1)


def weigh(scores, peak, total):
    high, low = [], []
    for c in range(scores.shape[1] // HD):
        w = jnp.exp2(scores[:, c * HD : (c + 1) * HD] - peak)
        total = total + w
        pair = split(w)
        high.append(pair[0])
        low.append(pair[1])
    return jnp.concatenate(high, axis=1), jnp.concatenate(low, axis=1), total


def summed_stacked(high, low, values):
    rows = high.shape[0]
    wide = dot(jnp.concatenate([high, low], axis=0), values)
    return wide[:rows, :HD] + wide[:rows, HD:] + (wide[rows:, :HD] + wide[rows:, HD:])


def summed(high, low, values):
    wide = dot(high, values)
    return wide[:, :HD] + wide[:, HD:] + dot(low, values[:, :HD])


def own_kernel(factor, me_ref, q_ref, q_other_ref, kv_ref, q_out, acc_out, peak_out, total_out, keys_ref, values_ref):
    group, tokens = q_out.shape[0], q_ref.shape[0]
    core = me_ref[0] & 1
    first = core == 0
    fill_terms(kv_ref, keys_ref, values_ref)
    seen = lax.broadcasted_iota(jnp.int32, (tokens, tokens), 1)
    seen = seen <= lax.broadcasted_iota(jnp.int32, (tokens, tokens), 0)

    def where(i):
        t = i % 2
        return i // 2, slice(t * tokens, (t + 1) * tokens), slice(0, (t + 1) * tokens)

    def score(i):
        g, rows, keys = where(i)
        at = pl.ds(pl.multiple_of((core * group + g) * HD, HD), HD)
        mine, other = q_ref[:, at], q_other_ref[g]
        queries = jnp.where(first, mine, other) if i % 2 == 0 else jnp.where(first, other, mine)
        pair = jnp.concatenate(split(queries * factor), axis=1)
        q_out[g, rows] = pair
        s = dot(score_terms(pair), keys_ref[: 3 * HD, keys])
        edge = jnp.where(seen, s[:, rows], NEGATIVE)
        return edge if i % 2 == 0 else jnp.concatenate([s[:, :tokens], edge], axis=1)

    def soften(i, s):
        g, rows, _ = where(i)
        peak = jnp.max(lane_max(s), axis=1, keepdims=True)
        peak_out[g, rows] = jnp.broadcast_to(peak, (tokens, HD))
        high, low, total_out[g, rows] = weigh(s, peak, jnp.zeros((tokens, HD), F32))
        return high, low

    def gather(i, terms):
        g, rows, keys = where(i)
        acc_out[g, rows] = summed(*terms, values_ref[keys])

    run(2 * group, score, soften, gather)


def term_scratch(keys):
    return [pltpu.VMEM((4 * HD, keys), BF16), pltpu.VMEM((keys, 2 * HD), BF16)]


def own_stage(me, q_soft, q_other, kv, after):
    tokens, width = q_soft.shape
    group = width // (2 * HD)
    stat = jax.ShapeDtypeStruct((group, 2 * tokens, HD), F32)
    return call(
        functools.partial(own_kernel, math.log2(math.e) / math.sqrt(HD)),
        [SMEM] + [VMEM] * 3,
        [VMEM] * 4,
        [jax.ShapeDtypeStruct((group, 2 * tokens, 2 * HD), BF16), stat, stat, stat],
        term_scratch(2 * tokens),
        after=after,
    )(me, q_soft, q_other, kv)


def later_kernel(distance, parts, heads, deep, stacked, me_ref, kv_ref, q_ref, acc_ref, peak_ref, total_ref, acc_out, peak_out, total_out, keys_ref, values_ref):
    size = q_ref.shape[1] // parts
    chip = me_ref[0] >> 1

    def where(i):
        return heads[i // parts], slice(i % parts * size, (i % parts + 1) * size)

    def score(i):
        if deep:
            return dot(deep_terms(q_ref[where(i)]), keys_ref[...])
        return dot(score_terms(q_ref[where(i)]), keys_ref[: 3 * HD])

    def soften(i, s):
        at = where(i)
        old = peak_ref[at]
        peak = jnp.maximum(jnp.max(lane_max(s), axis=1, keepdims=True), old)
        shrink = jnp.exp2(old - peak)
        peak_out[at] = peak
        high, low, total_out[at] = weigh(s, peak, total_ref[at] * shrink)
        return high, low, shrink

    def gather(i, terms):
        at = where(i)
        product = summed_stacked if stacked else summed
        acc_out[at] = acc_ref[at] * terms[2] + product(*terms[:2], values_ref[...])

    @pl.when(lax.bitwise_xor(chip, distance) < chip)
    def _():
        fill_terms(kv_ref, keys_ref, values_ref)
        run(parts * len(heads), score, soften, gather)


def later_stage(me, distance, heads, kv, q_terms, acc, peak, total, after, deep=False, stacked=False, parts=4):
    return call(
        functools.partial(later_kernel, distance, parts, heads, deep, stacked),
        [SMEM] + [VMEM] * 5,
        [VMEM] * 3,
        [jax.ShapeDtypeStruct(acc.shape, F32)] * 3,
        term_scratch(kv.shape[1]),
        alias={3: 0, 4: 1, 5: 2},
        after=after,
    )(me, kv, q_terms, acc, peak, total)


def last_kernel(distance, whose, heads, columns, deep, stacked, me_ref, kv_ref, q_ref, acc_ref, peak_ref, total_ref, *refs):
    if columns is None:
        out_ref, keys_ref, values_ref = refs
    else:
        theirs_ref, done_ref, energy_ref, energy_other_ref, gain_ref, linear_ref = refs[:6]
        lin_hbm, soft_hbm, lin_ref, out_ref, sems, keys_ref, values_ref = refs[6:]
    group, rows, _ = q_ref.shape
    tokens = rows // 2
    core, chip = me_ref[0] & 1, me_ref[0] >> 1
    side = core if whose == "own" else 1 - core
    at = pl.ds(pl.multiple_of(side * tokens, tokens), tokens)
    copies = []

    def copy(source, target):
        copies.append(pltpu.make_async_copy(source, target, sems.at[len(copies)]))
        return copies[-1]

    def columns_of(whose, g, count):
        return pl.ds(pl.multiple_of((whose * group + g) * HD, HD), count * HD)

    if columns is not None:
        blocks = [pl.ds(n * (tokens // 4), tokens // 4) for n in range(4)]
        for block in blocks:
            to = soft_hbm.at[block, columns_of(1 - core, 0, group)]
            copy(theirs_ref.at[block], to).start()
        factor = lax.rsqrt((energy_ref[:8] + energy_other_ref[:8]) / columns + EPSILON)
        factor = factor.T[:, 0:1]
        for n, block in enumerate(blocks):
            rows = slice(n * (tokens // 4), (n + 1) * (tokens // 4))
            lin_ref[rows] = linear_ref[rows] * factor[rows] * gain_ref[...]
            copy(lin_ref.at[block], lin_hbm.at[block]).start()
        for block in blocks:
            to = soft_hbm.at[block, columns_of(core, 0, group - len(heads))]
            copy(done_ref.at[block], to).start()
        own_copies = [
            copy(out_ref.at[:, pl.ds(n * HD, HD)], soft_hbm.at[:, columns_of(core, g, 1)])
            for n, g in enumerate(heads)
        ]

    def finish(n, acc, total):
        out_ref[:, n * HD : (n + 1) * HD] = acc / jnp.sum(total, axis=1, keepdims=True)
        if columns is not None:
            own_copies[n].start()

    def score(n):
        if deep:
            return dot(deep_terms(q_ref[heads[n], at]), keys_ref[...])
        return dot(score_terms(q_ref[heads[n], at]), keys_ref[: 3 * HD])

    def soften(n, s):
        old = peak_ref[heads[n], at]
        peak = jnp.maximum(jnp.max(lane_max(s), axis=1, keepdims=True), old)
        shrink = jnp.exp2(old - peak)
        return *weigh(s, peak, total_ref[heads[n], at] * shrink), shrink

    def gather(n, terms):
        high, low, total, shrink = terms
        new = (summed_stacked if stacked else summed)(high, low, values_ref[...])
        finish(n, acc_ref[heads[n], at] * shrink + new, total)

    visible = lax.bitwise_xor(chip, distance) < chip

    @pl.when(visible)
    def _():
        fill_terms(kv_ref, keys_ref, values_ref)
        run(len(heads), score, soften, gather)

    @pl.when(jnp.logical_not(visible))
    def _():
        for n, g in enumerate(heads):
            finish(n, acc_ref[g, at], total_ref[g, at])

    for each in copies:
        each.wait()


def last_stage(me, distance, whose, heads, operands, after, extra=None, deep=False, stacked=False):
    group, rows, _ = operands[1].shape
    tokens = rows // 2
    part = jax.ShapeDtypeStruct((tokens, len(heads) * HD), F32)
    scratch = term_scratch(operands[0].shape[1])
    out_shape, out_spec, columns = part, VMEM, None
    if extra is not None:
        columns, more = extra
        operands = [*operands, *more]
        linear = more[-1]
        out_shape = [
            jax.ShapeDtypeStruct(linear.shape, F32),
            jax.ShapeDtypeStruct((tokens, 2 * group * HD), F32),
        ]
        out_spec = [HBM] * 2
        scratch = [
            pltpu.VMEM(linear.shape, F32),
            pltpu.VMEM(part.shape, F32),
            pltpu.SemaphoreType.DMA((12 + len(heads),)),
        ] + scratch
    return call(
        functools.partial(last_kernel, distance, whose, heads, columns, deep, stacked),
        [SMEM] + [VMEM] * len(operands),
        out_spec,
        out_shape,
        scratch,
        after=after,
    )(me, *operands)


def plus_kernel(a_ref, b_ref, out_ref):
    out_ref[...] = a_ref[...] + b_ref[...]


def plus(a, b, after):
    return call(
        plus_kernel, [VMEM] * 2, VMEM, jax.ShapeDtypeStruct(a.shape, F32), after=after
    )(a, b)


def copy_kernel(source_ref, out_ref):
    out_ref[...] = source_ref[...]


def copied(array, after):
    return call(copy_kernel, [VMEM], VMEM, jax.ShapeDtypeStruct(array.shape, F32), after=after)(
        array
    )


def relay_kernel(me_ref, own_ref, across_ref, out_ref):
    @pl.when((me_ref[0] & 1) == 0)
    def _():
        out_ref[...] = own_ref[...]

    @pl.when((me_ref[0] & 1) == 1)
    def _():
        out_ref[...] = across_ref[...]


def relayed(me, own, across, after):
    return call(
        relay_kernel,
        [SMEM, VMEM, VMEM],
        VMEM,
        jax.ShapeDtypeStruct(own.shape, F32),
        after=after,
    )(me, own, across)


def body(q_lin, k_lin, v_lin, log_decay, lin_gain, q_soft, k_soft, v_soft):
    chips = lax.axis_size("ctx") // 2
    heads = lax.axis_size("head")
    me = lax.axis_index("ctx")
    me_flag = me.reshape(1).astype(jnp.int32)
    assert k_soft.shape[1] == 2 * HD
    swap_pairs = [(2 * c + e, 2 * c + 1 - e) for c in range(chips) for e in range(2)]

    def swap(array):
        return lax.ppermute(array, "ctx", swap_pairs)

    def across(array, distance, wanted=lambda c, e: True):
        pairs = [
            (2 * (c ^ distance) + e, 2 * c + e)
            for c in range(chips)
            for e in range(2)
            if wanted(c, e)
        ]
        return lax.ppermute(array, "ctx", pairs)

    square = chips == 4
    kv_mine, kv_send = halves(me & 1, k_soft, v_soft)
    kv_other = swap(kv_send)
    states, sums = local_states(log_decay, k_lin, v_lin, [kv_mine])
    others = swap(states)
    kv, q_send = pair_block(me_flag, kv_mine, kv_other, q_soft, [sums])
    q_other = swap(q_send)
    total, prefix = chip_total(me_flag, states, others, [q_send]), None
    inside, terms = inside_blocks(q_lin, k_lin, v_lin, sums, [total])

    def exchanged(array, step):
        return lax.ppermute(array, "head", [(i, i ^ step) for i in range(heads)])

    def sent(distance, array):
        return across(array, distance, lambda c, e: c ^ distance < c)

    def stage(distance, heads, carried, after, deep=False, stacked=False):
        return later_stage(
            me_flag, distance, heads, arrived[distance], q_terms, *carried, after, deep, stacked
        )

    bits = chips.bit_length() - 1
    arrived, token = {}, inside
    if square:
        arrived[2] = sent(2, kv)
        token = copied(kv, [inside])
        arrived[1] = sent(1, token)
    else:
        for distance in range(1, chips):
            arrived[distance] = sent(distance, kv)
    q_terms, *carried = own_stage(me_flag, q_soft, q_other, kv, [token])
    group = q_terms.shape[0]
    all_heads, front, back = range(group), range(group // 2), range(group // 2, group)
    token = carried[0]
    if square:
        relay = relayed(me_flag, kv, arrived[2], [token])
        arrived[3] = lax.ppermute(relay, "ctx", [(0, 6), (2, 4), (5, 7), (7, 5)])
    for bit in range(bits):
        last = bit == bits - 1
        theirs = across(total, 1 << bit, lambda c, e: not last or c ^ (1 << bit) < c)
        prefix, total = turn(me_flag, bit, total, theirs, prefix, last, [token] + ([arrived[1]] if square and last else []))
        distance = 2 if square else bit + 1
        if not (square and last):
            waits = [prefix, relay] if square else [prefix]
            carried = stage(distance, all_heads, carried, waits, stacked=True)
            token = carried[0]
    prefix_other = swap(prefix)
    left = [1] if square else range(bits + 1, chips - 1)
    for distance in left[:-1]:
        carried = stage(distance, all_heads, carried, [prefix])
    carried = stage(left[-1], front, carried, [prefix], deep=True)
    linear, energy = linear_blocks(
        me_flag, terms, inside, sums, prefix, prefix_other, others, [carried[0]]
    )
    energies, step = [], 1
    while step < heads:
        energies.append(step)
        step *= 2
    other = exchanged(energy, energies[0])
    carried = stage(left[-1], back, carried, [energy])
    operands = [arrived[chips - 1], q_terms, *carried]
    for step in energies[1:]:
        energy = plus(energy, other, [carried[0]])
        other = exchanged(energy, step)

    theirs = last_stage(
        me_flag, chips - 1, "other", all_heads, operands, [energy], deep=True, stacked=True
    )
    done = last_stage(me_flag, chips - 1, "own", front, operands, [theirs])
    columns = q_lin.shape[1] * heads
    more = [swap(theirs), done, energy, other, lin_gain.reshape(1, -1), linear]
    return tuple(
        last_stage(me_flag, chips - 1, "own", back, operands, [], (columns, more))
    )


def solution(mesh):
    return jax.shard_map(
        body,
        mesh=mesh,
        in_specs=(
            P("ctx", "head"),
            P("ctx", "head"),
            P("ctx", "head"),
            P("head", "ctx"),
            P("head"),
            P("ctx", "head"),
            P("ctx", "head"),
            P("ctx", "head"),
        ),
        out_specs=(P("ctx", "head"), P("ctx", "head")),
        check_vma=False,
    )
```

```python
import functools
import math

import jax
import jax.numpy as jnp
from jax import lax
from jax.experimental import pallas as pl
from jax.experimental.pallas import tpu as pltpu
from jax.sharding import PartitionSpec as P

HD = 128
NEGATIVE = -1e30
EPSILON = 1e-05
ENERGY_ROWS = 16
F32 = jnp.float32
BF16 = jnp.bfloat16
NT = (((1,), (1,)), ((), ()))
VMEM_LIMIT = 32 * 1024 * 1024
VMEM = pl.BlockSpec(memory_space=pltpu.VMEM)
SMEM = pl.BlockSpec(memory_space=pltpu.SMEM)
ANY = pl.BlockSpec(memory_space=pl.ANY)
HBM = pl.BlockSpec(memory_space=pltpu.HBM)


def split(x):
    high = x.astype(BF16)
    low = (x - high.astype(F32)).astype(BF16)
    return high, low


def dot(a, b):
    return jnp.dot(a, b, preferred_element_type=F32)


def three_term(a, b):
    a_high, a_low = split(a)
    b_high, b_low = split(b)
    wide = dot(a_high, jnp.concatenate([b_high, b_low], axis=1))
    n = b.shape[1]
    return wide[:, :n] + wide[:, n:] + dot(a_low, b_high)


def call(kernel, in_specs, out_specs, out_shape, scratch=(), alias=None, after=()):
    count = len(in_specs)

    def ordered(*refs):
        kernel(*refs[:count], *refs[count + len(after) :])

    made = pl.pallas_call(
        ordered,
        in_specs=in_specs + [ANY] * len(after),
        out_specs=out_specs,
        out_shape=out_shape,
        scratch_shapes=list(scratch),
        input_output_aliases=alias or {},
        cost_estimate=pl.CostEstimate(flops=1, bytes_accessed=1, transcendentals=0),
        compiler_params=pltpu.CompilerParams(vmem_limit_bytes=VMEM_LIMIT),
    )
    return lambda *operands: made(*operands, *after)


def state_kernel(rate_ref, k_ref, v_ref, packed_ref, sums_ref):
    tokens = k_ref.shape[0]
    heads = rate_ref.shape[0]
    half = heads // 2
    upto = lax.broadcasted_iota(jnp.int32, (tokens, tokens), 0)
    upto = (upto <= lax.broadcasted_iota(jnp.int32, (tokens, tokens), 1)).astype(F32)
    sums = jnp.dot(
        rate_ref[...], upto, precision=lax.Precision.HIGHEST, preferred_element_type=F32
    )
    sums_ref[...] = sums
    totals = sums[:, tokens - 1 : tokens]
    trailing = jnp.exp(totals - sums)
    for side in range(2):
        packed_ref[side, half * HD :] = jnp.zeros((8, HD), F32)
    for h in range(heads):
        side, i = h // half, h % half
        at = slice(h * HD, (h + 1) * HD)
        packed_ref[side, i * HD : (i + 1) * HD] = three_term(
            k_ref[:, at].T * trailing[h : h + 1], v_ref[:, at]
        )
        packed_ref[side, half * HD + i : half * HD + i + 1] = jnp.broadcast_to(
            totals[h : h + 1], (1, HD)
        )


def local_states(rates, k_lin, v_lin, after):
    tokens = k_lin.shape[0]
    heads = rates.shape[0]
    return call(
        state_kernel,
        [VMEM] * 3,
        [VMEM] * 2,
        [
            jax.ShapeDtypeStruct((2, heads // 2 * HD + 8, HD), F32),
            jax.ShapeDtypeStruct((heads, tokens), F32),
        ],
        after=after,
    )(rates, k_lin, v_lin)


def join(half, first, second, out_ref):
    decay = jnp.exp(second[half * HD :, :])
    for i in range(half):
        at = slice(i * HD, (i + 1) * HD)
        out_ref[at] = first[at] * decay[i : i + 1] + second[at]
    out_ref[half * HD :] = first[half * HD :] + second[half * HD :]


def chip_kernel(half, me_ref, states_ref, others_ref, out_ref):
    core = me_ref[0] & 1

    @pl.when(core == 0)
    def _():
        join(half, states_ref[0], others_ref[0], out_ref)

    @pl.when(core == 1)
    def _():
        join(half, others_ref[1], states_ref[1], out_ref)


def chip_total(me, states, others, after):
    _, packed, _ = states.shape
    return call(
        functools.partial(chip_kernel, (packed - 8) // HD),
        [SMEM, VMEM, VMEM],
        VMEM,
        jax.ShapeDtypeStruct((packed, HD), F32),
        after=after,
    )(me, states, others)


def turn_kernel(half, bit, first, last, me_ref, total_ref, theirs_ref, *refs):
    refs = list(refs)
    before_ref = None if first else refs.pop(0)
    prefix_ref = refs.pop(0)
    total_out = None if last else refs.pop(0)
    late = (me_ref[0] >> (bit + 1)) & 1

    @pl.when(late == 0)
    def _():
        prefix_ref[...] = jnp.zeros_like(prefix_ref) if first else before_ref[...]
        if not last:
            join(half, total_ref[...], theirs_ref[...], total_out)

    @pl.when(late == 1)
    def _():
        if first:
            prefix_ref[...] = theirs_ref[...]
        else:
            join(half, theirs_ref[...], before_ref[...], prefix_ref)
        if not last:
            join(half, theirs_ref[...], total_ref[...], total_out)


def turn(me, bit, total, theirs, before, last, after):
    packed = total.shape[0]
    operands = [total, theirs] + ([] if before is None else [before])
    count = 1 if last else 2
    out = call(
        functools.partial(turn_kernel, (packed - 8) // HD, bit, before is None, last),
        [SMEM] + [VMEM] * len(operands),
        [VMEM] * count,
        [jax.ShapeDtypeStruct((packed, HD), F32)] * count,
        after=after,
    )(me, *operands)
    return out[0], (None if last else out[1])


def inside_kernel(q_ref, k_ref, v_ref, sums_ref, out_ref, terms_ref):
    tokens = q_ref.shape[0]
    heads = sums_ref.shape[0]
    causal = lax.broadcasted_iota(jnp.int32, (tokens, tokens), 0) >= lax.broadcasted_iota(
        jnp.int32, (tokens, tokens), 1
    )
    columns = sums_ref[...].T
    for h in range(heads):
        at = slice(h * HD, (h + 1) * HD)
        q_high, q_low = split(q_ref[:, at])
        k_high, k_low = split(k_ref[:, at])
        terms_ref[h, :, :HD] = q_high
        terms_ref[h, :, HD:] = q_low
        scores = lax.dot_general(
            jnp.concatenate([q_high, q_low, q_high], axis=1),
            jnp.concatenate([k_high, k_high, k_low], axis=1),
            NT,
            preferred_element_type=F32,
        )
        gaps = columns[:, h : h + 1] - sums_ref[h : h + 1, :]
        weights = jnp.where(causal, jnp.exp(jnp.where(causal, gaps, 0.0)), 0.0)
        out_ref[h] = three_term(scores * weights, v_ref[:, at])


def inside_blocks(q_lin, k_lin, v_lin, sums, after):
    tokens = q_lin.shape[0]
    heads = sums.shape[0]
    return call(
        inside_kernel,
        [VMEM] * 4,
        [VMEM] * 2,
        [
            jax.ShapeDtypeStruct((heads, tokens, HD), F32),
            jax.ShapeDtypeStruct((heads, tokens, 2 * HD), BF16),
        ],
        after=after,
    )(q_lin, k_lin, v_lin, sums)


def linear_kernel(me_ref, terms_ref, inside_ref, sums_ref, mine_ref, theirs_ref, other_ref, out_ref, energy_ref):
    heads, tokens, _ = inside_ref.shape
    half = heads // 2
    core = me_ref[0] & 1
    leading = jnp.exp(sums_ref[...]).T
    squares = jnp.zeros((tokens, HD), F32)
    for side in range(2):
        decay = jnp.exp(other_ref[side, half * HD :])
        for i in range(half):
            h = side * half + i
            at = slice(i * HD, (i + 1) * HD)
            prior = jnp.where(core == side, mine_ref[at], theirs_ref[at])
            prior = jnp.where(core == 1, prior * decay[i : i + 1] + other_ref[side, at], prior)
            high, low = split(prior)
            carried = dot(
                score_terms(terms_ref[h]), jnp.concatenate([high, high, low], axis=0)
            )
            linear = inside_ref[h] + leading[:, h : h + 1] * carried
            out_ref[:, h * HD : (h + 1) * HD] = linear
            squares = squares + linear * linear
    energy_ref[...] = lax.dot_general(
        jnp.ones((energy_ref.shape[0], HD), F32),
        squares,
        NT,
        precision=lax.Precision.HIGHEST,
        preferred_element_type=F32,
    )


def linear_blocks(me, terms, inside, sums, mine, theirs, other, after):
    heads, tokens, _ = inside.shape
    return call(
        linear_kernel,
        [SMEM] + [VMEM] * 6,
        [VMEM] * 2,
        [
            jax.ShapeDtypeStruct((tokens, heads * HD), F32),
            jax.ShapeDtypeStruct((ENERGY_ROWS, tokens), F32),
        ],
        after=after,
    )(me, terms, inside, sums, mine, theirs, other)


def halves(core, *arrays):
    early = [array[:, :HD] for array in arrays]
    late = [array[:, HD:] for array in arrays]
    mine = jnp.stack([jnp.where(core == 0, a, b) for a, b in zip(early, late)])
    theirs = jnp.stack([jnp.where(core == 0, b, a) for a, b in zip(early, late)])
    return mine, theirs


def pair_kernel(me_ref, mine_ref, other_ref, q_ref, out_ref, send_ref):
    tokens = mine_ref.shape[1]
    group = send_ref.shape[0]
    core = me_ref[0] & 1
    first = core == 0
    for side in range(2):
        mine, other = mine_ref[side], other_ref[side]
        out_ref[side, :tokens] = jnp.where(first, mine, other)
        out_ref[side, tokens:] = jnp.where(first, other, mine)
    for g in range(group):
        at = pl.ds(pl.multiple_of(((1 - core) * group + g) * HD, HD), HD)
        send_ref[g] = q_ref[:, at]


def pair_block(me, mine, other, q_soft, after):
    _, tokens, _ = mine.shape
    group = q_soft.shape[1] // (2 * HD)
    return call(
        pair_kernel,
        [SMEM] + [VMEM] * 3,
        [VMEM] * 2,
        [
            jax.ShapeDtypeStruct((2, 2 * tokens, HD), F32),
            jax.ShapeDtypeStruct((group, tokens, HD), F32),
        ],
        after=after,
    )(me, mine, other, q_soft)


def run(count, score, soften, gather):
    scores, before = score(0), None
    for i in range(count):
        following = score(i + 1) if i + 1 < count else None
        if before is not None:
            gather(i - 1, before)
        before = soften(i, scores)
        scores = following
    gather(count - 1, before)


def fill_terms(kv_ref, keys_ref, values_ref):
    k_high, k_low = split(kv_ref[0].T)
    keys_ref[:HD] = k_high
    keys_ref[HD : 2 * HD] = k_high
    keys_ref[2 * HD :] = k_low
    v_high, v_low = split(kv_ref[1])
    values_ref[:, :HD] = v_high
    values_ref[:, HD:] = v_low


def lane_max(array):
    peak = array[:, :HD]
    for c in range(1, array.shape[1] // HD):
        peak = jnp.maximum(peak, array[:, c * HD : (c + 1) * HD])
    return peak


def score_terms(pair):
    return jnp.concatenate([pair, pair[:, :HD]], axis=1)


def weigh(scores, peak, total):
    high, low = [], []
    for c in range(scores.shape[1] // HD):
        w = jnp.exp2(scores[:, c * HD : (c + 1) * HD] - peak)
        total = total + w
        pair = split(w)
        high.append(pair[0])
        low.append(pair[1])
    return jnp.concatenate(high, axis=1), jnp.concatenate(low, axis=1), total


def summed(high, low, values):
    wide = dot(high, values)
    return wide[:, :HD] + wide[:, HD:] + dot(low, values[:, :HD])


def own_kernel(factor, me_ref, q_ref, q_other_ref, kv_ref, q_out, acc_out, peak_out, total_out, keys_ref, values_ref):
    group, tokens = q_out.shape[0], q_ref.shape[0]
    core = me_ref[0] & 1
    first = core == 0
    fill_terms(kv_ref, keys_ref, values_ref)
    seen = lax.broadcasted_iota(jnp.int32, (tokens, tokens), 1)
    seen = seen <= lax.broadcasted_iota(jnp.int32, (tokens, tokens), 0)

    def where(i):
        t = i % 2
        return i // 2, slice(t * tokens, (t + 1) * tokens), slice(0, (t + 1) * tokens)

    def score(i):
        g, rows, keys = where(i)
        at = pl.ds(pl.multiple_of((core * group + g) * HD, HD), HD)
        mine, other = q_ref[:, at], q_other_ref[g]
        queries = jnp.where(first, mine, other) if i % 2 == 0 else jnp.where(first, other, mine)
        pair = jnp.concatenate(split(queries * factor), axis=1)
        q_out[g, rows] = pair
        s = dot(score_terms(pair), keys_ref[:, keys])
        edge = jnp.where(seen, s[:, rows], NEGATIVE)
        return edge if i % 2 == 0 else jnp.concatenate([s[:, :tokens], edge], axis=1)

    def soften(i, s):
        g, rows, _ = where(i)
        peak = jnp.max(lane_max(s), axis=1, keepdims=True)
        peak_out[g, rows] = jnp.broadcast_to(peak, (tokens, HD))
        high, low, total_out[g, rows] = weigh(s, peak, jnp.zeros((tokens, HD), F32))
        return high, low

    def gather(i, terms):
        g, rows, keys = where(i)
        acc_out[g, rows] = summed(*terms, values_ref[keys])

    run(2 * group, score, soften, gather)


def term_scratch(keys):
    return [pltpu.VMEM((3 * HD, keys), BF16), pltpu.VMEM((keys, 2 * HD), BF16)]


def own_stage(me, q_soft, q_other, kv, after):
    tokens, width = q_soft.shape
    group = width // (2 * HD)
    stat = jax.ShapeDtypeStruct((group, 2 * tokens, HD), F32)
    return call(
        functools.partial(own_kernel, math.log2(math.e) / math.sqrt(HD)),
        [SMEM] + [VMEM] * 3,
        [VMEM] * 4,
        [jax.ShapeDtypeStruct((group, 2 * tokens, 2 * HD), BF16), stat, stat, stat],
        term_scratch(2 * tokens),
        after=after,
    )(me, q_soft, q_other, kv)


def later_kernel(distance, parts, heads, fresh, me_ref, *refs):
    if fresh:
        kv_ref, q_ref, acc_ref, peak_ref, total_ref = refs[:5]
        acc_out, peak_out, total_out, keys_ref, values_ref = refs[5:]
    else:
        keys_ref, values_ref, q_ref, acc_ref, peak_ref, total_ref = refs[:6]
        acc_out, peak_out, total_out = refs[6:]
    size = q_ref.shape[1] // parts
    chip = me_ref[0] >> 1

    def where(i):
        return heads[i // parts], slice(i % parts * size, (i % parts + 1) * size)

    def score(i):
        return dot(score_terms(q_ref[where(i)]), keys_ref[...])

    def soften(i, s):
        at = where(i)
        old = peak_ref[at]
        peak = jnp.maximum(jnp.max(lane_max(s), axis=1, keepdims=True), old)
        shrink = jnp.exp2(old - peak)
        peak_out[at] = peak
        high, low, total_out[at] = weigh(s, peak, total_ref[at] * shrink)
        return high, low, shrink

    def gather(i, terms):
        at = where(i)
        acc_out[at] = acc_ref[at] * terms[2] + summed(*terms[:2], values_ref[...])

    @pl.when(lax.bitwise_xor(chip, distance) < chip)
    def _():
        if fresh:
            fill_terms(kv_ref, keys_ref, values_ref)
        run(parts * len(heads), score, soften, gather)


def term_shapes(keys):
    return [
        jax.ShapeDtypeStruct((3 * HD, keys), BF16),
        jax.ShapeDtypeStruct((keys, 2 * HD), BF16),
    ]


def later_stage(me, distance, heads, kv, q_terms, acc, peak, total, after, parts=4):
    fresh = not isinstance(kv, tuple)
    operands = [kv] if fresh else list(kv)
    shift = 1 + len(operands)
    out_shape = [jax.ShapeDtypeStruct(acc.shape, F32)] * 3
    if fresh:
        out_shape += term_shapes(kv.shape[1])
    out = call(
        functools.partial(later_kernel, distance, parts, heads, fresh),
        [SMEM] + [VMEM] * (len(operands) + 4),
        [VMEM] * len(out_shape),
        out_shape,
        alias={shift + 1: 0, shift + 2: 1, shift + 3: 2},
        after=after,
    )(me, *operands, q_terms, acc, peak, total)
    return out[:3], tuple(out[3:]) if fresh else kv


def last_kernel(distance, whose, heads, columns, me_ref, *refs):
    fresh = whose == "other"
    if fresh:
        kv_ref, q_ref, acc_ref, peak_ref, total_ref, out_ref, keys_ref, values_ref = refs
    else:
        keys_ref, values_ref, q_ref, acc_ref, peak_ref, total_ref, *refs = refs
    if columns is not None:
        theirs_ref, done_ref, energy_ref, energy_other_ref, gain_ref, linear_ref = refs[:6]
        lin_hbm, soft_hbm, lin_ref, out_ref, sems = refs[6:]
    elif not fresh:
        (out_ref,) = refs
    group, rows, _ = q_ref.shape
    tokens = rows // 2
    core, chip = me_ref[0] & 1, me_ref[0] >> 1
    side = core if whose == "own" else 1 - core
    at = pl.ds(pl.multiple_of(side * tokens, tokens), tokens)
    copies = []

    def copy(source, target):
        copies.append(pltpu.make_async_copy(source, target, sems.at[len(copies)]))
        return copies[-1]

    def columns_of(whose, g, count):
        return pl.ds(pl.multiple_of((whose * group + g) * HD, HD), count * HD)

    if columns is not None:
        blocks = [pl.ds(n * (tokens // 4), tokens // 4) for n in range(4)]
        for block in blocks:
            to = soft_hbm.at[block, columns_of(1 - core, 0, group)]
            copy(theirs_ref.at[block], to).start()
        factor = lax.rsqrt((energy_ref[:8] + energy_other_ref[:8]) / columns + EPSILON)
        factor = factor.T[:, 0:1]
        for block in blocks:
            to = soft_hbm.at[block, columns_of(core, 0, group - len(heads))]
            copy(done_ref.at[block], to).start()
        lin_copies = [copy(lin_ref.at[block], lin_hbm.at[block]) for block in blocks]
        own_copies = [
            copy(out_ref.at[:, pl.ds(n * HD, HD)], soft_hbm.at[:, columns_of(core, g, 1)])
            for n, g in enumerate(heads)
        ]

    def scale_rows(n):
        rows = slice(n * (tokens // 4), (n + 1) * (tokens // 4))
        lin_ref[rows] = linear_ref[rows] * factor[rows] * gain_ref[...]
        lin_copies[n].start()

    def finish(n, acc, total):
        out_ref[:, n * HD : (n + 1) * HD] = acc / jnp.sum(total, axis=1, keepdims=True)
        if columns is not None:
            own_copies[n].start()

    def score(n):
        return dot(score_terms(q_ref[heads[n], at]), keys_ref[...])

    def soften(n, s):
        old = peak_ref[heads[n], at]
        peak = jnp.maximum(jnp.max(lane_max(s), axis=1, keepdims=True), old)
        shrink = jnp.exp2(old - peak)
        return *weigh(s, peak, total_ref[heads[n], at] * shrink), shrink

    def gather(n, terms):
        high, low, total, shrink = terms
        new = summed(high, low, values_ref[...])
        finish(n, acc_ref[heads[n], at] * shrink + new, total)

    def gather_and_scale(n, terms):
        gather(n, terms)
        if n == 0:
            for block in range(2, 4):
                scale_rows(block)

    if columns is not None:
        for block in range(2):
            scale_rows(block)
    visible = lax.bitwise_xor(chip, distance) < chip

    @pl.when(visible)
    def _():
        if fresh:
            fill_terms(kv_ref, keys_ref, values_ref)
        run(len(heads), score, soften, gather if columns is None else gather_and_scale)

    @pl.when(jnp.logical_not(visible))
    def _():
        for n, g in enumerate(heads):
            finish(n, acc_ref[g, at], total_ref[g, at])
        if columns is not None:
            for block in range(2, 4):
                scale_rows(block)

    for each in copies:
        each.wait()


def last_stage(me, distance, whose, heads, kv, operands, after, extra=None):
    group, rows, _ = operands[0].shape
    tokens = rows // 2
    part = jax.ShapeDtypeStruct((tokens, len(heads) * HD), F32)
    fresh, columns, scratch = whose == "other", None, []
    operands = [kv, *operands] if fresh else [*kv, *operands]
    if extra is not None:
        columns, more = extra
        operands = [*operands, *more]
        linear = more[-1]
        out_shape = [
            jax.ShapeDtypeStruct(linear.shape, F32),
            jax.ShapeDtypeStruct((tokens, 2 * group * HD), F32),
        ]
        out_spec = [HBM] * 2
        scratch = [
            pltpu.VMEM(linear.shape, F32),
            pltpu.VMEM(part.shape, F32),
            pltpu.SemaphoreType.DMA((12 + len(heads),)),
        ]
    else:
        out_shape = [part] + (term_shapes(kv.shape[1]) if fresh else [])
        out_spec = [VMEM] * len(out_shape)
    return call(
        functools.partial(last_kernel, distance, whose, heads, columns),
        [SMEM] + [VMEM] * len(operands),
        out_spec,
        out_shape,
        scratch,
        after=after,
    )(me, *operands)


def plus_kernel(a_ref, b_ref, out_ref):
    out_ref[...] = a_ref[...] + b_ref[...]


def plus(a, b, after):
    return call(
        plus_kernel, [VMEM] * 2, VMEM, jax.ShapeDtypeStruct(a.shape, F32), after=after
    )(a, b)


def copy_kernel(source_ref, out_ref):
    out_ref[...] = source_ref[...]


def copied(array, after):
    return call(copy_kernel, [VMEM], VMEM, jax.ShapeDtypeStruct(array.shape, F32), after=after)(
        array
    )


def relay_kernel(me_ref, own_ref, across_ref, out_ref):
    @pl.when((me_ref[0] & 1) == 0)
    def _():
        out_ref[...] = own_ref[...]

    @pl.when((me_ref[0] & 1) == 1)
    def _():
        out_ref[...] = across_ref[...]


def relayed(me, own, across, after):
    return call(
        relay_kernel,
        [SMEM, VMEM, VMEM],
        VMEM,
        jax.ShapeDtypeStruct(own.shape, F32),
        after=after,
    )(me, own, across)


def body(q_lin, k_lin, v_lin, log_decay, lin_gain, q_soft, k_soft, v_soft):
    chips = lax.axis_size("ctx") // 2
    heads = lax.axis_size("head")
    me = lax.axis_index("ctx")
    me_flag = me.reshape(1).astype(jnp.int32)
    assert k_soft.shape[1] == 2 * HD
    swap_pairs = [(2 * c + e, 2 * c + 1 - e) for c in range(chips) for e in range(2)]

    def swap(array):
        return lax.ppermute(array, "ctx", swap_pairs)

    def across(array, distance, wanted=lambda c, e: True):
        pairs = [
            (2 * (c ^ distance) + e, 2 * c + e)
            for c in range(chips)
            for e in range(2)
            if wanted(c, e)
        ]
        return lax.ppermute(array, "ctx", pairs)

    square = chips == 4
    kv_mine, kv_send = halves(me & 1, k_soft, v_soft)
    kv_other = swap(kv_send)
    states, sums = local_states(log_decay, k_lin, v_lin, [kv_mine])
    others = swap(states)
    kv, q_send = pair_block(me_flag, kv_mine, kv_other, q_soft, [sums])
    q_other = swap(q_send)
    total, prefix = chip_total(me_flag, states, others, [q_send]), None
    inside, terms = inside_blocks(q_lin, k_lin, v_lin, sums, [total])

    def exchanged(array, step):
        return lax.ppermute(array, "head", [(i, i ^ step) for i in range(heads)])

    def sent(distance, array):
        return across(array, distance, lambda c, e: c ^ distance < c)

    def stage(kv, distance, heads, carried, after):
        return later_stage(me_flag, distance, heads, kv, q_terms, *carried, after)

    bits = chips.bit_length() - 1
    arrived, token = {}, inside
    if square:
        arrived[2] = sent(2, kv)
        token = copied(kv, [inside])
        arrived[1] = sent(1, token)
    else:
        for distance in range(1, chips):
            arrived[distance] = sent(distance, kv)
    q_terms, *carried = own_stage(me_flag, q_soft, q_other, kv, [token])
    group = q_terms.shape[0]
    all_heads, front, back = range(group), range(group // 2), range(group // 2, group)
    token = carried[0]
    if square:
        relay = relayed(me_flag, kv, arrived[2], [token])
        arrived[3] = lax.ppermute(relay, "ctx", [(0, 6), (2, 4), (5, 7), (7, 5)])
    for bit in range(bits):
        last = bit == bits - 1
        theirs = across(total, 1 << bit, lambda c, e: not last or c ^ (1 << bit) < c)
        prefix, total = turn(me_flag, bit, total, theirs, prefix, last, [token] + ([arrived[1]] if square and last else []))
        distance = 2 if square else bit + 1
        if not (square and last):
            waits = [prefix, relay] if square else [prefix]
            carried, _ = stage(arrived[distance], distance, all_heads, carried, waits)
            token = carried[0]
    prefix_other = swap(prefix)
    left = [1] if square else range(bits + 1, chips - 1)
    for distance in left[:-1]:
        carried, _ = stage(arrived[distance], distance, all_heads, carried, [prefix])
    carried, kept = stage(arrived[left[-1]], left[-1], front, carried, [prefix])
    linear, energy = linear_blocks(
        me_flag, terms, inside, sums, prefix, prefix_other, others, [carried[0]]
    )
    energies, step = [], 1
    while step < heads:
        energies.append(step)
        step *= 2
    other = exchanged(energy, energies[0])
    carried, _ = stage(kept, left[-1], back, carried, [energy])
    operands = [q_terms, *carried]
    for step in energies[1:]:
        energy = plus(energy, other, [carried[0]])
        other = exchanged(energy, step)

    theirs, *kept = last_stage(
        me_flag, chips - 1, "other", all_heads, arrived[chips - 1], operands, [energy]
    )
    (done,) = last_stage(me_flag, chips - 1, "own", front, kept, operands, [])
    columns = q_lin.shape[1] * heads
    more = [swap(theirs), done, energy, other, lin_gain.reshape(1, -1), linear]
    return tuple(
        last_stage(me_flag, chips - 1, "own", back, kept, operands, [], (columns, more))
    )


def solution(mesh):
    return jax.shard_map(
        body,
        mesh=mesh,
        in_specs=(
            P("ctx", "head"),
            P("ctx", "head"),
            P("ctx", "head"),
            P("head", "ctx"),
            P("head"),
            P("ctx", "head"),
            P("ctx", "head"),
            P("ctx", "head"),
        ),
        out_specs=(P("ctx", "head"), P("ctx", "head")),
        check_vma=False,
    )
```

```python
import functools
import math

import jax
import jax.numpy as jnp
from jax import lax
from jax.experimental import pallas as pl
from jax.experimental.pallas import tpu as pltpu
from jax.sharding import PartitionSpec as P

HD = 128
NEGATIVE = -1e30
EPSILON = 1e-05
ENERGY_ROWS = 16
F32 = jnp.float32
BF16 = jnp.bfloat16
NT = (((1,), (1,)), ((), ()))
VMEM_LIMIT = 32 * 1024 * 1024
VMEM = pl.BlockSpec(memory_space=pltpu.VMEM)
SMEM = pl.BlockSpec(memory_space=pltpu.SMEM)
ANY = pl.BlockSpec(memory_space=pl.ANY)
HBM = pl.BlockSpec(memory_space=pltpu.HBM)


def split(x):
    high = x.astype(BF16)
    low = (x - high.astype(F32)).astype(BF16)
    return high, low


def dot(a, b):
    return jnp.dot(a, b, preferred_element_type=F32)


def three_term(a, b):
    a_high, a_low = split(a)
    b_high, b_low = split(b)
    wide = dot(a_high, jnp.concatenate([b_high, b_low], axis=1))
    n = b.shape[1]
    return wide[:, :n] + wide[:, n:] + dot(a_low, b_high)


def call(kernel, in_specs, out_specs, out_shape, scratch=(), alias=None, after=()):
    count = len(in_specs)

    def ordered(*refs):
        kernel(*refs[:count], *refs[count + len(after) :])

    made = pl.pallas_call(
        ordered,
        in_specs=in_specs + [ANY] * len(after),
        out_specs=out_specs,
        out_shape=out_shape,
        scratch_shapes=list(scratch),
        input_output_aliases=alias or {},
        cost_estimate=pl.CostEstimate(flops=1, bytes_accessed=1, transcendentals=0),
        compiler_params=pltpu.CompilerParams(vmem_limit_bytes=VMEM_LIMIT),
    )
    return lambda *operands: made(*operands, *after)


def state_kernel(rate_ref, k_ref, v_ref, packed_ref, sums_ref):
    tokens = k_ref.shape[0]
    heads = rate_ref.shape[0]
    half = heads // 2
    upto = lax.broadcasted_iota(jnp.int32, (tokens, tokens), 0)
    upto = (upto <= lax.broadcasted_iota(jnp.int32, (tokens, tokens), 1)).astype(F32)
    sums = jnp.dot(
        rate_ref[...], upto, precision=lax.Precision.HIGHEST, preferred_element_type=F32
    )
    sums_ref[...] = sums
    totals = sums[:, tokens - 1 : tokens]
    trailing = jnp.exp(totals - sums)
    for side in range(2):
        packed_ref[side, half * HD :] = jnp.zeros((8, HD), F32)
    for h in range(heads):
        side, i = h // half, h % half
        at = slice(h * HD, (h + 1) * HD)
        packed_ref[side, i * HD : (i + 1) * HD] = three_term(
            k_ref[:, at].T * trailing[h : h + 1], v_ref[:, at]
        )
        packed_ref[side, half * HD + i : half * HD + i + 1] = jnp.broadcast_to(
            totals[h : h + 1], (1, HD)
        )


def local_states(rates, k_lin, v_lin, after):
    tokens = k_lin.shape[0]
    heads = rates.shape[0]
    return call(
        state_kernel,
        [VMEM] * 3,
        [VMEM] * 2,
        [
            jax.ShapeDtypeStruct((2, heads // 2 * HD + 8, HD), F32),
            jax.ShapeDtypeStruct((heads, tokens), F32),
        ],
        after=after,
    )(rates, k_lin, v_lin)


def join(half, first, second, out_ref):
    decay = jnp.exp(second[half * HD :, :])
    for i in range(half):
        at = slice(i * HD, (i + 1) * HD)
        out_ref[at] = first[at] * decay[i : i + 1] + second[at]
    out_ref[half * HD :] = first[half * HD :] + second[half * HD :]


def chip_kernel(half, me_ref, states_ref, others_ref, out_ref):
    core = me_ref[0] & 1

    @pl.when(core == 0)
    def _():
        join(half, states_ref[0], others_ref[0], out_ref)

    @pl.when(core == 1)
    def _():
        join(half, others_ref[1], states_ref[1], out_ref)


def chip_total(me, states, others, after):
    _, packed, _ = states.shape
    return call(
        functools.partial(chip_kernel, (packed - 8) // HD),
        [SMEM, VMEM, VMEM],
        VMEM,
        jax.ShapeDtypeStruct((packed, HD), F32),
        after=after,
    )(me, states, others)


def turn_kernel(half, bit, first, last, me_ref, total_ref, theirs_ref, *refs):
    refs = list(refs)
    before_ref = None if first else refs.pop(0)
    prefix_ref = refs.pop(0)
    total_out = None if last else refs.pop(0)
    late = (me_ref[0] >> (bit + 1)) & 1

    @pl.when(late == 0)
    def _():
        prefix_ref[...] = jnp.zeros_like(prefix_ref) if first else before_ref[...]
        if not last:
            join(half, total_ref[...], theirs_ref[...], total_out)

    @pl.when(late == 1)
    def _():
        if first:
            prefix_ref[...] = theirs_ref[...]
        else:
            join(half, theirs_ref[...], before_ref[...], prefix_ref)
        if not last:
            join(half, theirs_ref[...], total_ref[...], total_out)


def turn(me, bit, total, theirs, before, last, after):
    packed = total.shape[0]
    operands = [total, theirs] + ([] if before is None else [before])
    count = 1 if last else 2
    out = call(
        functools.partial(turn_kernel, (packed - 8) // HD, bit, before is None, last),
        [SMEM] + [VMEM] * len(operands),
        [VMEM] * count,
        [jax.ShapeDtypeStruct((packed, HD), F32)] * count,
        after=after,
    )(me, *operands)
    return out[0], (None if last else out[1])


def inside_kernel(q_ref, k_ref, v_ref, sums_ref, out_ref, terms_ref):
    tokens = q_ref.shape[0]
    heads = sums_ref.shape[0]
    causal = lax.broadcasted_iota(jnp.int32, (tokens, tokens), 0) >= lax.broadcasted_iota(
        jnp.int32, (tokens, tokens), 1
    )
    columns = sums_ref[...].T
    for h in range(heads):
        at = slice(h * HD, (h + 1) * HD)
        q_high, q_low = split(q_ref[:, at])
        k_high, k_low = split(k_ref[:, at])
        terms_ref[h, :, :HD] = q_high
        terms_ref[h, :, HD:] = q_low
        scores = lax.dot_general(
            jnp.concatenate([q_high, q_low, q_high], axis=1),
            jnp.concatenate([k_high, k_high, k_low], axis=1),
            NT,
            preferred_element_type=F32,
        )
        gaps = columns[:, h : h + 1] - sums_ref[h : h + 1, :]
        weights = jnp.where(causal, jnp.exp(jnp.where(causal, gaps, 0.0)), 0.0)
        out_ref[h] = three_term(scores * weights, v_ref[:, at])


def inside_blocks(q_lin, k_lin, v_lin, sums, after):
    tokens = q_lin.shape[0]
    heads = sums.shape[0]
    return call(
        inside_kernel,
        [VMEM] * 4,
        [VMEM] * 2,
        [
            jax.ShapeDtypeStruct((heads, tokens, HD), F32),
            jax.ShapeDtypeStruct((heads, tokens, 2 * HD), BF16),
        ],
        after=after,
    )(q_lin, k_lin, v_lin, sums)


def linear_kernel(me_ref, terms_ref, inside_ref, sums_ref, mine_ref, theirs_ref, other_ref, out_ref, energy_ref):
    heads, tokens, _ = inside_ref.shape
    half = heads // 2
    core = me_ref[0] & 1
    leading = jnp.exp(sums_ref[...]).T
    squares = jnp.zeros((tokens, HD), F32)
    for side in range(2):
        decay = jnp.exp(other_ref[side, half * HD :])
        for i in range(half):
            h = side * half + i
            at = slice(i * HD, (i + 1) * HD)
            prior = jnp.where(core == side, mine_ref[at], theirs_ref[at])
            prior = jnp.where(core == 1, prior * decay[i : i + 1] + other_ref[side, at], prior)
            high, low = split(prior)
            carried = dot(
                score_terms(terms_ref[h]), jnp.concatenate([high, high, low], axis=0)
            )
            linear = inside_ref[h] + leading[:, h : h + 1] * carried
            out_ref[:, h * HD : (h + 1) * HD] = linear
            squares = squares + linear * linear
    energy_ref[...] = lax.dot_general(
        jnp.ones((energy_ref.shape[0], HD), F32),
        squares,
        NT,
        precision=lax.Precision.HIGHEST,
        preferred_element_type=F32,
    )


def linear_blocks(me, terms, inside, sums, mine, theirs, other, after):
    heads, tokens, _ = inside.shape
    return call(
        linear_kernel,
        [SMEM] + [VMEM] * 6,
        [VMEM] * 2,
        [
            jax.ShapeDtypeStruct((tokens, heads * HD), F32),
            jax.ShapeDtypeStruct((ENERGY_ROWS, tokens), F32),
        ],
        after=after,
    )(me, terms, inside, sums, mine, theirs, other)


def halves(core, *arrays):
    early = [array[:, :HD] for array in arrays]
    late = [array[:, HD:] for array in arrays]
    mine = jnp.stack([jnp.where(core == 0, a, b) for a, b in zip(early, late)])
    theirs = jnp.stack([jnp.where(core == 0, b, a) for a, b in zip(early, late)])
    return mine, theirs


def pair_kernel(me_ref, mine_ref, other_ref, q_ref, out_ref, send_ref):
    tokens = mine_ref.shape[1]
    group = send_ref.shape[0]
    core = me_ref[0] & 1
    first = core == 0
    for side in range(2):
        mine, other = mine_ref[side], other_ref[side]
        out_ref[side, :tokens] = jnp.where(first, mine, other)
        out_ref[side, tokens:] = jnp.where(first, other, mine)
    for g in range(group):
        at = pl.ds(pl.multiple_of(((1 - core) * group + g) * HD, HD), HD)
        send_ref[g] = q_ref[:, at]


def pair_block(me, mine, other, q_soft, after):
    _, tokens, _ = mine.shape
    group = q_soft.shape[1] // (2 * HD)
    return call(
        pair_kernel,
        [SMEM] + [VMEM] * 3,
        [VMEM] * 2,
        [
            jax.ShapeDtypeStruct((2, 2 * tokens, HD), F32),
            jax.ShapeDtypeStruct((group, tokens, HD), F32),
        ],
        after=after,
    )(me, mine, other, q_soft)


def run(count, score, soften, gather):
    scores, before = score(0), None
    for i in range(count):
        following = score(i + 1) if i + 1 < count else None
        if before is not None:
            gather(i - 1, before)
        before = soften(i, scores)
        scores = following
    gather(count - 1, before)


def fill_terms(kv_ref, keys_ref, values_ref):
    k_high, k_low = split(kv_ref[0].T)
    keys_ref[:HD] = k_high
    keys_ref[HD : 2 * HD] = k_high
    keys_ref[2 * HD :] = k_low
    v_high, v_low = split(kv_ref[1])
    values_ref[:, :HD] = v_high
    values_ref[:, HD:] = v_low


def lane_max(array):
    peak = array[:, :HD]
    for c in range(1, array.shape[1] // HD):
        peak = jnp.maximum(peak, array[:, c * HD : (c + 1) * HD])
    return peak


def score_terms(pair):
    return jnp.concatenate([pair, pair[:, :HD]], axis=1)


def weigh(scores, peak, total):
    high, low = [], []
    for c in range(scores.shape[1] // HD):
        w = jnp.exp2(scores[:, c * HD : (c + 1) * HD] - peak)
        total = total + w
        pair = split(w)
        high.append(pair[0])
        low.append(pair[1])
    return jnp.concatenate(high, axis=1), jnp.concatenate(low, axis=1), total


def summed(high, low, values):
    wide = dot(high, values)
    return wide[:, :HD] + wide[:, HD:] + dot(low, values[:, :HD])


def own_kernel(factor, me_ref, q_ref, q_other_ref, kv_ref, q_out, acc_out, peak_out, total_out, keys_ref, values_ref):
    group, tokens = q_out.shape[0], q_ref.shape[0]
    core = me_ref[0] & 1
    first = core == 0
    fill_terms(kv_ref, keys_ref, values_ref)
    seen = lax.broadcasted_iota(jnp.int32, (tokens, tokens), 1)
    seen = seen <= lax.broadcasted_iota(jnp.int32, (tokens, tokens), 0)

    def where(i):
        t = i % 2
        return i // 2, slice(t * tokens, (t + 1) * tokens), slice(0, (t + 1) * tokens)

    def score(i):
        g, rows, keys = where(i)
        at = pl.ds(pl.multiple_of((core * group + g) * HD, HD), HD)
        mine, other = q_ref[:, at], q_other_ref[g]
        queries = jnp.where(first, mine, other) if i % 2 == 0 else jnp.where(first, other, mine)
        pair = jnp.concatenate(split(queries * factor), axis=1)
        q_out[g, rows] = pair
        s = dot(score_terms(pair), keys_ref[:, keys])
        edge = jnp.where(seen, s[:, rows], NEGATIVE)
        return edge if i % 2 == 0 else jnp.concatenate([s[:, :tokens], edge], axis=1)

    def soften(i, s):
        g, rows, _ = where(i)
        peak = jnp.max(lane_max(s), axis=1, keepdims=True)
        peak_out[g, rows] = jnp.broadcast_to(peak, (tokens, HD))
        high, low, total_out[g, rows] = weigh(s, peak, jnp.zeros((tokens, HD), F32))
        return high, low

    def gather(i, terms):
        g, rows, keys = where(i)
        acc_out[g, rows] = summed(*terms, values_ref[keys])

    run(2 * group, score, soften, gather)


def term_scratch(keys):
    return [pltpu.VMEM((3 * HD, keys), BF16), pltpu.VMEM((keys, 2 * HD), BF16)]


def own_stage(me, q_soft, q_other, kv, after):
    tokens, width = q_soft.shape
    group = width // (2 * HD)
    stat = jax.ShapeDtypeStruct((group, 2 * tokens, HD), F32)
    return call(
        functools.partial(own_kernel, math.log2(math.e) / math.sqrt(HD)),
        [SMEM] + [VMEM] * 3,
        [VMEM] * 4,
        [jax.ShapeDtypeStruct((group, 2 * tokens, 2 * HD), BF16), stat, stat, stat],
        term_scratch(2 * tokens),
        after=after,
    )(me, q_soft, q_other, kv)


def later_kernel(distance, parts, heads, fresh, me_ref, *refs):
    if fresh:
        kv_ref, q_ref, acc_ref, peak_ref, total_ref = refs[:5]
        acc_out, peak_out, total_out, keys_ref, values_ref = refs[5:]
    else:
        keys_ref, values_ref, q_ref, acc_ref, peak_ref, total_ref = refs[:6]
        acc_out, peak_out, total_out = refs[6:]
    size = q_ref.shape[1] // parts
    chip = me_ref[0] >> 1

    def where(i):
        return heads[i // parts], slice(i % parts * size, (i % parts + 1) * size)

    def score(i):
        return dot(score_terms(q_ref[where(i)]), keys_ref[...])

    def soften(i, s):
        at = where(i)
        old = peak_ref[at]
        peak = jnp.maximum(jnp.max(lane_max(s), axis=1, keepdims=True), old)
        shrink = jnp.exp2(old - peak)
        peak_out[at] = peak
        high, low, total_out[at] = weigh(s, peak, total_ref[at] * shrink)
        return high, low, shrink

    def gather(i, terms):
        at = where(i)
        acc_out[at] = acc_ref[at] * terms[2] + summed(*terms[:2], values_ref[...])

    @pl.when(lax.bitwise_xor(chip, distance) < chip)
    def _():
        if fresh:
            fill_terms(kv_ref, keys_ref, values_ref)
        run(parts * len(heads), score, soften, gather)


def term_shapes(keys):
    return [
        jax.ShapeDtypeStruct((3 * HD, keys), BF16),
        jax.ShapeDtypeStruct((keys, 2 * HD), BF16),
    ]


def later_stage(me, distance, heads, kv, q_terms, acc, peak, total, after, keep, parts=4):
    fresh = not isinstance(kv, tuple)
    operands = [kv] if fresh else list(kv)
    shift = 1 + len(operands)
    out_shape = [jax.ShapeDtypeStruct(acc.shape, F32)] * 3
    scratch = []
    if fresh and keep:
        out_shape += term_shapes(kv.shape[1])
    elif fresh:
        scratch = [pltpu.VMEM(each.shape, each.dtype) for each in term_shapes(kv.shape[1])]
    out = call(
        functools.partial(later_kernel, distance, parts, heads, fresh),
        [SMEM] + [VMEM] * (len(operands) + 4),
        [VMEM] * len(out_shape),
        out_shape,
        scratch,
        alias={shift + 1: 0, shift + 2: 1, shift + 3: 2},
        after=after,
    )(me, *operands, q_terms, acc, peak, total)
    return out[:3], tuple(out[3:])


def last_kernel(distance, whose, heads, columns, me_ref, *refs):
    fresh = whose == "other"
    if fresh:
        kv_ref, q_ref, acc_ref, peak_ref, total_ref, out_ref, keys_ref, values_ref = refs
    else:
        keys_ref, values_ref, q_ref, acc_ref, peak_ref, total_ref, *refs = refs
    if columns is not None:
        theirs_ref, done_ref, energy_ref, energy_other_ref, gain_ref, linear_ref = refs[:6]
        lin_hbm, soft_hbm, lin_ref, out_ref, sems = refs[6:]
    elif not fresh:
        (out_ref,) = refs
    group, rows, _ = q_ref.shape
    tokens = rows // 2
    core, chip = me_ref[0] & 1, me_ref[0] >> 1
    side = core if whose == "own" else 1 - core
    at = pl.ds(pl.multiple_of(side * tokens, tokens), tokens)
    copies = []

    def copy(source, target):
        copies.append(pltpu.make_async_copy(source, target, sems.at[len(copies)]))
        return copies[-1]

    def columns_of(whose, g, count):
        return pl.ds(pl.multiple_of((whose * group + g) * HD, HD), count * HD)

    if columns is not None:
        blocks = [pl.ds(n * (tokens // 4), tokens // 4) for n in range(4)]
        for block in blocks:
            to = soft_hbm.at[block, columns_of(1 - core, 0, group)]
            copy(theirs_ref.at[block], to).start()
        factor = lax.rsqrt((energy_ref[:8] + energy_other_ref[:8]) / columns + EPSILON)
        factor = factor.T[:, 0:1]
        for block in blocks:
            to = soft_hbm.at[block, columns_of(core, 0, group - len(heads))]
            copy(done_ref.at[block], to).start()
        lin_copies = [copy(lin_ref.at[block], lin_hbm.at[block]) for block in blocks]
        own_copies = [
            copy(out_ref.at[:, pl.ds(n * HD, HD)], soft_hbm.at[:, columns_of(core, g, 1)])
            for n, g in enumerate(heads)
        ]

    def scale_rows(n):
        rows = slice(n * (tokens // 4), (n + 1) * (tokens // 4))
        lin_ref[rows] = linear_ref[rows] * factor[rows] * gain_ref[...]
        lin_copies[n].start()

    def finish(n, acc, total):
        out_ref[:, n * HD : (n + 1) * HD] = acc / jnp.sum(total, axis=1, keepdims=True)
        if columns is not None:
            own_copies[n].start()

    def score(n):
        return dot(score_terms(q_ref[heads[n], at]), keys_ref[...])

    def soften(n, s):
        old = peak_ref[heads[n], at]
        peak = jnp.maximum(jnp.max(lane_max(s), axis=1, keepdims=True), old)
        shrink = jnp.exp2(old - peak)
        return *weigh(s, peak, total_ref[heads[n], at] * shrink), shrink

    def gather(n, terms):
        high, low, total, shrink = terms
        new = summed(high, low, values_ref[...])
        finish(n, acc_ref[heads[n], at] * shrink + new, total)

    def gather_and_scale(n, terms):
        gather(n, terms)
        if n == 0:
            for block in range(2, 4):
                scale_rows(block)

    if columns is not None:
        for block in range(2):
            scale_rows(block)
    visible = lax.bitwise_xor(chip, distance) < chip

    @pl.when(visible)
    def _():
        if fresh:
            fill_terms(kv_ref, keys_ref, values_ref)
        run(len(heads), score, soften, gather if columns is None else gather_and_scale)

    @pl.when(jnp.logical_not(visible))
    def _():
        for n, g in enumerate(heads):
            finish(n, acc_ref[g, at], total_ref[g, at])
        if columns is not None:
            for block in range(2, 4):
                scale_rows(block)

    for each in copies:
        each.wait()


def last_stage(me, distance, whose, heads, kv, operands, after, extra=None):
    group, rows, _ = operands[0].shape
    tokens = rows // 2
    part = jax.ShapeDtypeStruct((tokens, len(heads) * HD), F32)
    fresh, columns, scratch = whose == "other", None, []
    operands = [kv, *operands] if fresh else [*kv, *operands]
    if extra is not None:
        columns, more = extra
        operands = [*operands, *more]
        linear = more[-1]
        out_shape = [
            jax.ShapeDtypeStruct(linear.shape, F32),
            jax.ShapeDtypeStruct((tokens, 2 * group * HD), F32),
        ]
        out_spec = [HBM] * 2
        scratch = [
            pltpu.VMEM(linear.shape, F32),
            pltpu.VMEM(part.shape, F32),
            pltpu.SemaphoreType.DMA((12 + len(heads),)),
        ]
    else:
        out_shape = [part] + (term_shapes(kv.shape[1]) if fresh else [])
        out_spec = [VMEM] * len(out_shape)
    return call(
        functools.partial(last_kernel, distance, whose, heads, columns),
        [SMEM] + [VMEM] * len(operands),
        out_spec,
        out_shape,
        scratch,
        after=after,
    )(me, *operands)


def plus_kernel(a_ref, b_ref, out_ref):
    out_ref[...] = a_ref[...] + b_ref[...]


def plus(a, b, after):
    return call(
        plus_kernel, [VMEM] * 2, VMEM, jax.ShapeDtypeStruct(a.shape, F32), after=after
    )(a, b)


def copy_kernel(source_ref, out_ref):
    out_ref[...] = source_ref[...]


def copied(array, after):
    return call(copy_kernel, [VMEM], VMEM, jax.ShapeDtypeStruct(array.shape, F32), after=after)(
        array
    )


def relay_kernel(me_ref, own_ref, across_ref, out_ref):
    @pl.when((me_ref[0] & 1) == 0)
    def _():
        out_ref[...] = own_ref[...]

    @pl.when((me_ref[0] & 1) == 1)
    def _():
        out_ref[...] = across_ref[...]


def relayed(me, own, across, after):
    return call(
        relay_kernel,
        [SMEM, VMEM, VMEM],
        VMEM,
        jax.ShapeDtypeStruct(own.shape, F32),
        after=after,
    )(me, own, across)


def body(q_lin, k_lin, v_lin, log_decay, lin_gain, q_soft, k_soft, v_soft):
    chips = lax.axis_size("ctx") // 2
    heads = lax.axis_size("head")
    me = lax.axis_index("ctx")
    me_flag = me.reshape(1).astype(jnp.int32)
    assert k_soft.shape[1] == 2 * HD
    swap_pairs = [(2 * c + e, 2 * c + 1 - e) for c in range(chips) for e in range(2)]

    def swap(array):
        return lax.ppermute(array, "ctx", swap_pairs)

    def across(array, distance, wanted=lambda c, e: True):
        pairs = [
            (2 * (c ^ distance) + e, 2 * c + e)
            for c in range(chips)
            for e in range(2)
            if wanted(c, e)
        ]
        return lax.ppermute(array, "ctx", pairs)

    square = chips == 4
    kv_mine, kv_send = halves(me & 1, k_soft, v_soft)
    kv_other = swap(kv_send)
    states, sums = local_states(log_decay, k_lin, v_lin, [kv_mine])
    others = swap(states)
    kv, q_send = pair_block(me_flag, kv_mine, kv_other, q_soft, [sums])
    q_other = swap(q_send)
    total, prefix = chip_total(me_flag, states, others, [q_send]), None
    inside, terms = inside_blocks(q_lin, k_lin, v_lin, sums, [total])

    def exchanged(array, step):
        return lax.ppermute(array, "head", [(i, i ^ step) for i in range(heads)])

    def sent(distance, array):
        return across(array, distance, lambda c, e: c ^ distance < c)

    def stage(kv, distance, heads, carried, after, keep=False):
        return later_stage(me_flag, distance, heads, kv, q_terms, *carried, after, keep)

    bits = chips.bit_length() - 1
    arrived, token = {}, inside
    if square:
        arrived[2] = sent(2, kv)
        token = copied(kv, [inside])
        arrived[1] = sent(1, token)
    else:
        for distance in range(1, chips):
            arrived[distance] = sent(distance, kv)
    q_terms, *carried = own_stage(me_flag, q_soft, q_other, kv, [token])
    group = q_terms.shape[0]
    all_heads, front, back = range(group), range(group // 2), range(group // 2, group)
    token = carried[0]
    if square:
        relay = relayed(me_flag, kv, arrived[2], [token])
        arrived[3] = lax.ppermute(relay, "ctx", [(0, 6), (2, 4), (5, 7), (7, 5)])
    for bit in range(bits):
        last = bit == bits - 1
        theirs = across(total, 1 << bit, lambda c, e: not last or c ^ (1 << bit) < c)
        prefix, total = turn(me_flag, bit, total, theirs, prefix, last, [token] + ([arrived[1]] if square and last else []))
        distance = 2 if square else bit + 1
        if not (square and last):
            waits = [prefix, relay] if square else [prefix]
            carried, _ = stage(arrived[distance], distance, all_heads, carried, waits)
            token = carried[0]
    prefix_other = swap(prefix)
    left = [1] if square else range(bits + 1, chips - 1)
    for distance in left[:-1]:
        carried, _ = stage(arrived[distance], distance, all_heads, carried, [prefix])
    carried, kept = stage(arrived[left[-1]], left[-1], front, carried, [prefix], True)
    linear, energy = linear_blocks(
        me_flag, terms, inside, sums, prefix, prefix_other, others, [carried[0]]
    )
    energies, step = [], 1
    while step < heads:
        energies.append(step)
        step *= 2
    other = exchanged(energy, energies[0])
    carried, _ = stage(kept, left[-1], back, carried, [energy])
    operands = [q_terms, *carried]
    split_at = 2 * group // 3
    for step in energies[1:]:
        energy = plus(energy, other, [carried[0]])
        other = exchanged(energy, step)

    theirs, *kept = last_stage(
        me_flag, chips - 1, "other", all_heads, arrived[chips - 1], operands, [energy]
    )
    (done,) = last_stage(me_flag, chips - 1, "own", all_heads[:split_at], kept, operands, [])
    columns = q_lin.shape[1] * heads
    more = [swap(theirs), done, energy, other, lin_gain.reshape(1, -1), linear]
    return tuple(
        last_stage(me_flag, chips - 1, "own", all_heads[split_at:], kept, operands, [], (columns, more))
    )


def solution(mesh):
    return jax.shard_map(
        body,
        mesh=mesh,
        in_specs=(
            P("ctx", "head"),
            P("ctx", "head"),
            P("ctx", "head"),
            P("head", "ctx"),
            P("head"),
            P("ctx", "head"),
            P("ctx", "head"),
            P("ctx", "head"),
        ),
        out_specs=(P("ctx", "head"), P("ctx", "head")),
        check_vma=False,
    )
```

```python
import functools
import math

import jax
import jax.numpy as jnp
from jax import lax
from jax.experimental import pallas as pl
from jax.experimental.pallas import tpu as pltpu
from jax.sharding import PartitionSpec as P

HD = 128
NEGATIVE = -1e30
EPSILON = 1e-05
ENERGY_ROWS = 8
F32 = jnp.float32
BF16 = jnp.bfloat16
NT = (((1,), (1,)), ((), ()))
VMEM_LIMIT = 32 * 1024 * 1024
VMEM = pl.BlockSpec(memory_space=pltpu.VMEM)
SMEM = pl.BlockSpec(memory_space=pltpu.SMEM)
ANY = pl.BlockSpec(memory_space=pl.ANY)
HBM = pl.BlockSpec(memory_space=pltpu.HBM)


def split(x):
    high = x.astype(BF16)
    low = (x - high.astype(F32)).astype(BF16)
    return high, low


def dot(a, b):
    return jnp.dot(a, b, preferred_element_type=F32)


def three_term(a, b):
    a_high, a_low = split(a)
    b_high, b_low = split(b)
    wide = dot(a_high, jnp.concatenate([b_high, b_low], axis=1))
    n = b.shape[1]
    return wide[:, :n] + wide[:, n:] + dot(a_low, b_high)


def call(kernel, in_specs, out_specs, out_shape, scratch=(), alias=None, after=()):
    count = len(in_specs)

    def ordered(*refs):
        kernel(*refs[:count], *refs[count + len(after) :])

    made = pl.pallas_call(
        ordered,
        in_specs=in_specs + [ANY] * len(after),
        out_specs=out_specs,
        out_shape=out_shape,
        scratch_shapes=list(scratch),
        input_output_aliases=alias or {},
        cost_estimate=pl.CostEstimate(flops=1, bytes_accessed=1, transcendentals=0),
        compiler_params=pltpu.CompilerParams(vmem_limit_bytes=VMEM_LIMIT),
    )
    return lambda *operands: made(*operands, *after)


def state_kernel(rate_ref, k_ref, v_ref, packed_ref, sums_ref):
    tokens = k_ref.shape[0]
    heads = rate_ref.shape[0]
    half = heads // 2
    upto = lax.broadcasted_iota(jnp.int32, (tokens, tokens), 0)
    upto = (upto <= lax.broadcasted_iota(jnp.int32, (tokens, tokens), 1)).astype(F32)
    sums = jnp.dot(
        rate_ref[...], upto, precision=lax.Precision.HIGHEST, preferred_element_type=F32
    )
    sums_ref[...] = sums
    totals = sums[:, tokens - 1 : tokens]
    trailing = jnp.exp(totals - sums)
    for side in range(2):
        packed_ref[side, half * HD :] = jnp.zeros((8, HD), F32)
    for h in range(heads):
        side, i = h // half, h % half
        at = slice(h * HD, (h + 1) * HD)
        packed_ref[side, i * HD : (i + 1) * HD] = three_term(
            k_ref[:, at].T * trailing[h : h + 1], v_ref[:, at]
        )
        packed_ref[side, half * HD + i : half * HD + i + 1] = jnp.broadcast_to(
            totals[h : h + 1], (1, HD)
        )


def local_states(rates, k_lin, v_lin, after):
    tokens = k_lin.shape[0]
    heads = rates.shape[0]
    return call(
        state_kernel,
        [VMEM] * 3,
        [VMEM] * 2,
        [
            jax.ShapeDtypeStruct((2, heads // 2 * HD + 8, HD), F32),
            jax.ShapeDtypeStruct((heads, tokens), F32),
        ],
        after=after,
    )(rates, k_lin, v_lin)


def join(half, first, second, out_ref):
    decay = jnp.exp(second[half * HD :, :])
    for i in range(half):
        at = slice(i * HD, (i + 1) * HD)
        out_ref[at] = first[at] * decay[i : i + 1] + second[at]
    out_ref[half * HD :] = first[half * HD :] + second[half * HD :]


def chip_kernel(half, me_ref, states_ref, others_ref, out_ref):
    core = me_ref[0] & 1

    @pl.when(core == 0)
    def _():
        join(half, states_ref[0], others_ref[0], out_ref)

    @pl.when(core == 1)
    def _():
        join(half, others_ref[1], states_ref[1], out_ref)


def chip_total(me, states, others, after):
    _, packed, _ = states.shape
    return call(
        functools.partial(chip_kernel, (packed - 8) // HD),
        [SMEM, VMEM, VMEM],
        VMEM,
        jax.ShapeDtypeStruct((packed, HD), F32),
        after=after,
    )(me, states, others)


def turn_kernel(half, bit, first, last, me_ref, total_ref, theirs_ref, *refs):
    refs = list(refs)
    before_ref = None if first else refs.pop(0)
    prefix_ref = refs.pop(0)
    total_out = None if last else refs.pop(0)
    late = (me_ref[0] >> (bit + 1)) & 1

    @pl.when(late == 0)
    def _():
        prefix_ref[...] = jnp.zeros_like(prefix_ref) if first else before_ref[...]
        if not last:
            join(half, total_ref[...], theirs_ref[...], total_out)

    @pl.when(late == 1)
    def _():
        if first:
            prefix_ref[...] = theirs_ref[...]
        else:
            join(half, theirs_ref[...], before_ref[...], prefix_ref)
        if not last:
            join(half, theirs_ref[...], total_ref[...], total_out)


def turn(me, bit, total, theirs, before, last, after):
    packed = total.shape[0]
    operands = [total, theirs] + ([] if before is None else [before])
    count = 1 if last else 2
    out = call(
        functools.partial(turn_kernel, (packed - 8) // HD, bit, before is None, last),
        [SMEM] + [VMEM] * len(operands),
        [VMEM] * count,
        [jax.ShapeDtypeStruct((packed, HD), F32)] * count,
        after=after,
    )(me, *operands)
    return out[0], (None if last else out[1])


def inside_kernel(q_ref, k_ref, v_ref, sums_ref, out_ref, terms_ref):
    tokens = q_ref.shape[0]
    heads = sums_ref.shape[0]
    causal = lax.broadcasted_iota(jnp.int32, (tokens, tokens), 0) >= lax.broadcasted_iota(
        jnp.int32, (tokens, tokens), 1
    )
    columns = sums_ref[...].T
    for h in range(heads):
        at = slice(h * HD, (h + 1) * HD)
        q_high, q_low = split(q_ref[:, at])
        k_high, k_low = split(k_ref[:, at])
        terms_ref[h, :, :HD] = q_high
        terms_ref[h, :, HD:] = q_low
        scores = lax.dot_general(
            jnp.concatenate([q_high, q_low, q_high], axis=1),
            jnp.concatenate([k_high, k_high, k_low], axis=1),
            NT,
            preferred_element_type=F32,
        )
        gaps = columns[:, h : h + 1] - sums_ref[h : h + 1, :]
        weights = jnp.where(causal, jnp.exp(jnp.where(causal, gaps, 0.0)), 0.0)
        out_ref[h] = three_term(scores * weights, v_ref[:, at])


def inside_blocks(q_lin, k_lin, v_lin, sums, after):
    tokens = q_lin.shape[0]
    heads = sums.shape[0]
    return call(
        inside_kernel,
        [VMEM] * 4,
        [VMEM] * 2,
        [
            jax.ShapeDtypeStruct((heads, tokens, HD), F32),
            jax.ShapeDtypeStruct((heads, tokens, 2 * HD), BF16),
        ],
        after=after,
    )(q_lin, k_lin, v_lin, sums)


def linear_kernel(me_ref, terms_ref, inside_ref, sums_ref, mine_ref, theirs_ref, other_ref, out_ref, energy_ref):
    heads, tokens, _ = inside_ref.shape
    half = heads // 2
    core = me_ref[0] & 1
    leading = jnp.exp(sums_ref[...]).T
    squares = jnp.zeros((tokens, HD), F32)
    for side in range(2):
        decay = jnp.exp(other_ref[side, half * HD :])
        for i in range(half):
            h = side * half + i
            at = slice(i * HD, (i + 1) * HD)
            prior = jnp.where(core == side, mine_ref[at], theirs_ref[at])
            prior = jnp.where(core == 1, prior * decay[i : i + 1] + other_ref[side, at], prior)
            high, low = split(prior)
            carried = dot(
                score_terms(terms_ref[h]), jnp.concatenate([high, high, low], axis=0)
            )
            linear = inside_ref[h] + leading[:, h : h + 1] * carried
            out_ref[:, h * HD : (h + 1) * HD] = linear
            squares = squares + linear * linear
    energy_ref[...] = lax.dot_general(
        jnp.ones((energy_ref.shape[0], HD), F32),
        squares,
        NT,
        precision=lax.Precision.HIGHEST,
        preferred_element_type=F32,
    )


def linear_blocks(me, terms, inside, sums, mine, theirs, other, after):
    heads, tokens, _ = inside.shape
    return call(
        linear_kernel,
        [SMEM] + [VMEM] * 6,
        [VMEM] * 2,
        [
            jax.ShapeDtypeStruct((tokens, heads * HD), F32),
            jax.ShapeDtypeStruct((ENERGY_ROWS, tokens), F32),
        ],
        after=after,
    )(me, terms, inside, sums, mine, theirs, other)


def halves(core, *arrays):
    early = [array[:, :HD] for array in arrays]
    late = [array[:, HD:] for array in arrays]
    mine = jnp.stack([jnp.where(core == 0, a, b) for a, b in zip(early, late)])
    theirs = jnp.stack([jnp.where(core == 0, b, a) for a, b in zip(early, late)])
    return mine, theirs


def pair_kernel(me_ref, mine_ref, other_ref, q_ref, out_ref, send_ref):
    tokens = mine_ref.shape[1]
    group = send_ref.shape[0]
    core = me_ref[0] & 1
    first = core == 0
    for side in range(2):
        mine, other = mine_ref[side], other_ref[side]
        out_ref[side, :tokens] = jnp.where(first, mine, other)
        out_ref[side, tokens:] = jnp.where(first, other, mine)
    for g in range(group):
        at = pl.ds(pl.multiple_of(((1 - core) * group + g) * HD, HD), HD)
        send_ref[g] = q_ref[:, at]


def pair_block(me, mine, other, q_soft, after):
    _, tokens, _ = mine.shape
    group = q_soft.shape[1] // (2 * HD)
    return call(
        pair_kernel,
        [SMEM] + [VMEM] * 3,
        [VMEM] * 2,
        [
            jax.ShapeDtypeStruct((2, 2 * tokens, HD), F32),
            jax.ShapeDtypeStruct((group, tokens, HD), F32),
        ],
        after=after,
    )(me, mine, other, q_soft)


def run(count, score, soften, gather):
    scores, before = score(0), None
    for i in range(count):
        following = score(i + 1) if i + 1 < count else None
        if before is not None:
            gather(i - 1, before)
        before = soften(i, scores)
        scores = following
    gather(count - 1, before)


def fill_terms(kv_ref, keys_ref, values_ref):
    k_high, k_low = split(kv_ref[0].T)
    keys_ref[:HD] = k_high
    keys_ref[HD : 2 * HD] = k_high
    keys_ref[2 * HD :] = k_low
    v_high, v_low = split(kv_ref[1])
    values_ref[:, :HD] = v_high
    values_ref[:, HD:] = v_low


def lane_max(array):
    peak = array[:, :HD]
    for c in range(1, array.shape[1] // HD):
        peak = jnp.maximum(peak, array[:, c * HD : (c + 1) * HD])
    return peak


def score_terms(pair):
    return jnp.concatenate([pair, pair[:, :HD]], axis=1)


def weigh(scores, peak, total):
    high, low = [], []
    for c in range(scores.shape[1] // HD):
        w = jnp.exp2(scores[:, c * HD : (c + 1) * HD] - peak)
        total = total + w
        pair = split(w)
        high.append(pair[0])
        low.append(pair[1])
    return jnp.concatenate(high, axis=1), jnp.concatenate(low, axis=1), total


def summed(high, low, values):
    wide = dot(high, values)
    return wide[:, :HD] + wide[:, HD:] + dot(low, values[:, :HD])


def own_kernel(factor, me_ref, q_ref, q_other_ref, kv_ref, q_out, acc_out, peak_out, total_out, keys_ref, values_ref):
    group, tokens = q_out.shape[0], q_ref.shape[0]
    core = me_ref[0] & 1
    first = core == 0
    fill_terms(kv_ref, keys_ref, values_ref)
    seen = lax.broadcasted_iota(jnp.int32, (tokens, tokens), 1)
    seen = seen <= lax.broadcasted_iota(jnp.int32, (tokens, tokens), 0)

    def where(i):
        t = i % 2
        return i // 2, slice(t * tokens, (t + 1) * tokens), slice(0, (t + 1) * tokens)

    def score(i):
        g, rows, keys = where(i)
        at = pl.ds(pl.multiple_of((core * group + g) * HD, HD), HD)
        mine, other = q_ref[:, at], q_other_ref[g]
        queries = jnp.where(first, mine, other) if i % 2 == 0 else jnp.where(first, other, mine)
        pair = jnp.concatenate(split(queries * factor), axis=1)
        q_out[g, rows] = pair
        s = dot(score_terms(pair), keys_ref[:, keys])
        edge = jnp.where(seen, s[:, rows], NEGATIVE)
        return edge if i % 2 == 0 else jnp.concatenate([s[:, :tokens], edge], axis=1)

    def soften(i, s):
        g, rows, _ = where(i)
        peak = jnp.max(lane_max(s), axis=1, keepdims=True)
        peak_out[g, rows] = jnp.broadcast_to(peak, (tokens, HD))
        high, low, total_out[g, rows] = weigh(s, peak, jnp.zeros((tokens, HD), F32))
        return high, low

    def gather(i, terms):
        g, rows, keys = where(i)
        acc_out[g, rows] = summed(*terms, values_ref[keys])

    run(2 * group, score, soften, gather)


def term_scratch(keys):
    return [pltpu.VMEM((3 * HD, keys), BF16), pltpu.VMEM((keys, 2 * HD), BF16)]


def own_stage(me, q_soft, q_other, kv, after):
    tokens, width = q_soft.shape
    group = width // (2 * HD)
    stat = jax.ShapeDtypeStruct((group, 2 * tokens, HD), F32)
    return call(
        functools.partial(own_kernel, math.log2(math.e) / math.sqrt(HD)),
        [SMEM] + [VMEM] * 3,
        [VMEM] * 4,
        [jax.ShapeDtypeStruct((group, 2 * tokens, 2 * HD), BF16), stat, stat, stat],
        term_scratch(2 * tokens),
        after=after,
    )(me, q_soft, q_other, kv)


def later_kernel(distance, parts, heads, fresh, me_ref, *refs):
    if fresh:
        kv_ref, q_ref, acc_ref, peak_ref, total_ref = refs[:5]
        acc_out, peak_out, total_out, keys_ref, values_ref = refs[5:]
    else:
        keys_ref, values_ref, q_ref, acc_ref, peak_ref, total_ref = refs[:6]
        acc_out, peak_out, total_out = refs[6:]
    size = q_ref.shape[1] // parts
    chip = me_ref[0] >> 1

    def where(i):
        return heads[i // parts], slice(i % parts * size, (i % parts + 1) * size)

    def score(i):
        return dot(score_terms(q_ref[where(i)]), keys_ref[...])

    def soften(i, s):
        at = where(i)
        old = peak_ref[at]
        peak = jnp.maximum(jnp.max(lane_max(s), axis=1, keepdims=True), old)
        shrink = jnp.exp2(old - peak)
        peak_out[at] = peak
        high, low, total_out[at] = weigh(s, peak, total_ref[at] * shrink)
        return high, low, shrink

    def gather(i, terms):
        at = where(i)
        acc_out[at] = acc_ref[at] * terms[2] + summed(*terms[:2], values_ref[...])

    @pl.when(lax.bitwise_xor(chip, distance) < chip)
    def _():
        if fresh:
            fill_terms(kv_ref, keys_ref, values_ref)
        run(parts * len(heads), score, soften, gather)


def term_shapes(keys):
    return [
        jax.ShapeDtypeStruct((3 * HD, keys), BF16),
        jax.ShapeDtypeStruct((keys, 2 * HD), BF16),
    ]


def later_stage(me, distance, heads, kv, q_terms, acc, peak, total, after, keep, parts=4):
    fresh = not isinstance(kv, tuple)
    operands = [kv] if fresh else list(kv)
    shift = 1 + len(operands)
    out_shape = [jax.ShapeDtypeStruct(acc.shape, F32)] * 3
    scratch = []
    if fresh and keep:
        out_shape += term_shapes(kv.shape[1])
    elif fresh:
        scratch = [pltpu.VMEM(each.shape, each.dtype) for each in term_shapes(kv.shape[1])]
    out = call(
        functools.partial(later_kernel, distance, parts, heads, fresh),
        [SMEM] + [VMEM] * (len(operands) + 4),
        [VMEM] * len(out_shape),
        out_shape,
        scratch,
        alias={shift + 1: 0, shift + 2: 1, shift + 3: 2},
        after=after,
    )(me, *operands, q_terms, acc, peak, total)
    return out[:3], tuple(out[3:])


def last_kernel(distance, whose, heads, columns, me_ref, *refs):
    fresh = whose == "other"
    if fresh:
        kv_ref, q_ref, acc_ref, peak_ref, total_ref, out_ref, keys_ref, values_ref = refs
    else:
        keys_ref, values_ref, q_ref, acc_ref, peak_ref, total_ref, *refs = refs
    if columns is not None:
        theirs_ref, done_ref, energy_ref, energy_other_ref, gain_ref, linear_ref = refs[:6]
        lin_hbm, soft_hbm, lin_ref, out_ref, sems = refs[6:]
    elif not fresh:
        (out_ref,) = refs
    group, rows, _ = q_ref.shape
    tokens = rows // 2
    core, chip = me_ref[0] & 1, me_ref[0] >> 1
    side = core if whose == "own" else 1 - core
    at = pl.ds(pl.multiple_of(side * tokens, tokens), tokens)
    copies = []

    def copy(source, target):
        copies.append(pltpu.make_async_copy(source, target, sems.at[len(copies)]))
        return copies[-1]

    def columns_of(whose, g, count):
        return pl.ds(pl.multiple_of((whose * group + g) * HD, HD), count * HD)

    if columns is not None:
        blocks = [pl.ds(n * (tokens // 4), tokens // 4) for n in range(4)]
        for block in blocks:
            to = soft_hbm.at[block, columns_of(1 - core, 0, group)]
            copy(theirs_ref.at[block], to).start()
        factor = lax.rsqrt((energy_ref[:8] + energy_other_ref[:8]) / columns + EPSILON)
        factor = factor.T[:, 0:1]
        for block in blocks:
            to = soft_hbm.at[block, columns_of(core, 0, group - len(heads))]
            copy(done_ref.at[block], to).start()
        lin_copies = [copy(lin_ref.at[block], lin_hbm.at[block]) for block in blocks]
        own_copies = [
            copy(out_ref.at[:, pl.ds(n * HD, HD)], soft_hbm.at[:, columns_of(core, g, 1)])
            for n, g in enumerate(heads)
        ]

    def scale_rows(n):
        rows = slice(n * (tokens // 4), (n + 1) * (tokens // 4))
        lin_ref[rows] = linear_ref[rows] * factor[rows] * gain_ref[...]
        lin_copies[n].start()

    def finish(n, acc, total):
        out_ref[:, n * HD : (n + 1) * HD] = acc / jnp.sum(total, axis=1, keepdims=True)
        if columns is not None:
            own_copies[n].start()

    def score(n):
        return dot(score_terms(q_ref[heads[n], at]), keys_ref[...])

    def soften(n, s):
        old = peak_ref[heads[n], at]
        peak = jnp.maximum(jnp.max(lane_max(s), axis=1, keepdims=True), old)
        shrink = jnp.exp2(old - peak)
        return *weigh(s, peak, total_ref[heads[n], at] * shrink), shrink

    def gather(n, terms):
        high, low, total, shrink = terms
        new = summed(high, low, values_ref[...])
        finish(n, acc_ref[heads[n], at] * shrink + new, total)

    def gather_and_scale(n, terms):
        gather(n, terms)
        if n == 0:
            for block in range(2, 4):
                scale_rows(block)

    if columns is not None:
        for block in range(2):
            scale_rows(block)
    visible = lax.bitwise_xor(chip, distance) < chip

    @pl.when(visible)
    def _():
        if fresh:
            fill_terms(kv_ref, keys_ref, values_ref)
        run(len(heads), score, soften, gather if columns is None else gather_and_scale)

    @pl.when(jnp.logical_not(visible))
    def _():
        for n, g in enumerate(heads):
            finish(n, acc_ref[g, at], total_ref[g, at])
        if columns is not None:
            for block in range(2, 4):
                scale_rows(block)

    for each in copies:
        each.wait()


def last_stage(me, distance, whose, heads, kv, operands, after, extra=None):
    group, rows, _ = operands[0].shape
    tokens = rows // 2
    part = jax.ShapeDtypeStruct((tokens, len(heads) * HD), F32)
    fresh, columns, scratch = whose == "other", None, []
    operands = [kv, *operands] if fresh else [*kv, *operands]
    if extra is not None:
        columns, more = extra
        operands = [*operands, *more]
        linear = more[-1]
        out_shape = [
            jax.ShapeDtypeStruct(linear.shape, F32),
            jax.ShapeDtypeStruct((tokens, 2 * group * HD), F32),
        ]
        out_spec = [HBM] * 2
        scratch = [
            pltpu.VMEM(linear.shape, F32),
            pltpu.VMEM(part.shape, F32),
            pltpu.SemaphoreType.DMA((12 + len(heads),)),
        ]
    else:
        out_shape = [part] + (term_shapes(kv.shape[1]) if fresh else [])
        out_spec = [VMEM] * len(out_shape)
    return call(
        functools.partial(last_kernel, distance, whose, heads, columns),
        [SMEM] + [VMEM] * len(operands),
        out_spec,
        out_shape,
        scratch,
        after=after,
    )(me, *operands)


def plus_kernel(a_ref, b_ref, out_ref):
    out_ref[...] = a_ref[...] + b_ref[...]


def plus(a, b, after):
    return call(
        plus_kernel, [VMEM] * 2, VMEM, jax.ShapeDtypeStruct(a.shape, F32), after=after
    )(a, b)


def copy_kernel(source_ref, out_ref):
    out_ref[...] = source_ref[...]


def copied(array, after):
    return call(copy_kernel, [VMEM], VMEM, jax.ShapeDtypeStruct(array.shape, F32), after=after)(
        array
    )


def relay_kernel(me_ref, own_ref, across_ref, out_ref):
    @pl.when((me_ref[0] & 1) == 0)
    def _():
        out_ref[...] = own_ref[...]

    @pl.when((me_ref[0] & 1) == 1)
    def _():
        out_ref[...] = across_ref[...]


def relayed(me, own, across, after):
    return call(
        relay_kernel,
        [SMEM, VMEM, VMEM],
        VMEM,
        jax.ShapeDtypeStruct(own.shape, F32),
        after=after,
    )(me, own, across)


def body(q_lin, k_lin, v_lin, log_decay, lin_gain, q_soft, k_soft, v_soft):
    chips = lax.axis_size("ctx") // 2
    heads = lax.axis_size("head")
    me = lax.axis_index("ctx")
    me_flag = me.reshape(1).astype(jnp.int32)
    assert k_soft.shape[1] == 2 * HD
    swap_pairs = [(2 * c + e, 2 * c + 1 - e) for c in range(chips) for e in range(2)]

    def swap(array):
        return lax.ppermute(array, "ctx", swap_pairs)

    def across(array, distance, wanted=lambda c, e: True):
        pairs = [
            (2 * (c ^ distance) + e, 2 * c + e)
            for c in range(chips)
            for e in range(2)
            if wanted(c, e)
        ]
        return lax.ppermute(array, "ctx", pairs)

    square = chips == 4
    kv_mine, kv_send = halves(me & 1, k_soft, v_soft)
    kv_other = swap(kv_send)
    states, sums = local_states(log_decay, k_lin, v_lin, [kv_mine])
    others = swap(states)
    kv, q_send = pair_block(me_flag, kv_mine, kv_other, q_soft, [sums])
    q_other = swap(q_send)
    total, prefix = chip_total(me_flag, states, others, [q_send]), None
    inside, terms = inside_blocks(q_lin, k_lin, v_lin, sums, [total])

    def exchanged(array, step):
        return lax.ppermute(array, "head", [(i, i ^ step) for i in range(heads)])

    def sent(distance, array):
        return across(array, distance, lambda c, e: c ^ distance < c)

    def stage(kv, distance, heads, carried, after, keep=False):
        return later_stage(me_flag, distance, heads, kv, q_terms, *carried, after, keep)

    bits = chips.bit_length() - 1
    arrived, token = {}, inside
    if square:
        arrived[2] = sent(2, kv)
        token = copied(kv, [inside])
        arrived[1] = sent(1, token)
    else:
        for distance in range(1, chips):
            arrived[distance] = sent(distance, kv)
    q_terms, *carried = own_stage(me_flag, q_soft, q_other, kv, [token])
    group = q_terms.shape[0]
    all_heads, front, back = range(group), range(group // 2), range(group // 2, group)
    token = carried[0]
    if square:
        relay = relayed(me_flag, kv, arrived[2], [token])
        arrived[3] = lax.ppermute(relay, "ctx", [(0, 6), (2, 4), (5, 7), (7, 5)])
    for bit in range(bits):
        last = bit == bits - 1
        theirs = across(total, 1 << bit, lambda c, e: not last or c ^ (1 << bit) < c)
        prefix, total = turn(me_flag, bit, total, theirs, prefix, last, [token] + ([arrived[1]] if square and last else []))
        distance = 2 if square else bit + 1
        if not (square and last):
            waits = [prefix, relay] if square else [prefix]
            carried, _ = stage(arrived[distance], distance, all_heads, carried, waits)
            token = carried[0]
    prefix_other = swap(prefix)
    left = [1] if square else range(bits + 1, chips - 1)
    for distance in left[:-1]:
        carried, _ = stage(arrived[distance], distance, all_heads, carried, [prefix])
    carried, kept = stage(arrived[left[-1]], left[-1], front, carried, [prefix], True)
    linear, energy = linear_blocks(
        me_flag, terms, inside, sums, prefix, prefix_other, others, [carried[0]]
    )
    energies, step = [], 1
    while step < heads:
        energies.append(step)
        step *= 2
    other = exchanged(energy, energies[0])
    carried, _ = stage(kept, left[-1], back, carried, [energy])
    operands = [q_terms, *carried]
    split_at = max(1, group - 1)
    for step in energies[1:]:
        energy = plus(energy, other, [carried[0]])
        other = exchanged(energy, step)

    theirs, *kept = last_stage(
        me_flag, chips - 1, "other", all_heads, arrived[chips - 1], operands, [energy]
    )
    (done,) = last_stage(me_flag, chips - 1, "own", all_heads[:split_at], kept, operands, [])
    columns = q_lin.shape[1] * heads
    more = [swap(theirs), done, energy, other, lin_gain.reshape(1, -1), linear]
    return tuple(
        last_stage(me_flag, chips - 1, "own", all_heads[split_at:], kept, operands, [], (columns, more))
    )


def solution(mesh):
    return jax.shard_map(
        body,
        mesh=mesh,
        in_specs=(
            P("ctx", "head"),
            P("ctx", "head"),
            P("ctx", "head"),
            P("head", "ctx"),
            P("head"),
            P("ctx", "head"),
            P("ctx", "head"),
            P("ctx", "head"),
        ),
        out_specs=(P("ctx", "head"), P("ctx", "head")),
        check_vma=False,
    )
```
